32 devices in a mesh: dp: 2 (over y), blk: 16 (over z, x, core).
Axes of the slice: x: 2, y: 2, z: 4, core: 2. Of those that a mesh axis runs over, the one named last changes fastest.
Arguments:
- residues: bfloat16 [4, 2048, 768], P('dp', 'blk'), may hold values from -6 to 6
- coordinates: bfloat16 [4, 3, 2048], P('dp', None, 'blk'), may hold values from -48 to 48
- segment_ids: int32 [4, 2048], P('dp', 'blk'), may hold values from 0 to 2, as said below
- time_steps: int32 [4, 3], P('dp'), may hold values from 0 to 999
- time_weight: bfloat16 [768, 768], P('dp'), may hold values from -0.21875 to 0.21875
- norm1_gain: bfloat16 [768], P('dp'), may hold values from 0.099609375 to 1.8984375
- norm1_bias: bfloat16 [768], P('dp'), may hold values from -1.5 to 1.5
- qkv_weight: bfloat16 [768, 2304], P('dp'), may hold values from -0.21875 to 0.21875
- bias_weight: bfloat16 [128, 32], P('dp'), may hold values from -3 to 3
- out_weight: bfloat16 [768, 768], P('dp'), may hold values from -1.25 to 1.25
- norm2_gain: bfloat16 [768], P('dp'), may hold values from 0.099609375 to 1.8984375
- norm2_bias: bfloat16 [768], P('dp'), may hold values from -1.5 to 1.5
- up_weight: bfloat16 [768, 3072], P('dp'), may hold values from -0.21875 to 0.21875
- down_weight: bfloat16 [3072, 768], P('dp'), may hold values from -0.109375 to 0.109375
- force_weight: bfloat16 [3, 768], P(None, 'dp'), may hold values from -0.21875 to 0.21875
- out_cotangent: bfloat16 [4, 2048, 768], P('dp', 'blk'), may hold values from -6 to 6
- force_cotangent: float32 [4, 3, 2048], P('dp', None, 'blk'), may hold values from -6 to 6
Outputs:
- block_out: bfloat16 [4, 2048, 768], P('dp', 'blk')
- forces: float32 [4, 3, 2048], P('dp', None, 'blk')
- residues_grad: float32 [4, 2048, 768], P('dp', 'blk')
- time_weight_grad: float32 [768, 768], P('dp')
- norm1_gain_grad: float32 [768], P('dp')
- norm1_bias_grad: float32 [768], P('dp')
- qkv_weight_grad: float32 [768, 2304], P('dp')
- bias_weight_grad: float32 [128, 32], P('dp')
- out_weight_grad: float32 [768, 768], P('dp')
- norm2_gain_grad: float32 [768], P('dp')
- norm2_bias_grad: float32 [768], P('dp')
- up_weight_grad: float32 [768, 3072], P('dp')
- down_weight_grad: float32 [3072, 768], P('dp')
- force_weight_grad: float32 [3, 768], P(None, 'dp')
The draws below stay inside these ranges and needn't reach their ends.
Inputs may be any that keep to these rules, and one draw needn't show every extreme that they name: `segment_ids`: each packed row holds proteins 0, 1 and 2 in that order, each one nonempty run of residues; protein 1 begins within the row's first 128 residues and ends within its last 128.
All inputs are finite; a program needn't handle non-finite values.
Results may differ from the reference program's by a relative error of at most 0.02.
Values may be sent and summed in bfloat16 or wider, within the bound.
No kernel may reach another device: no remote copies, remote signals or barrier semaphores. Data moves between devices by JAX's collectives and lax.ppermute only.
A program may use at most 256 MiB of HBM per device.

```python
import jax
import jax.numpy as jnp
from jax import lax

D = 768
HEADS = 32
HEAD_DIM = 24
FF = 3072
KERNELS = 128
TOK_DEV = 128
PROTEINS = 3
TOKENS_MB = 2048
BATCH = 4


def draw_segment_ids(key, part):
    first_key, second_key = jax.random.split(jax.random.fold_in(key, 17))
    begins = jax.random.randint(first_key, (BATCH, 1), 1, TOK_DEV)
    finishes = TOKENS_MB - jax.random.randint(second_key, (BATCH, 1), 1, TOK_DEV)
    position = jnp.arange(TOKENS_MB, dtype=jnp.int32)[None, :]
    return (position >= begins).astype(jnp.int32) + (position >= finishes).astype(jnp.int32)


def touch_ends(result, stream_key, least, largest):
    spot = [jax.random.randint(jax.random.fold_in(stream_key, axis), (), 0, length) for axis, length in enumerate(result.shape)]
    widest = result.shape.index(max(result.shape))
    beside = spot[:widest] + [(spot[widest] + 1) % result.shape[widest]] + spot[widest + 1:]
    return result.at[tuple(spot)].set(least).at[tuple(beside)].set(largest)


def block_scale(key, extent, cuts, smallest, high):
    factor_of = 1.0
    for dim, parts in cuts:
        heights = jax.random.uniform(jax.random.fold_in(jax.random.fold_in(key, 6), dim), (parts,), jnp.float32, smallest / len(cuts), high / len(cuts))
        factor_of = factor_of * jnp.repeat(jnp.exp(heights), extent[dim] // parts).reshape((-1,) + (1,) * (len(extent) - 1 - dim))
    return factor_of


def bell_draw(key, dims, deviation, bound, shards=(), held_as=jnp.bfloat16):
    values = jax.random.normal(key, dims, jnp.float32) * deviation
    if len(shards) > 0:
        values = block_scale(key, dims, shards, -0.22, 0.18) * values
    return jnp.clip(values, min=-bound, max=bound).astype(held_as)


def setup_inputs(seed: int = 0) -> dict:
    arg_keys = jax.random.split(jax.random.key(seed), 18)
    return {
        "residues": bell_draw(arg_keys[0], (BATCH, TOKENS_MB, D), 1.0, 6.0, ((0, 2), (1, 16))),
        "coordinates": bell_draw(arg_keys[1], (BATCH, 3, TOKENS_MB), 8.0, 48.0, ((0, 2), (2, 16))),
        "segment_ids": draw_segment_ids(jax.random.fold_in(arg_keys[17], 71), 0),
        "time_steps": touch_ends(jax.random.randint(arg_keys[3], (BATCH, PROTEINS), 0, 1000), jax.random.fold_in(arg_keys[3], 1), 0, 999).astype(jnp.int32),
        "time_weight": bell_draw(arg_keys[4], (D, D), D ** -0.5, 0.21875, ((0, 2),)),
        "norm1_gain": jnp.clip(1.0 + 0.18 * jax.random.normal(arg_keys[5], (D,), jnp.float32), 0.099609375, 1.8984375).astype(jnp.bfloat16),
        "norm1_bias": bell_draw(arg_keys[6], (D,), 0.3, 1.5, ((0, 2),)),
        "qkv_weight": bell_draw(arg_keys[7], (D, 3 * D), D ** -0.5, 0.21875, ((0, 2),)),
        "bias_weight": bell_draw(arg_keys[8], (KERNELS, HEADS), 0.5, 3.0, ((0, 2),)),
        "out_weight": bell_draw(arg_keys[9], (D, D), (D // 32) ** -0.5, 1.25, ((0, 2),)),
        "norm2_gain": jnp.clip(1.0 + 0.18 * jax.random.normal(arg_keys[10], (D,), jnp.float32), 0.099609375, 1.8984375).astype(jnp.bfloat16),
        "norm2_bias": bell_draw(arg_keys[11], (D,), 0.3, 1.5, ((0, 2),)),
        "up_weight": bell_draw(arg_keys[12], (D, FF), D ** -0.5, 0.21875, ((0, 2),)),
        "down_weight": bell_draw(arg_keys[13], (FF, D), FF ** -0.5, 0.109375, ((0, 2),)),
        "force_weight": bell_draw(arg_keys[14], (3, D), D ** -0.5, 0.21875, ((1, 2),)),
        "out_cotangent": bell_draw(arg_keys[15], (BATCH, TOKENS_MB, D), 1.0, 6.0, ((0, 2), (1, 16))),
        "force_cotangent": bell_draw(arg_keys[16], (BATCH, 3, TOKENS_MB), 1.0, 6.0, ((0, 2), (2, 16)), jnp.float32),
    }


@jax.custom_vjp
def low(v):
    return lax.optimization_barrier(v.astype(jnp.bfloat16)).astype(jnp.float32)

@jax.custom_vjp
def low_back(v):
    return v

def low_keep(v):
    return (low(v), None)

def low_pass(kept, grad):
    return (grad,)

def back_keep(v):
    return (v, None)

def back_low(kept, grad):
    return (low(grad),)
low.defvjp(low_keep, low_pass)
low_back.defvjp(back_keep, back_low)
eps = 1e-05
cutoff = 24.0
masked_value = -1e+30
highest = lax.Precision.HIGHEST

def matmul(left, right):
    return jnp.dot(left, right, precision=highest, preferred_element_type=jnp.float32)

def layer_norm(values, norm_gain, norm_shift):
    centred = values - lax.optimization_barrier(jnp.mean(values, axis=-1, keepdims=True))
    spread = lax.optimization_barrier(jnp.mean(centred * centred, axis=-1, keepdims=True))
    return centred * lax.rsqrt(spread + eps) * norm_gain + norm_shift

def time_features(stamps, feature_width):
    half_width = feature_width // 2
    frequency = jnp.exp(-jnp.log(10000.0) * jnp.arange(half_width, dtype=jnp.float32) / half_width)
    angles = stamps[:, None] * frequency[None, :]
    return jnp.concatenate([jnp.sin(angles), jnp.cos(angles)], axis=1)

def kernel_table(distance, kernel_count):
    centres = jnp.arange(kernel_count, dtype=jnp.float32) * (cutoff / kernel_count)
    scaled = (distance[..., None] - centres) * (kernel_count / (2.0 * cutoff))
    return jnp.exp(-0.5 * scaled * scaled)

def distances(query_points, key_points):
    squared = jnp.zeros((query_points.shape[0], key_points.shape[0]), jnp.float32)
    for component in range(3):
        offset = query_points[:, component][:, None] - key_points[:, component][None, :]
        squared = squared + offset * offset
    return jnp.sqrt(squared)

def layer_row(residue_row, coord_row, segment_row, step_row, time_values, gain_one, shift_one, qkv_values, bias_values, out_values, gain_two, shift_two, up_values, down_values, force_values):
    row_length = residue_row.shape[0]
    stamps = step_row[segment_row].astype(jnp.float32)
    features = low(time_features(stamps, D))
    first = residue_row + low_back(matmul(features, time_values))
    normed = low(layer_norm(first, gain_one, shift_one))
    projected = low_back(low(matmul(normed, qkv_values)))
    query_heads = projected[:, :D].reshape(row_length, HEADS, HEAD_DIM)
    key_heads = projected[:, D:2 * D].reshape(row_length, HEADS, HEAD_DIM)
    value_heads = projected[:, 2 * D:].reshape(row_length, HEADS, HEAD_DIM)
    points = jnp.transpose(coord_row)
    score_scale = 1.0 / HEAD_DIM ** 0.5
    query_block = 128 if row_length % 128 == 0 else row_length

    def attend(block_start):
        query_part = lax.dynamic_slice_in_dim(query_heads, block_start, query_block, 0)
        point_part = lax.dynamic_slice_in_dim(points, block_start, query_block, 0)
        segment_part = lax.dynamic_slice_in_dim(segment_row, block_start, query_block, 0)
        kernels = low(kernel_table(distances(point_part, points), KERNELS))
        pair_bias = jnp.einsum('qkc,ch->hqk', kernels, bias_values, precision=highest)
        scores = jnp.einsum('qhd,khd->hqk', query_part, key_heads, precision=highest) * score_scale + pair_bias
        logits = low_back(scores)
        matches = (segment_part[:, None] == segment_row[None, :])[None]
        probs = jax.nn.softmax(jnp.where(matches, logits, masked_value), axis=-1)
        mixed = jnp.einsum('hqk,khd->qhd', low(probs), value_heads, precision=highest)
        return mixed.reshape(query_block, D)
    starts = jnp.arange(row_length // query_block, dtype=jnp.int32) * query_block
    attended = lax.map(jax.checkpoint(attend), starts).reshape(row_length, D)
    attended = low_back(low(attended))
    second = first + low_back(matmul(attended, out_values))
    normed_two = low(layer_norm(second, gain_two, shift_two))
    hidden = low_back(matmul(normed_two, up_values))
    activated = low(jax.nn.gelu(hidden, approximate=False))
    third = second + low_back(matmul(activated, down_values))
    forces = jnp.einsum('cd,qd->cq', force_values, low(third), precision=highest)
    return (third, forces)

def reference(residues, coordinates, segment_ids, time_steps, time_weight, norm1_gain, norm1_bias, qkv_weight, bias_weight, out_weight, norm2_gain, norm2_bias, up_weight, down_weight, force_weight, out_cotangent, force_cotangent):
    coord_values = coordinates.astype(jnp.float32)

    def forward(residue_values, time_values, gain_one, shift_one, qkv_values, bias_values, out_values, gain_two, shift_two, up_values, down_values, force_values):

        def row_step(carry_value, items):
            residue_row, coord_row, segment_row, step_row = items
            third, forces = layer_row(residue_row, coord_row, segment_row, step_row, time_values, gain_one, shift_one, qkv_values, bias_values, out_values, gain_two, shift_two, up_values, down_values, force_values)
            return (carry_value, (third, forces))
        unused, results = lax.scan(row_step, jnp.float32(0.0), (residue_values, coord_values, segment_ids, time_steps))
        return (results[0], results[1])
    outputs, pullback = jax.vjp(forward, residues.astype(jnp.float32), time_weight.astype(jnp.float32), norm1_gain.astype(jnp.float32), norm1_bias.astype(jnp.float32), qkv_weight.astype(jnp.float32), bias_weight.astype(jnp.float32), out_weight.astype(jnp.float32), norm2_gain.astype(jnp.float32), norm2_bias.astype(jnp.float32), up_weight.astype(jnp.float32), down_weight.astype(jnp.float32), force_weight.astype(jnp.float32))
    grads = pullback((out_cotangent.astype(jnp.float32), force_cotangent.astype(jnp.float32)))
    return (outputs[0].astype(jnp.bfloat16), outputs[1], grads[0], grads[1], grads[2], grads[3], grads[4], grads[5], grads[6], grads[7], grads[8], grads[9], grads[10], grads[11])
```

```python
import functools
import jax
import jax.numpy as jnp
import numpy as np
from jax import lax
from jax.sharding import PartitionSpec as P
from jax.experimental import pallas as pl
from jax.experimental.pallas import tpu as pltpu

D = 768
HEADS = 32
HEAD_DIM = 24
KERNELS = 128
GROUPS = 4
GROUP_HEADS = 8
GROUP_DIM = 192
GROUP_PAD = 256
LOG2E = 1.4426950408889634
SCALE = HEAD_DIM ** -0.5
SPAN = 8
NA = KERNELS // SPAN
masked_value = -1e30
VMEM_LIMIT = 60 * 2**20
FORWARD_TILE = 32
BACKWARD_TILE = 64
FINE = 8


def cost(micros, bytes_moved):
    return pl.CostEstimate(flops=int(micros * 1.1e9), bytes_accessed=int(bytes_moved), transcendentals=0)


def distance_tile(q_ref, k_ref):
    total = None
    for axis in range(3):
        offset = q_ref[:, axis:axis + 1] - k_ref[axis:axis + 1, :]
        total = offset * offset if total is None else total + offset * offset
    return jnp.sqrt(total) * (KERNELS / 48.0)


def kernel_rows(x):
    centre = lax.broadcasted_iota(jnp.int32, (NA, 1), 0).astype(jnp.float32) * (SPAN / 2.0) + SPAN / 4.0
    y = jnp.clip(x - centre, -24.0, 24.0)
    up_step = jnp.exp2(y * (0.5 * LOG2E))
    down_step = jnp.exp2(y * (-0.5 * LOG2E))
    middle = jnp.exp2((y * y) * (-0.5 * LOG2E))
    above = [middle]
    for _ in range(SPAN // 2 - 1):
        above.append(above[-1] * up_step)
    below = []
    current = middle
    for _ in range(SPAN // 2):
        current = current * down_step
        below.append(current)
    rows = below[::-1] + above
    return jnp.concatenate([r.astype(jnp.bfloat16) for r in rows], axis=0)


def kernel_order():
    step = np.arange(SPAN) - SPAN // 2
    order = np.array([[a * SPAN + SPAN // 2 + b for a in range(NA)] for b in step]).reshape(-1)
    factor = np.repeat(np.exp(-(step ** 2) / 8.0), NA).astype(np.float32)
    return order, factor


def bias_kernel(chunk, q_ref, k_ref, w_ref, *refs):
    out_ref, x_ref, m_ref = refs[-3:]
    rows = q_ref.shape[0]
    keys = k_ref.shape[1]
    x_ref[...] = distance_tile(q_ref, k_ref)
    m_ref[...] = jnp.where(q_ref[:, 3:4] == k_ref[3:4, :], 0.0, masked_value)
    w = w_ref[...]

    def step(t, carry):
        for start in range(0, keys, chunk):
            cols = slice(start, start + chunk)
            values = []
            for q in (2 * t, 2 * t + 1):
                value = jnp.dot(w, kernel_rows(x_ref[pl.ds(q, 1), cols]), preferred_element_type=jnp.float32)
                values.append(value + m_ref[pl.ds(q, 1), cols])
            for g in range(GROUPS):
                both = jnp.concatenate([value[g * GROUP_HEADS:(g + 1) * GROUP_HEADS] for value in values], axis=0)
                out_ref[g, pl.ds(t * 2 * GROUP_HEADS, 2 * GROUP_HEADS), cols] = both.astype(out_ref.dtype)
        return carry

    lax.fori_loop(0, rows // 2, step, 0, unroll=True)


def pair_bias(q_where, k_where, w, first, steps, previous):
    rows, keys = q_where.shape[0], k_where.shape[1]
    in_specs = [
        pl.BlockSpec((FINE, 8), lambda i: (i + first, 0)),
        pl.BlockSpec((8, keys), lambda i: (0, 0)),
        pl.BlockSpec((HEADS, KERNELS), lambda i: (0, 0)),
    ]
    operands = [q_where, k_where, w]
    aliases = {}
    if previous is not None:
        in_specs.append(pl.BlockSpec(memory_space=pl.ANY))
        operands.append(previous)
        aliases = {3: 0}
    return pl.pallas_call(
        functools.partial(bias_kernel, 256),
        grid=(steps,),
        in_specs=in_specs,
        out_specs=pl.BlockSpec((GROUPS, FINE * GROUP_HEADS, keys), lambda i: (0, i + first, 0)),
        out_shape=jax.ShapeDtypeStruct((GROUPS, rows * GROUP_HEADS, keys), jnp.bfloat16),
        scratch_shapes=[pltpu.VMEM((FINE, keys), jnp.float32), pltpu.VMEM((FINE, keys), jnp.float32)],
        input_output_aliases=aliases,
        cost_estimate=cost(1.5 * steps, FINE * steps * HEADS * keys * 2),
        compiler_params=pltpu.CompilerParams(vmem_limit_bytes=VMEM_LIMIT),
        name="pair_bias",
    )(*operands)


def project_kernel(x_ref, w_ref, turn_ref, key_ref, value_ref, w_turn_ref):
    @pl.when(pl.program_id(0) == 0)
    def turn_weight():
        w_turn_ref[...] = w_ref[...].T

    x = x_ref[...]
    rows = x.shape[0]
    turn_ref[...] = lax.dot_general(
        w_turn_ref[...], x, (((1,), (1,)), ((), ())), preferred_element_type=jnp.float32
    ).astype(turn_ref.dtype)
    flat = jnp.dot(x, w_ref[...], preferred_element_type=jnp.float32)
    for out_ref, first, filler in ((key_ref, 0, 0.0), (value_ref, D, 1.0)):
        for g in range(GROUPS):
            part = flat[:, first + g * GROUP_DIM:first + (g + 1) * GROUP_DIM]
            wide = jnp.concatenate([part, jnp.full((rows, GROUP_PAD - GROUP_DIM), filler, jnp.float32)], axis=1)
            out_ref[:, g * GROUP_PAD:(g + 1) * GROUP_PAD] = wide.astype(out_ref.dtype)


def project(values, weight):
    keys, depth = values.shape
    width = weight.shape[1]
    wide = GROUPS * GROUP_PAD
    block = 256
    return pl.pallas_call(
        project_kernel,
        grid=(keys // block,),
        in_specs=[
            pl.BlockSpec((block, depth), lambda i: (i, 0)),
            pl.BlockSpec((depth, width), lambda i: (0, 0)),
        ],
        out_specs=[
            pl.BlockSpec((width, block), lambda i: (0, i)),
            pl.BlockSpec((block, wide), lambda i: (i, 0)),
            pl.BlockSpec((block, wide), lambda i: (i, 0)),
        ],
        out_shape=[
            jax.ShapeDtypeStruct((width, keys), jnp.bfloat16),
            jax.ShapeDtypeStruct((keys, wide), jnp.bfloat16),
            jax.ShapeDtypeStruct((keys, wide), jnp.bfloat16),
        ],
        scratch_shapes=[pltpu.VMEM((width, depth), jnp.bfloat16)],
        cost_estimate=cost(12, keys * (depth + 3 * width) * 2),
        compiler_params=pltpu.CompilerParams(vmem_limit_bytes=VMEM_LIMIT),
        name="project",
    )(values, weight)


def head_mask(width):
    head = lax.broadcasted_iota(jnp.int32, (GROUP_HEADS, width), 0)
    lane = lax.broadcasted_iota(jnp.int32, (GROUP_HEADS, width), 1)
    return ((lane >= head * HEAD_DIM) & (lane < (head + 1) * HEAD_DIM)).astype(jnp.float32)


def spread_heads(values, mask):
    rows, width = values.shape
    return (values[:, None, :] * mask[None]).reshape(rows * GROUP_HEADS, width)


def gather_heads(values, mask):
    rows, width = values.shape
    return jnp.sum(values.reshape(rows // GROUP_HEADS, GROUP_HEADS, width) * mask[None], axis=1)


def forward_kernel(chunk, q_ref, kt_ref, v_ref, bias_ref, p_ref, o_ref, inv_ref, s_ref):
    keys = kt_ref.shape[1]
    mask = head_mask(GROUP_PAD)

    for g in range(GROUPS):
        rows = slice(g * GROUP_DIM, (g + 1) * GROUP_DIM)
        spread = spread_heads(q_ref[g].astype(jnp.float32), mask).astype(jnp.bfloat16)[:, :GROUP_DIM]
        peak = None
        for start in range(0, keys, chunk):
            s = jnp.dot(spread, kt_ref[rows, start:start + chunk], preferred_element_type=jnp.float32)
            s = s * (SCALE * LOG2E) + bias_ref[g, :, start:start + chunk].astype(jnp.float32)
            s_ref[:, start:start + chunk] = s
            for lane in range(0, chunk, 128):
                part = s[:, lane:lane + 128]
                peak = part if peak is None else jnp.maximum(peak, part)
        top = jnp.max(peak, axis=1, keepdims=True)
        for start in range(0, keys, chunk):
            p_ref[g, :, start:start + chunk] = jnp.exp2(s_ref[:, start:start + chunk] - top).astype(jnp.bfloat16)
        mixed = jnp.dot(p_ref[g], v_ref[:, g * GROUP_PAD:(g + 1) * GROUP_PAD], preferred_element_type=jnp.float32)
        inverse = 1.0 / mixed[:, GROUP_DIM:GROUP_DIM + 1]
        o_ref[g] = gather_heads(mixed * inverse, mask)
        inv_ref[g] = gather_heads(jnp.broadcast_to(inverse, mixed.shape), mask)


def attend(q, turned, value_flat, bias):
    rows, keys = q.shape[1], turned.shape[1]
    tile = min(FORWARD_TILE, FORWARD_TILE * 2048 // keys)
    whole = pl.Buffered(1)
    return pl.pallas_call(
        functools.partial(forward_kernel, 512),
        grid=(rows // tile,),
        in_specs=[
            pl.BlockSpec((GROUPS, tile, GROUP_PAD), lambda i: (0, i, 0)),
            pl.BlockSpec((D, keys), lambda i: (0, 0), pipeline_mode=whole),
            pl.BlockSpec((keys, GROUPS * GROUP_PAD), lambda i: (0, 0), pipeline_mode=whole),
            pl.BlockSpec((GROUPS, tile * GROUP_HEADS, keys), lambda i: (0, i, 0)),
        ],
        out_specs=[
            pl.BlockSpec((GROUPS, tile * GROUP_HEADS, keys), lambda i: (0, i, 0)),
            pl.BlockSpec((GROUPS, tile, GROUP_PAD), lambda i: (0, i, 0)),
            pl.BlockSpec((GROUPS, tile, GROUP_PAD), lambda i: (0, i, 0)),
        ],
        out_shape=[
            jax.ShapeDtypeStruct((GROUPS, rows * GROUP_HEADS, keys), jnp.bfloat16),
            jax.ShapeDtypeStruct((GROUPS, rows, GROUP_PAD), jnp.float32),
            jax.ShapeDtypeStruct((GROUPS, rows, GROUP_PAD), jnp.float32),
        ],
        scratch_shapes=[
            pltpu.VMEM((tile * GROUP_HEADS, keys), jnp.float32),
        ],
        input_output_aliases={3: 0},
        cost_estimate=cost(45, rows * HEADS * keys * 4),
        compiler_params=pltpu.CompilerParams(vmem_limit_bytes=VMEM_LIMIT),
        name="attend",
    )(q, turned, value_flat, bias)


def backward_kernel(chunk, q_ref, do_ref, o_ref, k_ref, vt_ref, p_ref, ds_ref, dq_ref, dkt_ref, dvt_ref, dk_acc, dv_acc):
    keys = vt_ref.shape[1]
    mask = head_mask(GROUP_PAD)
    tile = pl.program_id(0)
    groups = q_ref.shape[0]

    @pl.when(tile == 0)
    def start_group():
        dk_acc[...] = jnp.zeros_like(dk_acc)
        dv_acc[...] = jnp.zeros_like(dv_acc)

    for g in range(groups):
        rows = slice(g * GROUP_DIM, (g + 1) * GROUP_DIM)
        q_wide = spread_heads(q_ref[g].astype(jnp.float32), mask)
        do_wide = spread_heads(do_ref[g].astype(jnp.float32), mask)
        o_wide = spread_heads(o_ref[g], mask)
        delta = jnp.sum(do_wide * o_wide, axis=1, keepdims=True)
        do_low = do_wide.astype(jnp.bfloat16)[:, :GROUP_DIM]
        do_turn = do_wide[:, :GROUP_DIM].T.astype(jnp.bfloat16)
        q_turn = q_wide[:, :GROUP_DIM].T.astype(jnp.bfloat16)
        for start in range(0, keys, chunk):
            cols = slice(start, start + chunk)
            dp = jnp.dot(do_low, vt_ref[rows, cols], preferred_element_type=jnp.float32)
            p = p_ref[g, :, cols]
            ds = (p.astype(jnp.float32) * (dp - delta)).astype(jnp.bfloat16)
            ds_ref[g, :, cols] = ds
            dv_acc[rows, cols] += jnp.dot(do_turn, p, preferred_element_type=jnp.float32)
            dk_acc[rows, cols] += jnp.dot(q_turn, ds, preferred_element_type=jnp.float32)
        dq = jnp.dot(ds_ref[g], k_ref[:, g * GROUP_PAD:(g + 1) * GROUP_PAD], preferred_element_type=jnp.float32)
        dq_ref[g] = gather_heads(dq, mask) * SCALE

    @pl.when(tile == pl.num_programs(0) - 1)
    def finish():
        dkt_ref[...] = (dk_acc[...] * SCALE).astype(dkt_ref.dtype)
        dvt_ref[...] = dv_acc[...].astype(dvt_ref.dtype)


def attend_back(q, do, o, key_flat, turned, p, part, parts):
    rows, keys = q.shape[1], turned.shape[1]
    tile = min(BACKWARD_TILE, BACKWARD_TILE * 2048 // keys)
    groups = GROUPS // parts
    width = groups * GROUP_DIM
    whole = pl.Buffered(1)
    narrow = pl.BlockSpec((groups, tile, GROUP_PAD), lambda i: (part, i, 0))
    return pl.pallas_call(
        functools.partial(backward_kernel, 512),
        grid=(rows // tile,),
        in_specs=[
            narrow,
            narrow,
            narrow,
            pl.BlockSpec((keys, groups * GROUP_PAD), lambda i: (0, part), pipeline_mode=whole),
            pl.BlockSpec((width, keys), lambda i: (part + parts, 0), pipeline_mode=whole),
            pl.BlockSpec((groups, tile * GROUP_HEADS, keys), lambda i: (part, i, 0)),
        ],
        out_specs=[
            pl.BlockSpec((groups, tile * GROUP_HEADS, keys), lambda i: (part, i, 0)),
            pl.BlockSpec((groups, tile, GROUP_PAD), lambda i: (0, i, 0)),
            pl.BlockSpec((width, keys), lambda i: (0, 0), pipeline_mode=whole),
            pl.BlockSpec((width, keys), lambda i: (0, 0), pipeline_mode=whole),
        ],
        out_shape=[
            jax.ShapeDtypeStruct(p.shape, p.dtype),
            jax.ShapeDtypeStruct((groups, rows, GROUP_PAD), jnp.float32),
            jax.ShapeDtypeStruct((width, keys), jnp.bfloat16),
            jax.ShapeDtypeStruct((width, keys), jnp.bfloat16),
        ],
        scratch_shapes=[
            pltpu.VMEM((width, keys), jnp.float32),
            pltpu.VMEM((width, keys), jnp.float32),
        ],
        input_output_aliases={5: 0},
        cost_estimate=cost(56 / parts, rows * HEADS * keys * 4 // parts),
        compiler_params=pltpu.CompilerParams(vmem_limit_bytes=VMEM_LIMIT),
        name="attend_back",
    )(q, do, o, key_flat, turned, p)


def table_grad_kernel(chunk, q_ref, k_ref, ds_ref, out_ref, x_ref):
    rows = q_ref.shape[0]
    keys = k_ref.shape[1]
    pair = 2 * GROUP_HEADS

    @pl.when(pl.program_id(0) == 0)
    def start_zero():
        out_ref[...] = jnp.zeros_like(out_ref)

    x_ref[...] = distance_tile(q_ref, k_ref)

    def step(t, total):
        for start in range(0, keys, chunk):
            x = x_ref[pl.ds(2 * t, 2), start:start + chunk]
            table = jnp.concatenate([kernel_rows(x[0:1]), kernel_rows(x[1:2])], axis=0)
            grads = jnp.concatenate(
                [ds_ref[g, pl.ds(t * pair, pair), start:start + chunk] for g in range(GROUPS)], axis=0
            )
            total = total + lax.dot_general(table, grads, (((1,), (1,)), ((), ())), preferred_element_type=jnp.float32)
        return total

    out_ref[...] += lax.fori_loop(0, rows // 2, step, jnp.zeros(out_ref.shape, jnp.float32), unroll=True)


def table_grad(q_where, k_where, ds, first, steps):
    rows, keys = q_where.shape[0], k_where.shape[1]
    wide = 2 * HEADS
    return pl.pallas_call(
        functools.partial(table_grad_kernel, 256),
        grid=(steps,),
        in_specs=[
            pl.BlockSpec((FINE, 8), lambda i: (i + first, 0)),
            pl.BlockSpec((8, keys), lambda i: (0, 0)),
            pl.BlockSpec((GROUPS, FINE * GROUP_HEADS, keys), lambda i: (0, i + first, 0)),
        ],
        out_specs=pl.BlockSpec((2 * KERNELS, wide), lambda i: (0, 0)),
        out_shape=jax.ShapeDtypeStruct((2 * KERNELS, wide), jnp.float32),
        scratch_shapes=[pltpu.VMEM((FINE, keys), jnp.float32)],
        cost_estimate=cost(1.6 * steps, FINE * steps * HEADS * keys * 2),
        compiler_params=pltpu.CompilerParams(vmem_limit_bytes=VMEM_LIMIT),
        name="table_grad",
    )(q_where, k_where, ds)


def table_sums(sums):
    sums = sums.reshape(2, KERNELS, GROUPS, 2, GROUP_HEADS)
    both = (sums[0, :, :, 0] + sums[1, :, :, 1]).reshape(KERNELS, HEADS)
    order, factor = kernel_order()
    return (both * factor[:, None])[np.argsort(order)]


def place_kernel(steps, s_ref, *refs):
    own_ref = refs[0]
    mine, other = refs[1:1 + steps], refs[1 + steps:1 + 2 * steps]
    out_ref = refs[-1]
    j = pl.program_id(0)
    place, core = s_ref[0], s_ref[1]
    away = lax.rem(place - j // 2 + steps + 1, steps + 1)

    @pl.when(away == 0)
    def own_part():
        out_ref[...] = own_ref[...]

    for step in range(1, steps + 1):
        @pl.when((away == step) & (core == j % 2))
        def fetched_part():
            out_ref[...] = mine[step - 1][...]

        @pl.when((away == step) & (core != j % 2))
        def passed_part():
            out_ref[...] = other[step - 1][...]


def place_shards(where, own, mine, other):
    steps = len(mine)
    rows, columns = own.shape
    half = rows // 2
    fixed = pl.BlockSpec((half, columns), lambda j, s: (0, 0))
    return pl.pallas_call(
        functools.partial(place_kernel, steps),
        grid_spec=pltpu.PrefetchScalarGridSpec(
            num_scalar_prefetch=1,
            grid=(2 * (steps + 1),),
            in_specs=[pl.BlockSpec((half, columns), lambda j, s: (j % 2, 0))] + [fixed] * (2 * steps),
            out_specs=pl.BlockSpec((half, columns), lambda j, s: (j, 0)),
        ),
        out_shape=jax.ShapeDtypeStruct(((steps + 1) * rows, columns), own.dtype),
        cost_estimate=cost(3, 2 * (steps + 1) * own.size * 2),
        compiler_params=pltpu.CompilerParams(vmem_limit_bytes=VMEM_LIMIT),
        name="place_shards",
    )(where, own, *mine, *other)


def assemble_kernel(xs, s_ref, *refs):
    out_ref = refs[-1]
    own_refs, other_refs = refs[:xs], refs[xs:2 * xs]
    zs, rows, half = own_refs[0].shape
    x, z, core = s_ref[0], s_ref[1], s_ref[2]
    jx = pl.program_id(0)
    from_x = lax.rem(x - jx + xs, xs)
    for step in range(xs):
        @pl.when(from_x == step)
        def copy_piece():
            for jz in range(zs):
                from_z = lax.rem(z - jz + zs, zs)
                own = own_refs[step][from_z].astype(jnp.float32)
                other = other_refs[step][from_z].astype(jnp.float32)
                first = core == 0
                out_ref[0, jz, :, :half] = jnp.where(first, own, other)
                out_ref[0, jz, :, half:] = jnp.where(first, other, own)


def assemble(where, own, other):
    xs = len(own)
    zs, rows, half = own[0].shape
    spec = pl.BlockSpec((zs, rows, half), lambda i, s: (0, 0, 0))
    whole = pl.pallas_call(
        functools.partial(assemble_kernel, xs),
        grid_spec=pltpu.PrefetchScalarGridSpec(
            num_scalar_prefetch=1,
            grid=(xs,),
            in_specs=[spec] * (2 * xs),
            out_specs=pl.BlockSpec((1, zs, rows, 2 * half), lambda i, s: (i, 0, 0, 0)),
        ),
        out_shape=jax.ShapeDtypeStruct((xs, zs, rows, 2 * half), jnp.float32),
        cost_estimate=cost(4, xs * zs * rows * half * 12),
        compiler_params=pltpu.CompilerParams(vmem_limit_bytes=VMEM_LIMIT),
        name="assemble",
    )(where, *own, *other)
    return whole.reshape(xs * zs * rows, 2 * half)


eps = 1e-05
highest = lax.Precision.HIGHEST
CHIP_ROW = 4


def layer_norm(values, norm_gain, norm_shift):
    centred = values - jnp.mean(values, axis=-1, keepdims=True)
    spread = jnp.mean(centred * centred, axis=-1, keepdims=True)
    return centred * lax.rsqrt(spread + eps) * norm_gain + norm_shift


def exact_gelu(values):
    return jax.nn.gelu(values, approximate=False)


def time_features(stamps, feature_width):
    half_width = feature_width // 2
    frequency = jnp.exp(-jnp.log(10000.0) * jnp.arange(half_width, dtype=jnp.float32) / half_width)
    angles = stamps[:, None] * frequency[None, :]
    return jnp.concatenate([jnp.sin(angles), jnp.cos(angles)], axis=1)


def shifted(values, axis, step):
    size = lax.axis_size(axis)
    return lax.ppermute(values, axis, [(i, (i + step) % size) for i in range(size)])


def part_of(values, index, count, axis):
    length = values.shape[axis] // count
    return lax.dynamic_slice_in_dim(values, index * length, length, axis)


def dot32(left, right, contract):
    return lax.dot_general(left, right, ((contract[:1], contract[1:]), ((), ())), preferred_element_type=jnp.float32)


def in_order(pieces):
    count = len(pieces)
    place = lax.axis_index("dp")
    chosen = []
    for index in range(count):
        step = lax.rem(place - index + count, count)
        picked = pieces[0]
        for other in range(1, count):
            picked = jnp.where(step == other, pieces[other], picked)
        chosen.append(picked)
    return jnp.stack(chosen)


def spread_dp(values):
    return [values] + [shifted(values, "dp", step) for step in range(1, lax.axis_size("dp"))]


def fetch_shards(weight):
    half = part_of(weight, lax.axis_index("core"), 2, 0)
    return [shifted(half, "dp", step) for step in range(1, lax.axis_size("dp"))]


def pass_on(mine):
    return [shifted(piece, "core", 1) for piece in mine]


def gather_weight(weight, mine, other):
    where = jnp.stack([lax.axis_index("dp"), lax.axis_index("core")]).astype(jnp.int32)
    return place_shards(where, weight, mine, other)


def tie(*groups):
    return lax.optimization_barrier(groups)


def send_parts(values, axis):
    count = lax.axis_size(axis)
    place = lax.axis_index(axis)
    own = part_of(values, place, count, 0)
    incoming = [
        shifted(part_of(values, lax.rem(place + step, count), count, 0).astype(jnp.bfloat16), axis, step)
        for step in range(1, count)
    ]
    return own, incoming


def add_parts(own, incoming):
    total = own.astype(jnp.float32)
    for share in incoming:
        total = total + share.astype(jnp.float32)
    return total


def reduce_chain(owned):
    for axis in ("x", "z"):
        own, incoming = yield send_parts(owned, axis)
        owned = add_parts(own, incoming)
    owned = owned.astype(jnp.bfloat16)
    owned, incoming = yield owned, [shifted(owned, "z", step) for step in range(1, lax.axis_size("z"))]
    pieces = jnp.stack([owned] + incoming)
    own = yield [pieces] + [shifted(pieces, "x", step) for step in range(1, lax.axis_size("x"))]
    own, other = yield own, [shifted(piece, "core", 1) for piece in own]
    where = jnp.stack([lax.axis_index(axis) for axis in ("x", "z", "core")]).astype(jnp.int32)
    return assemble(where, own, other)


def weight_chain(inputs, grads):
    core = lax.axis_index("core")
    count = lax.axis_size("dp")
    place = lax.axis_index("dp")
    own_right = part_of(grads, core, 2, 1)
    inputs, other_left, own_right, other_right = yield (
        inputs, shifted(inputs, "core", 1), own_right, shifted(part_of(grads, 1 - core, 2, 1), "core", 1)
    )
    left = jnp.concatenate([inputs, other_left], axis=0)
    right = jnp.concatenate([own_right, other_right], axis=0)
    incoming = []
    for step in range(1, count):
        share = dot32(part_of(left, lax.rem(place + step, count), count, 1), right, (0, 0)).astype(jnp.bfloat16)
        incoming.append(shifted(share, "dp", step))
    left, right, incoming = yield left, right, incoming
    owned = add_parts(dot32(part_of(left, place, count, 1), right, (0, 0)), incoming)
    return (yield from reduce_chain(owned))


def table_chain(local):
    core = lax.axis_index("core")
    own = part_of(local, core, 2, 1)
    own, other = yield own, shifted(part_of(local, 1 - core, 2, 1), "core", 1)
    own, incoming = yield send_parts(own.astype(jnp.float32) + other.astype(jnp.float32), "dp")
    return (yield from reduce_chain(add_parts(own, incoming)))


def share_chain(shares):
    x_count, z_count = shares.shape[:2]
    own, incoming = yield shares[0], [shifted(shares[step], "x", -step) for step in range(1, x_count)]
    total = add_parts(own, incoming)
    low = total.astype(jnp.bfloat16)
    own, incoming = yield total[0], [shifted(low[step], "z", -step) for step in range(1, z_count)]
    return add_parts(own, incoming)


class Flight:
    def __init__(self, chain):
        self.chain = chain
        self.values = next(chain)
        self.result = None

    def land(self, values):
        try:
            self.values = self.chain.send(values)
        except StopIteration as stop:
            self.values, self.result = None, stop.value


def advance(inputs, *flights):
    flights = [flight for flight in flights if flight.values is not None]
    inputs, landed = lax.optimization_barrier((inputs, [flight.values for flight in flights]))
    for flight, values in zip(flights, landed):
        flight.land(values)
    return inputs


def finish(flight):
    while flight.values is not None:
        flight.land(flight.values)
    return flight.result


def sum_all(values):
    for axis in ("core", "dp", "x", "z"):
        values = functools.reduce(
            jnp.add, [shifted(values, axis, step) for step in range(1, lax.axis_size(axis))], values
        )
    return values


def by_group(values):
    wide = values.reshape(values.shape[0], GROUPS, GROUP_DIM)
    wide = jnp.pad(wide, ((0, 0), (0, 0), (0, GROUP_PAD - GROUP_DIM)))
    return jnp.transpose(wide, (1, 0, 2))


def flat_groups(values):
    return jnp.transpose(values[:, :, :GROUP_DIM], (1, 0, 2)).reshape(values.shape[1], D)


def body(
    residues,
    coordinates,
    segment_ids,
    time_steps,
    time_weight,
    norm1_gain,
    norm1_bias,
    qkv_weight,
    bias_weight,
    out_weight,
    norm2_gain,
    norm2_bias,
    up_weight,
    down_weight,
    force_weight,
    out_cotangent,
    force_cotangent,
):
    core = lax.axis_index("core")
    place = lax.axis_index("dp")
    dp_count = lax.axis_size("dp")
    x_count, z_count = lax.axis_size("x"), lax.axis_size("z")
    held = residues.shape[1]

    def take_row(values):
        mine = lax.dynamic_index_in_dim(values, core, 0, keepdims=False)
        other = lax.dynamic_index_in_dim(values, 1 - core, 0, keepdims=False)
        return mine, shifted(other, "core", 1)

    def give_row(values, axis):
        mine = lax.slice_in_dim(values, 0, held, axis=axis)
        other = shifted(lax.slice_in_dim(values, held, 2 * held, axis=axis), "core", 1)
        first_row = jnp.where(core == 0, mine, other)
        second_row = jnp.where(core == 0, other, mine)
        return jnp.stack([first_row, second_row])

    where_own = jnp.concatenate(
        [coordinates, segment_ids[:, None, :].astype(jnp.bfloat16)], axis=1
    )
    where_rows = jnp.concatenate(take_row(where_own), axis=1)
    bias_parts = [bias_weight] + [shifted(bias_weight, "dp", step) for step in range(1, dp_count)]
    residue_parts = take_row(residues)
    my_steps = lax.dynamic_index_in_dim(time_steps, core, 0, keepdims=False)
    step_list = [my_steps] + [shifted(my_steps, "dp", step) for step in range(1, dp_count)]

    where_keys = where_rows[None]
    reach = 1
    while reach < z_count:
        where_keys = jnp.concatenate([where_keys, shifted(where_keys, "z", reach)], axis=0)
        reach *= 2
    where_columns = [where_keys[:z_count]]
    for x_step in range(1, x_count):
        where_columns.append(shifted(where_columns[0], "x", x_step))
    (
        where_columns,
        where_rows,
        bias_parts,
        residue_parts,
        step_list,
        (norm1_gain, norm1_bias, norm2_gain, norm2_bias, force_weight),
        (time_weight, qkv_weight, out_weight, up_weight, down_weight),
        (out_cotangent, force_cotangent),
    ) = tie(
        where_columns,
        where_rows,
        bias_parts,
        residue_parts,
        step_list,
        (norm1_gain, norm1_bias, norm2_gain, norm2_bias, force_weight),
        (time_weight, qkv_weight, out_weight, up_weight, down_weight),
        (out_cotangent, force_cotangent),
    )
    key_where = jnp.transpose(jnp.concatenate(where_columns, axis=0).astype(jnp.float32), (1, 0, 2))
    key_where = jnp.pad(key_where.reshape(4, -1), ((0, 4), (0, 0)))
    query_where = jnp.pad(jnp.transpose(where_rows).astype(jnp.float32), ((0, 0), (0, 4)))
    segment_rows = where_rows[3]
    residue_rows = jnp.concatenate(residue_parts, axis=0).astype(jnp.float32)

    bias_full = in_order(bias_parts).reshape(KERNELS, HEADS)
    order, factor = kernel_order()
    table_weight = (
        jnp.transpose(bias_full).astype(jnp.float32)[:, order] * (factor * LOG2E)
    ).astype(jnp.bfloat16)
    tiles = 2 * held // FINE
    lead = tiles // 8
    bias = pair_bias(query_where, key_where, table_weight, 0, lead, None)

    vectors = in_order(
        spread_dp(jnp.concatenate([jnp.stack([norm1_gain, norm1_bias, norm2_gain, norm2_bias]), force_weight], axis=0))
    )
    vectors = jnp.transpose(vectors, (1, 0, 2)).reshape(7, D)
    gain_one, shift_one, gain_two, shift_two = [vectors[i:i + 1].astype(jnp.float32) for i in range(4)]
    force_full = vectors[4:]
    proteins = my_steps.shape[0]
    features = time_features(jnp.concatenate(step_list).astype(jnp.float32), D).astype(jnp.bfloat16)
    features = part_of(features, place, dp_count, 1)
    stamp_part = jnp.dot(features, time_weight, preferred_element_type=jnp.float32)
    stamp_rows = stamp_part[:proteins]
    for step in range(1, dp_count):
        stamp_rows = stamp_rows + shifted(
            stamp_part[step * proteins:(step + 1) * proteins], "dp", -step
        )
    query_own, pair_own = qkv_weight[:, :D], qkv_weight[:, D:]
    pair_half = fetch_shards(pair_own)
    query_half = fetch_shards(query_own)
    bias, stamp_rows, vectors_ready = tie(bias, stamp_rows, (gain_one, shift_one))
    gain_one, shift_one = vectors_ready

    def by_protein(table):
        picked = jnp.zeros((2 * held, table.shape[1]), jnp.float32)
        for index in range(proteins):
            picked = picked + jnp.where((segment_rows == index)[:, None], table[index][None, :], 0.0)
        return picked

    first = residue_rows + by_protein(stamp_rows)
    normed, norm_one_back = jax.vjp(layer_norm, first, gain_one, shift_one)
    normed_low = normed.astype(jnp.bfloat16)

    columns = [[None] * z_count for _ in range(x_count)]
    current = normed_low
    done = lead
    out_half = up_half = down_half = None
    for z_step in range(z_count):
        steps = (tiles - done) // (z_count - z_step)
        across = [current]
        for x_step in range(1, x_count):
            across.append(shifted(across[-1], "x", 1))
        following = shifted(current, "z", 1) if z_step < z_count - 1 else current
        bias = pair_bias(query_where, key_where, table_weight, done, steps, bias)
        done += steps
        bias, current, across = tie(bias, following, across)
        for x_step in range(x_count):
            columns[x_step][z_step] = across[x_step]
        if z_step == 1:
            bias, pair_half, query_half, later = tie(bias, pair_half, query_half, (out_weight, up_weight, down_weight))
            out_weight, up_weight, down_weight = later
            out_half, up_half, down_half = fetch_shards(out_weight), fetch_shards(up_weight), fetch_shards(down_weight)
            pair_passed = pass_on(pair_half)
            query_passed = pass_on(query_half)
    normed_all = jnp.concatenate([piece for column in columns for piece in column], axis=0)

    query_weight = gather_weight(query_own, query_half, query_passed)
    pair_weight = gather_weight(pair_own, pair_half, pair_passed)
    query = by_group(jnp.dot(normed_low, query_weight, preferred_element_type=jnp.float32).astype(jnp.bfloat16))
    turned, key_flat, value_flat = project(normed_all, pair_weight)
    probs, attended, inverse = attend(query, turned, value_flat, bias)
    attended_low = flat_groups(attended).astype(jnp.bfloat16)
    attended_low, out_half, up_half, down_half, cotangents = tie(
        attended_low, out_half, up_half, down_half, (out_cotangent, force_cotangent)
    )
    out_cotangent, force_cotangent = cotangents
    out_full = gather_weight(out_weight, out_half, pass_on(out_half))
    up_full = gather_weight(up_weight, up_half, pass_on(up_half))
    down_full = gather_weight(down_weight, down_half, pass_on(down_half))
    cot_rows = jnp.concatenate(take_row(out_cotangent), axis=0).astype(jnp.float32)
    force_cot = jnp.concatenate(take_row(force_cotangent), axis=1)

    second = first + jnp.dot(attended_low, out_full, preferred_element_type=jnp.float32)
    normed_two, norm_two_back = jax.vjp(layer_norm, second, gain_two, shift_two)
    normed_two_low = normed_two.astype(jnp.bfloat16)
    hidden = jnp.dot(normed_two_low, up_full, preferred_element_type=jnp.float32)
    activated, gelu_back = jax.vjp(exact_gelu, hidden)
    activated_low = activated.astype(jnp.bfloat16)
    third = second + jnp.dot(activated_low, down_full, preferred_element_type=jnp.float32)
    block_low = third.astype(jnp.bfloat16)
    forces = jnp.einsum("cd,qd->cq", force_full, block_low, preferred_element_type=jnp.float32)
    third_grad = cot_rows + jnp.einsum(
        "cq,cd->qd", force_cot, force_full.astype(jnp.float32), precision=highest
    )
    force_grad = jnp.einsum(
        "cq,qd->cd", force_cot, block_low.astype(jnp.float32), precision=highest
    )
    third_low = third_grad.astype(jnp.bfloat16)
    activated_grad = dot32(third_low, down_full, (1, 1))
    hidden_grad = gelu_back(activated_grad)[0].astype(jnp.bfloat16)
    normed_two_grad = dot32(hidden_grad, up_full, (1, 1))
    second_part, gain_two_grad, shift_two_grad = norm_two_back(normed_two_grad)
    second_grad = third_grad + second_part
    second_low = second_grad.astype(jnp.bfloat16)
    attended_grad = by_group(dot32(second_low, out_full, (1, 1)).astype(jnp.bfloat16))
    scaled_grad = (attended_grad.astype(jnp.float32) * inverse).astype(jnp.bfloat16)

    down = Flight(weight_chain(activated_low, third_low))
    up = Flight(weight_chain(normed_two_low, hidden_grad))
    out = Flight(weight_chain(attended_low, second_low))

    scaled_grad = advance(scaled_grad, down)
    first_back = attend_back(query, scaled_grad, attended, key_flat, turned, probs, 0, 2)
    first_back, scaled_grad = advance((first_back, scaled_grad), down, up, out)
    second_back = attend_back(query, scaled_grad, attended, key_flat, turned, first_back[0], 1, 2)
    backs = advance([first_back[1:], second_back[1:], second_back[0]], down, up, out)
    logit_grad = backs.pop()
    query_grad = flat_groups(jnp.concatenate([back[0] for back in backs], axis=0)).astype(jnp.bfloat16)
    pair_grad_turn = jnp.concatenate([back[1] for back in backs] + [back[2] for back in backs], axis=0)

    pair_share = dot32(pair_grad_turn, pair_weight, (0, 1)).astype(jnp.bfloat16)
    own = pair_share.reshape(x_count, z_count, 2 * held, D)
    shares = [Flight(share_chain(own[..., part * (D // 2):(part + 1) * (D // 2)])) for part in range(2)]
    query_part = dot32(normed_low, query_grad, (0, 0)).astype(jnp.bfloat16)
    pair_part = dot32(normed_all, pair_grad_turn, (0, 1)).astype(jnp.bfloat16)
    table = Flight(table_chain(jnp.concatenate([query_part, pair_part], axis=1)))

    sums = None
    flights = [down, up, out, table] + shares
    steps = tiles // 4
    for part in range(4):
        logit_grad = advance(logit_grad, *flights)
        piece = table_grad(query_where, key_where, logit_grad, part * steps, steps)
        piece, logit_grad = tie(piece, logit_grad)
        sums = piece if sums is None else sums + piece
    bias_grad = table_sums(sums)
    pair_normed_grad = jnp.concatenate([finish(share) for share in shares], axis=1)
    down_grad, up_grad, out_grad, qkv_grad = [finish(flight) for flight in (down, up, out, table)]

    normed_grad = dot32(query_grad, query_weight, (1, 1)) + pair_normed_grad
    first_part, gain_one_grad, shift_one_grad = norm_one_back(normed_grad)
    first_grad = second_grad + first_part
    first_low = first_grad.astype(jnp.bfloat16).astype(jnp.float32)
    protein_sum = jnp.stack(
        [
            jnp.sum(jnp.where((segment_rows == index)[:, None], first_low, 0.0), axis=0)
            for index in range(proteins)
        ]
    )
    slots = 2 * dp_count
    slot = jnp.arange(slots) == 2 * place + core
    protein_slots = jnp.where(slot[:, None, None], protein_sum[None], 0.0)
    packed = jnp.concatenate(
        [
            gain_one_grad.reshape(-1),
            shift_one_grad.reshape(-1),
            gain_two_grad.reshape(-1),
            shift_two_grad.reshape(-1),
            force_grad.reshape(-1),
            bias_grad.reshape(-1),
            protein_slots.reshape(-1),
        ]
    )
    packed = sum_all(packed)
    vectors = packed[:4 * D].reshape(4, D)
    vectors = part_of(vectors, place, dp_count, 1)
    force_sum = part_of(packed[4 * D:7 * D].reshape(3, D), place, dp_count, 1)
    table_end = 7 * D + KERNELS * HEADS
    bias_sum = part_of(packed[7 * D:table_end].reshape(KERNELS, HEADS), place, dp_count, 0)
    protein_all = packed[table_end:].reshape(slots, proteins, D)
    other_steps = lax.dynamic_index_in_dim(time_steps, 1 - core, 0, keepdims=False)
    both_steps = jnp.where(core == 0, jnp.stack([my_steps, other_steps]), jnp.stack([other_steps, my_steps]))
    all_features = time_features(both_steps.reshape(-1).astype(jnp.float32), D).astype(jnp.bfloat16)
    all_features = in_order(spread_dp(all_features)).reshape(slots * proteins, D)
    time_grad = jnp.einsum(
        "sd,se->de",
        part_of(all_features, place, dp_count, 1).astype(jnp.float32),
        protein_all.reshape(slots * proteins, D),
        precision=highest,
    )

    return (
        give_row(block_low, 0),
        give_row(forces, 1),
        give_row(first_grad, 0),
        time_grad,
        vectors[0],
        vectors[1],
        qkv_grad,
        bias_sum,
        out_grad,
        vectors[2],
        vectors[3],
        up_grad,
        down_grad,
        force_sum,
    )


def solution(mesh):
    chips = mesh.shape["blk"] // 2
    rows = CHIP_ROW if chips % CHIP_ROW == 0 else 1
    fine = jax.sharding.Mesh(
        mesh.devices.reshape(mesh.shape["dp"], rows, chips // rows, 2), ("dp", "z", "x", "core")
    )
    blk = ("z", "x", "core")
    return jax.shard_map(
        body,
        mesh=fine,
        in_specs=(
            P("dp", blk, None),
            P("dp", None, blk),
            P("dp", blk),
            P("dp", None),
            P("dp", None),
            P("dp"),
            P("dp"),
            P("dp", None),
            P("dp", None),
            P("dp", None),
            P("dp"),
            P("dp"),
            P("dp", None),
            P("dp", None),
            P(None, "dp"),
            P("dp", blk, None),
            P("dp", None, blk),
        ),
        out_specs=(
            P("dp", blk, None),
            P("dp", None, blk),
            P("dp", blk, None),
            P("dp", None),
            P("dp"),
            P("dp"),
            P("dp", None),
            P("dp", None),
            P("dp", None),
            P("dp"),
            P("dp"),
            P("dp", None),
            P("dp", None),
            P(None, "dp"),
        ),
        check_vma=False,
    )
```

```python
import functools
import jax
import jax.numpy as jnp
import numpy as np
from jax import lax
from jax.sharding import PartitionSpec as P
from jax.experimental import pallas as pl
from jax.experimental.pallas import tpu as pltpu

D = 768
HEADS = 32
HEAD_DIM = 24
KERNELS = 128
GROUPS = 4
GROUP_HEADS = 8
GROUP_DIM = 192
GROUP_PAD = 256
LOG2E = 1.4426950408889634
SCALE = HEAD_DIM ** -0.5
SPAN = 8
NA = KERNELS // SPAN
masked_value = -1e30
VMEM_LIMIT = 60 * 2**20
FORWARD_TILE = 32
BACKWARD_TILE = 64
FINE = 8
KERNEL_COST = 2.5e8


def cost(micros, bytes_moved):
    return pl.CostEstimate(flops=int(micros * KERNEL_COST), bytes_accessed=int(bytes_moved), transcendentals=0)


def distance_tile(q_ref, k_ref):
    total = None
    for axis in range(3):
        offset = q_ref[:, axis:axis + 1] - k_ref[axis:axis + 1, :]
        total = offset * offset if total is None else total + offset * offset
    return jnp.sqrt(total) * (KERNELS / 48.0)


def kernel_rows(x):
    centre = lax.broadcasted_iota(jnp.int32, (NA, 1), 0).astype(jnp.float32) * (SPAN / 2.0) + SPAN / 4.0
    y = jnp.clip(x - centre, -24.0, 24.0)
    up_step = jnp.exp2(y * (0.5 * LOG2E))
    down_step = jnp.exp2(y * (-0.5 * LOG2E))
    middle = jnp.exp2((y * y) * (-0.5 * LOG2E))
    above = [middle]
    for _ in range(SPAN // 2 - 1):
        above.append(above[-1] * up_step)
    below = []
    current = middle
    for _ in range(SPAN // 2):
        current = current * down_step
        below.append(current)
    rows = below[::-1] + above
    return jnp.concatenate([r.astype(jnp.bfloat16) for r in rows], axis=0)


def kernel_order():
    step = np.arange(SPAN) - SPAN // 2
    order = np.array([[a * SPAN + SPAN // 2 + b for a in range(NA)] for b in step]).reshape(-1)
    factor = np.repeat(np.exp(-(step ** 2) / 8.0), NA).astype(np.float32)
    return order, factor


def bias_kernel(chunk, q_ref, k_ref, w_ref, *refs):
    out_ref, x_ref, m_ref = refs[-3:]
    rows = q_ref.shape[0]
    keys = k_ref.shape[1]
    x_ref[...] = distance_tile(q_ref, k_ref)
    m_ref[...] = jnp.where(q_ref[:, 3:4] == k_ref[3:4, :], 0.0, masked_value)
    w = w_ref[...]

    def step(t, carry):
        for start in range(0, keys, chunk):
            cols = slice(start, start + chunk)
            values = []
            for q in (2 * t, 2 * t + 1):
                value = jnp.dot(w, kernel_rows(x_ref[pl.ds(q, 1), cols]), preferred_element_type=jnp.float32)
                values.append(value + m_ref[pl.ds(q, 1), cols])
            for g in range(GROUPS):
                both = jnp.concatenate([value[g * GROUP_HEADS:(g + 1) * GROUP_HEADS] for value in values], axis=0)
                out_ref[g, pl.ds(t * 2 * GROUP_HEADS, 2 * GROUP_HEADS), cols] = both.astype(out_ref.dtype)
        return carry

    lax.fori_loop(0, rows // 2, step, 0, unroll=True)


def pair_bias(q_where, k_where, w, first, steps, previous):
    rows, keys = q_where.shape[0], k_where.shape[1]
    in_specs = [
        pl.BlockSpec((FINE, 8), lambda i: (i + first, 0)),
        pl.BlockSpec((8, keys), lambda i: (0, 0)),
        pl.BlockSpec((HEADS, KERNELS), lambda i: (0, 0)),
    ]
    operands = [q_where, k_where, w]
    aliases = {}
    if previous is not None:
        in_specs.append(pl.BlockSpec(memory_space=pl.ANY))
        operands.append(previous)
        aliases = {3: 0}
    return pl.pallas_call(
        functools.partial(bias_kernel, 256),
        grid=(steps,),
        in_specs=in_specs,
        out_specs=pl.BlockSpec((GROUPS, FINE * GROUP_HEADS, keys), lambda i: (0, i + first, 0)),
        out_shape=jax.ShapeDtypeStruct((GROUPS, rows * GROUP_HEADS, keys), jnp.bfloat16),
        scratch_shapes=[pltpu.VMEM((FINE, keys), jnp.float32), pltpu.VMEM((FINE, keys), jnp.float32)],
        input_output_aliases=aliases,
        cost_estimate=cost(1.5 * steps, FINE * steps * HEADS * keys * 2),
        compiler_params=pltpu.CompilerParams(vmem_limit_bytes=VMEM_LIMIT),
        name="pair_bias",
    )(*operands)


def project_kernel(x_ref, w_ref, turn_ref, key_ref, value_ref, w_turn_ref):
    @pl.when(pl.program_id(0) == 0)
    def turn_weight():
        w_turn_ref[...] = w_ref[...].T

    x = x_ref[...]
    rows = x.shape[0]
    turn_ref[...] = lax.dot_general(
        w_turn_ref[...], x, (((1,), (1,)), ((), ())), preferred_element_type=jnp.float32
    ).astype(turn_ref.dtype)
    flat = jnp.dot(x, w_ref[...], preferred_element_type=jnp.float32)
    for out_ref, first, filler in ((key_ref, 0, 0.0), (value_ref, D, 1.0)):
        for g in range(GROUPS):
            part = flat[:, first + g * GROUP_DIM:first + (g + 1) * GROUP_DIM]
            wide = jnp.concatenate([part, jnp.full((rows, GROUP_PAD - GROUP_DIM), filler, jnp.float32)], axis=1)
            out_ref[:, g * GROUP_PAD:(g + 1) * GROUP_PAD] = wide.astype(out_ref.dtype)


def project(values, weight):
    keys, depth = values.shape
    width = weight.shape[1]
    wide = GROUPS * GROUP_PAD
    block = 256
    return pl.pallas_call(
        project_kernel,
        grid=(keys // block,),
        in_specs=[
            pl.BlockSpec((block, depth), lambda i: (i, 0)),
            pl.BlockSpec((depth, width), lambda i: (0, 0)),
        ],
        out_specs=[
            pl.BlockSpec((width, block), lambda i: (0, i)),
            pl.BlockSpec((block, wide), lambda i: (i, 0)),
            pl.BlockSpec((block, wide), lambda i: (i, 0)),
        ],
        out_shape=[
            jax.ShapeDtypeStruct((width, keys), jnp.bfloat16),
            jax.ShapeDtypeStruct((keys, wide), jnp.bfloat16),
            jax.ShapeDtypeStruct((keys, wide), jnp.bfloat16),
        ],
        scratch_shapes=[pltpu.VMEM((width, depth), jnp.bfloat16)],
        cost_estimate=cost(12, keys * (depth + 3 * width) * 2),
        compiler_params=pltpu.CompilerParams(vmem_limit_bytes=VMEM_LIMIT),
        name="project",
    )(values, weight)


def head_mask(width):
    head = lax.broadcasted_iota(jnp.int32, (GROUP_HEADS, width), 0)
    lane = lax.broadcasted_iota(jnp.int32, (GROUP_HEADS, width), 1)
    return ((lane >= head * HEAD_DIM) & (lane < (head + 1) * HEAD_DIM)).astype(jnp.float32)


def spread_heads(values, mask):
    rows, width = values.shape
    return (values[:, None, :] * mask[None]).reshape(rows * GROUP_HEADS, width)


def gather_heads(values, mask):
    rows, width = values.shape
    return jnp.sum(values.reshape(rows // GROUP_HEADS, GROUP_HEADS, width) * mask[None], axis=1)


def forward_kernel(chunk, q_ref, kt_ref, v_ref, bias_ref, p_ref, o_ref, inv_ref, s_ref):
    keys = kt_ref.shape[1]
    mask = head_mask(GROUP_PAD)

    for g in range(GROUPS):
        rows = slice(g * GROUP_DIM, (g + 1) * GROUP_DIM)
        spread = spread_heads(q_ref[g].astype(jnp.float32), mask).astype(jnp.bfloat16)[:, :GROUP_DIM]
        peak = None
        for start in range(0, keys, chunk):
            s = jnp.dot(spread, kt_ref[rows, start:start + chunk], preferred_element_type=jnp.float32)
            s = s * (SCALE * LOG2E) + bias_ref[g, :, start:start + chunk].astype(jnp.float32)
            s_ref[:, start:start + chunk] = s
            for lane in range(0, chunk, 128):
                part = s[:, lane:lane + 128]
                peak = part if peak is None else jnp.maximum(peak, part)
        top = jnp.max(peak, axis=1, keepdims=True)
        for start in range(0, keys, chunk):
            p_ref[g, :, start:start + chunk] = jnp.exp2(s_ref[:, start:start + chunk] - top).astype(jnp.bfloat16)
        mixed = jnp.dot(p_ref[g], v_ref[:, g * GROUP_PAD:(g + 1) * GROUP_PAD], preferred_element_type=jnp.float32)
        inverse = 1.0 / mixed[:, GROUP_DIM:GROUP_DIM + 1]
        o_ref[g] = gather_heads(mixed * inverse, mask)
        inv_ref[g] = gather_heads(jnp.broadcast_to(inverse, mixed.shape), mask)


def attend(q, turned, value_flat, bias):
    rows, keys = q.shape[1], turned.shape[1]
    tile = min(FORWARD_TILE, FORWARD_TILE * 2048 // keys)
    whole = pl.Buffered(1)
    return pl.pallas_call(
        functools.partial(forward_kernel, 512),
        grid=(rows // tile,),
        in_specs=[
            pl.BlockSpec((GROUPS, tile, GROUP_PAD), lambda i: (0, i, 0)),
            pl.BlockSpec((D, keys), lambda i: (0, 0), pipeline_mode=whole),
            pl.BlockSpec((keys, GROUPS * GROUP_PAD), lambda i: (0, 0), pipeline_mode=whole),
            pl.BlockSpec((GROUPS, tile * GROUP_HEADS, keys), lambda i: (0, i, 0)),
        ],
        out_specs=[
            pl.BlockSpec((GROUPS, tile * GROUP_HEADS, keys), lambda i: (0, i, 0)),
            pl.BlockSpec((GROUPS, tile, GROUP_PAD), lambda i: (0, i, 0)),
            pl.BlockSpec((GROUPS, tile, GROUP_PAD), lambda i: (0, i, 0)),
        ],
        out_shape=[
            jax.ShapeDtypeStruct((GROUPS, rows * GROUP_HEADS, keys), jnp.bfloat16),
            jax.ShapeDtypeStruct((GROUPS, rows, GROUP_PAD), jnp.float32),
            jax.ShapeDtypeStruct((GROUPS, rows, GROUP_PAD), jnp.float32),
        ],
        scratch_shapes=[
            pltpu.VMEM((tile * GROUP_HEADS, keys), jnp.float32),
        ],
        input_output_aliases={3: 0},
        cost_estimate=cost(45, rows * HEADS * keys * 4),
        compiler_params=pltpu.CompilerParams(vmem_limit_bytes=VMEM_LIMIT),
        name="attend",
    )(q, turned, value_flat, bias)


def backward_kernel(chunk, q_ref, do_ref, o_ref, k_ref, vt_ref, p_ref, ds_ref, dq_ref, dkt_ref, dvt_ref, dk_acc, dv_acc):
    keys = vt_ref.shape[1]
    mask = head_mask(GROUP_PAD)
    tile = pl.program_id(0)
    groups = q_ref.shape[0]

    @pl.when(tile == 0)
    def start_group():
        dk_acc[...] = jnp.zeros_like(dk_acc)
        dv_acc[...] = jnp.zeros_like(dv_acc)

    for g in range(groups):
        rows = slice(g * GROUP_DIM, (g + 1) * GROUP_DIM)
        q_wide = spread_heads(q_ref[g].astype(jnp.float32), mask)
        do_wide = spread_heads(do_ref[g].astype(jnp.float32), mask)
        o_wide = spread_heads(o_ref[g], mask)
        delta = jnp.sum(do_wide * o_wide, axis=1, keepdims=True)
        do_low = do_wide.astype(jnp.bfloat16)[:, :GROUP_DIM]
        do_turn = do_wide[:, :GROUP_DIM].T.astype(jnp.bfloat16)
        q_turn = q_wide[:, :GROUP_DIM].T.astype(jnp.bfloat16)
        for start in range(0, keys, chunk):
            cols = slice(start, start + chunk)
            dp = jnp.dot(do_low, vt_ref[rows, cols], preferred_element_type=jnp.float32)
            p = p_ref[g, :, cols]
            ds = (p.astype(jnp.float32) * (dp - delta)).astype(jnp.bfloat16)
            ds_ref[g, :, cols] = ds
            dv_acc[rows, cols] += jnp.dot(do_turn, p, preferred_element_type=jnp.float32)
            dk_acc[rows, cols] += jnp.dot(q_turn, ds, preferred_element_type=jnp.float32)
        dq = jnp.dot(ds_ref[g], k_ref[:, g * GROUP_PAD:(g + 1) * GROUP_PAD], preferred_element_type=jnp.float32)
        dq_ref[g] = gather_heads(dq, mask) * SCALE

    @pl.when(tile == pl.num_programs(0) - 1)
    def finish():
        dkt_ref[...] = (dk_acc[...] * SCALE).astype(dkt_ref.dtype)
        dvt_ref[...] = dv_acc[...].astype(dvt_ref.dtype)


def attend_back(q, do, o, key_flat, turned, p, part, parts):
    rows, keys = q.shape[1], turned.shape[1]
    tile = min(BACKWARD_TILE, BACKWARD_TILE * 2048 // keys)
    groups = GROUPS // parts
    width = groups * GROUP_DIM
    whole = pl.Buffered(1)
    narrow = pl.BlockSpec((groups, tile, GROUP_PAD), lambda i: (part, i, 0))
    return pl.pallas_call(
        functools.partial(backward_kernel, 512),
        grid=(rows // tile,),
        in_specs=[
            narrow,
            narrow,
            narrow,
            pl.BlockSpec((keys, groups * GROUP_PAD), lambda i: (0, part), pipeline_mode=whole),
            pl.BlockSpec((width, keys), lambda i: (part + parts, 0), pipeline_mode=whole),
            pl.BlockSpec((groups, tile * GROUP_HEADS, keys), lambda i: (part, i, 0)),
        ],
        out_specs=[
            pl.BlockSpec((groups, tile * GROUP_HEADS, keys), lambda i: (part, i, 0)),
            pl.BlockSpec((groups, tile, GROUP_PAD), lambda i: (0, i, 0)),
            pl.BlockSpec((width, keys), lambda i: (0, 0), pipeline_mode=whole),
            pl.BlockSpec((width, keys), lambda i: (0, 0), pipeline_mode=whole),
        ],
        out_shape=[
            jax.ShapeDtypeStruct(p.shape, p.dtype),
            jax.ShapeDtypeStruct((groups, rows, GROUP_PAD), jnp.float32),
            jax.ShapeDtypeStruct((width, keys), jnp.bfloat16),
            jax.ShapeDtypeStruct((width, keys), jnp.bfloat16),
        ],
        scratch_shapes=[
            pltpu.VMEM((width, keys), jnp.float32),
            pltpu.VMEM((width, keys), jnp.float32),
        ],
        input_output_aliases={5: 0},
        cost_estimate=cost(56 / parts, rows * HEADS * keys * 4 // parts),
        compiler_params=pltpu.CompilerParams(vmem_limit_bytes=VMEM_LIMIT),
        name="attend_back",
    )(q, do, o, key_flat, turned, p)


def table_grad_kernel(chunk, q_ref, k_ref, ds_ref, out_ref, x_ref):
    rows = q_ref.shape[0]
    keys = k_ref.shape[1]
    pair = 2 * GROUP_HEADS

    @pl.when(pl.program_id(0) == 0)
    def start_zero():
        out_ref[...] = jnp.zeros_like(out_ref)

    x_ref[...] = distance_tile(q_ref, k_ref)

    def step(t, total):
        for start in range(0, keys, chunk):
            x = x_ref[pl.ds(2 * t, 2), start:start + chunk]
            table = jnp.concatenate([kernel_rows(x[0:1]), kernel_rows(x[1:2])], axis=0)
            grads = jnp.concatenate(
                [ds_ref[g, pl.ds(t * pair, pair), start:start + chunk] for g in range(GROUPS)], axis=0
            )
            total = total + lax.dot_general(table, grads, (((1,), (1,)), ((), ())), preferred_element_type=jnp.float32)
        return total

    out_ref[...] += lax.fori_loop(0, rows // 2, step, jnp.zeros(out_ref.shape, jnp.float32), unroll=True)


def table_grad(q_where, k_where, ds, first, steps):
    rows, keys = q_where.shape[0], k_where.shape[1]
    wide = 2 * HEADS
    return pl.pallas_call(
        functools.partial(table_grad_kernel, 256),
        grid=(steps,),
        in_specs=[
            pl.BlockSpec((FINE, 8), lambda i: (i + first, 0)),
            pl.BlockSpec((8, keys), lambda i: (0, 0)),
            pl.BlockSpec((GROUPS, FINE * GROUP_HEADS, keys), lambda i: (0, i + first, 0)),
        ],
        out_specs=pl.BlockSpec((2 * KERNELS, wide), lambda i: (0, 0)),
        out_shape=jax.ShapeDtypeStruct((2 * KERNELS, wide), jnp.float32),
        scratch_shapes=[pltpu.VMEM((FINE, keys), jnp.float32)],
        cost_estimate=cost(1.6 * steps, FINE * steps * HEADS * keys * 2),
        compiler_params=pltpu.CompilerParams(vmem_limit_bytes=VMEM_LIMIT),
        name="table_grad",
    )(q_where, k_where, ds)


def table_sums(sums):
    sums = sums.reshape(2, KERNELS, GROUPS, 2, GROUP_HEADS)
    both = (sums[0, :, :, 0] + sums[1, :, :, 1]).reshape(KERNELS, HEADS)
    order, factor = kernel_order()
    return (both * factor[:, None])[np.argsort(order)]


def place_kernel(steps, s_ref, *refs):
    own_ref = refs[0]
    mine, other = refs[1:1 + steps], refs[1 + steps:1 + 2 * steps]
    out_ref = refs[-1]
    j = pl.program_id(0)
    place, core = s_ref[0], s_ref[1]
    away = lax.rem(place - j // 2 + steps + 1, steps + 1)

    @pl.when(away == 0)
    def own_part():
        out_ref[...] = own_ref[...]

    for step in range(1, steps + 1):
        @pl.when((away == step) & (core == j % 2))
        def fetched_part():
            out_ref[...] = mine[step - 1][...]

        @pl.when((away == step) & (core != j % 2))
        def passed_part():
            out_ref[...] = other[step - 1][...]


def place_shards(where, own, mine, other):
    steps = len(mine)
    rows, columns = own.shape
    half = rows // 2
    fixed = pl.BlockSpec((half, columns), lambda j, s: (0, 0))
    return pl.pallas_call(
        functools.partial(place_kernel, steps),
        grid_spec=pltpu.PrefetchScalarGridSpec(
            num_scalar_prefetch=1,
            grid=(2 * (steps + 1),),
            in_specs=[pl.BlockSpec((half, columns), lambda j, s: (j % 2, 0))] + [fixed] * (2 * steps),
            out_specs=pl.BlockSpec((half, columns), lambda j, s: (j, 0)),
        ),
        out_shape=jax.ShapeDtypeStruct(((steps + 1) * rows, columns), own.dtype),
        cost_estimate=cost(3, 2 * (steps + 1) * own.size * 2),
        compiler_params=pltpu.CompilerParams(vmem_limit_bytes=VMEM_LIMIT),
        name="place_shards",
    )(where, own, *mine, *other)


def assemble_kernel(xs, widths, s_ref, *refs):
    own_refs, other_refs, out_refs = refs[:xs], refs[xs:2 * xs], refs[2 * xs:]
    zs = own_refs[0].shape[0]
    x, core = s_ref[0], s_ref[1]
    jx = pl.program_id(0)
    from_x = lax.rem(x - jx + xs, xs)
    first = core == 0
    for step in range(xs):
        @pl.when(from_x == step)
        def copy_piece():
            for jz in range(zs):
                begin = 0
                for half, out_ref in zip(widths, out_refs):
                    own = own_refs[step][jz, :, begin:begin + half].astype(jnp.float32)
                    other = other_refs[step][jz, :, begin:begin + half].astype(jnp.float32)
                    out_ref[0, jz, :, :half] = jnp.where(first, own, other)
                    out_ref[0, jz, :, half:] = jnp.where(first, other, own)
                    begin += half


def assemble(where, own, other, widths):
    xs = len(own)
    zs, rows, columns = own[0].shape
    spec = pl.BlockSpec((zs, rows, columns), lambda i, s: (0, 0, 0))
    wholes = pl.pallas_call(
        functools.partial(assemble_kernel, xs, widths),
        grid_spec=pltpu.PrefetchScalarGridSpec(
            num_scalar_prefetch=1,
            grid=(xs,),
            in_specs=[spec] * (2 * xs),
            out_specs=[pl.BlockSpec((1, zs, rows, 2 * half), lambda i, s: (i, 0, 0, 0)) for half in widths],
        ),
        out_shape=[jax.ShapeDtypeStruct((xs, zs, rows, 2 * half), jnp.float32) for half in widths],
        cost_estimate=cost(4, xs * zs * rows * columns * 12),
        compiler_params=pltpu.CompilerParams(vmem_limit_bytes=VMEM_LIMIT),
        name="assemble",
    )(where, *own, *other)
    return [whole.reshape(xs * zs * rows, -1) for whole in wholes]


eps = 1e-05
highest = lax.Precision.HIGHEST
CHIP_ROW = 4
Z_EXCHANGE = True


def layer_norm(values, norm_gain, norm_shift):
    centred = values - jnp.mean(values, axis=-1, keepdims=True)
    spread = jnp.mean(centred * centred, axis=-1, keepdims=True)
    return centred * lax.rsqrt(spread + eps) * norm_gain + norm_shift


def exact_gelu(values):
    return jax.nn.gelu(values, approximate=False)


def time_features(stamps, feature_width):
    half_width = feature_width // 2
    frequency = jnp.exp(-jnp.log(10000.0) * jnp.arange(half_width, dtype=jnp.float32) / half_width)
    angles = stamps[:, None] * frequency[None, :]
    return jnp.concatenate([jnp.sin(angles), jnp.cos(angles)], axis=1)


def shifted(values, axis, step):
    size = lax.axis_size(axis)
    return lax.ppermute(values, axis, [(i, (i + step) % size) for i in range(size)])


def part_of(values, index, count, axis):
    length = values.shape[axis] // count
    return lax.dynamic_slice_in_dim(values, index * length, length, axis)


def dot32(left, right, contract):
    return lax.dot_general(left, right, ((contract[:1], contract[1:]), ((), ())), preferred_element_type=jnp.float32)


def in_order(pieces):
    count = len(pieces)
    place = lax.axis_index("dp")
    chosen = []
    for index in range(count):
        step = lax.rem(place - index + count, count)
        picked = pieces[0]
        for other in range(1, count):
            picked = jnp.where(step == other, pieces[other], picked)
        chosen.append(picked)
    return jnp.stack(chosen)


def spread_dp(values):
    return [values] + [shifted(values, "dp", step) for step in range(1, lax.axis_size("dp"))]


def fetch_shards(weight):
    half = part_of(weight, lax.axis_index("core"), 2, 0)
    return [shifted(half, "dp", step) for step in range(1, lax.axis_size("dp"))]


def pass_on(mine):
    return [shifted(piece, "core", 1) for piece in mine]


def gather_weight(weight, mine, other):
    where = jnp.stack([lax.axis_index("dp"), lax.axis_index("core")]).astype(jnp.int32)
    return place_shards(where, weight, mine, other)


def tie(*groups):
    return lax.optimization_barrier(groups)


def add_parts(own, incoming):
    total = own.astype(jnp.float32)
    for share in incoming:
        total = total + share.astype(jnp.float32)
    return total


def turn_back(values, axis):
    count, place = lax.axis_size(axis), lax.axis_index(axis)
    ring = jnp.concatenate([values, values], axis=0)[::-1]
    return lax.dynamic_slice_in_dim(ring, count - 1 - place, count, 0)


def reduce_chain(local, hops, widths):
    left = ["dp", "x", "z"]
    for axis in hops:
        dim = left.index(axis)
        left.pop(dim)
        count, place = lax.axis_size(axis), lax.axis_index(axis)
        if axis == "z" and Z_EXCHANGE:
            local = yield lax.all_to_all(local.astype(jnp.bfloat16), "z", dim, 0)
            local = jnp.sum(local.astype(jnp.float32), axis=0)
            continue
        own = lax.dynamic_index_in_dim(local, place, dim, keepdims=False)
        incoming = [
            shifted(
                lax.dynamic_index_in_dim(local, lax.rem(place + step, count), dim, keepdims=False).astype(jnp.bfloat16),
                axis,
                step,
            )
            for step in range(1, count)
        ]
        own, incoming = yield own, incoming
        local = add_parts(own, incoming)
    owned = local.astype(jnp.bfloat16)
    if Z_EXCHANGE:
        copies = jnp.broadcast_to(owned[None], (lax.axis_size("z"),) + owned.shape)
        pieces = yield lax.all_to_all(copies, "z", 0, 0)
    else:
        owned, incoming = yield owned, [shifted(owned, "z", step) for step in range(1, lax.axis_size("z"))]
        pieces = turn_back(jnp.stack([owned] + incoming), "z")
    own = yield [pieces] + [shifted(pieces, "x", step) for step in range(1, lax.axis_size("x"))]
    own, other = yield own, [shifted(piece, "core", 1) for piece in own]
    where = jnp.stack([lax.axis_index(axis) for axis in ("x", "core")]).astype(jnp.int32)
    return assemble(where, own, other, widths)


def by_owner(values):
    counts = [lax.axis_size(axis) for axis in ("dp", "x", "z")]
    return values.reshape(counts + [-1, values.shape[1]])


def weight_chain(factors, hops):
    core = lax.axis_index("core")
    moving = []
    for inputs, grads in factors:
        moving.append((
            inputs, shifted(inputs, "core", 1),
            part_of(grads, core, 2, 1), shifted(part_of(grads, 1 - core, 2, 1), "core", 1),
        ))
    moving = yield moving
    local = [
        dot32(jnp.concatenate([left, other_left], axis=0), jnp.concatenate([right, other_right], axis=0), (0, 0))
        .astype(jnp.bfloat16)
        for left, other_left, right, other_right in moving
    ]
    return (yield from reduce_chain(by_owner(jnp.concatenate(local, axis=1)), hops, [part.shape[1] for part in local]))


def table_chain(local, hops):
    core = lax.axis_index("core")
    own = part_of(local, core, 2, 1)
    own, other = yield own, shifted(part_of(local, 1 - core, 2, 1), "core", 1)
    chip = (own.astype(jnp.float32) + other.astype(jnp.float32)).astype(jnp.bfloat16)
    return (yield from reduce_chain(by_owner(chip), hops, [chip.shape[1]]))


def share_chain(shares):
    x_count, z_count = shares.shape[:2]
    own, incoming = yield shares[0], [shifted(shares[step], "x", -step) for step in range(1, x_count)]
    total = add_parts(own, incoming)
    if Z_EXCHANGE:
        low = turn_back(total.astype(jnp.bfloat16), "z")
        return jnp.sum((yield lax.all_to_all(low, "z", 0, 0)).astype(jnp.float32), axis=0)
    low = total.astype(jnp.bfloat16)
    own, incoming = yield total[0], [shifted(low[step], "z", -step) for step in range(1, z_count)]
    return add_parts(own, incoming)


class Flight:
    def __init__(self, chain):
        self.chain = chain
        self.values = next(chain)
        self.result = None

    def land(self, values):
        try:
            self.values = self.chain.send(values)
        except StopIteration as stop:
            self.values, self.result = None, stop.value


def advance(inputs, *flights):
    flights = [flight for flight in flights if flight.values is not None]
    inputs, landed = lax.optimization_barrier((inputs, [flight.values for flight in flights]))
    for flight, values in zip(flights, landed):
        flight.land(values)
    return inputs


def finish(flight):
    while flight.values is not None:
        flight.land(flight.values)
    return flight.result


def sum_all(values):
    for axis in ("core", "dp", "x", "z"):
        values = functools.reduce(
            jnp.add, [shifted(values, axis, step) for step in range(1, lax.axis_size(axis))], values
        )
    return values


def by_group(values):
    wide = values.reshape(values.shape[0], GROUPS, GROUP_DIM)
    wide = jnp.pad(wide, ((0, 0), (0, 0), (0, GROUP_PAD - GROUP_DIM)))
    return jnp.transpose(wide, (1, 0, 2))


def flat_groups(values):
    return jnp.transpose(values[:, :, :GROUP_DIM], (1, 0, 2)).reshape(values.shape[1], D)


def body(
    residues,
    coordinates,
    segment_ids,
    time_steps,
    time_weight,
    norm1_gain,
    norm1_bias,
    qkv_weight,
    bias_weight,
    out_weight,
    norm2_gain,
    norm2_bias,
    up_weight,
    down_weight,
    force_weight,
    out_cotangent,
    force_cotangent,
):
    core = lax.axis_index("core")
    place = lax.axis_index("dp")
    dp_count = lax.axis_size("dp")
    x_count, z_count = lax.axis_size("x"), lax.axis_size("z")
    held = residues.shape[1]

    def take_row(values):
        mine = lax.dynamic_index_in_dim(values, core, 0, keepdims=False)
        other = lax.dynamic_index_in_dim(values, 1 - core, 0, keepdims=False)
        return mine, shifted(other, "core", 1)

    def give_row(values, axis):
        mine = lax.slice_in_dim(values, 0, held, axis=axis)
        other = shifted(lax.slice_in_dim(values, held, 2 * held, axis=axis), "core", 1)
        first_row = jnp.where(core == 0, mine, other)
        second_row = jnp.where(core == 0, other, mine)
        return jnp.stack([first_row, second_row])

    where_own = jnp.concatenate(
        [coordinates, segment_ids[:, None, :].astype(jnp.bfloat16)], axis=1
    )
    where_rows = jnp.concatenate(take_row(where_own), axis=1)
    bias_parts = [bias_weight] + [shifted(bias_weight, "dp", step) for step in range(1, dp_count)]
    residue_parts = take_row(residues)
    my_steps = lax.dynamic_index_in_dim(time_steps, core, 0, keepdims=False)
    step_list = [my_steps] + [shifted(my_steps, "dp", step) for step in range(1, dp_count)]

    where_keys = where_rows[None]
    reach = 1
    while reach < z_count:
        where_keys = jnp.concatenate([where_keys, shifted(where_keys, "z", reach)], axis=0)
        reach *= 2
    where_columns = [where_keys[:z_count]]
    for x_step in range(1, x_count):
        where_columns.append(shifted(where_columns[0], "x", x_step))
    (
        where_columns,
        where_rows,
        bias_parts,
        residue_parts,
        step_list,
        (norm1_gain, norm1_bias, norm2_gain, norm2_bias, force_weight),
        (time_weight, qkv_weight, out_weight, up_weight, down_weight),
        (out_cotangent, force_cotangent),
    ) = tie(
        where_columns,
        where_rows,
        bias_parts,
        residue_parts,
        step_list,
        (norm1_gain, norm1_bias, norm2_gain, norm2_bias, force_weight),
        (time_weight, qkv_weight, out_weight, up_weight, down_weight),
        (out_cotangent, force_cotangent),
    )
    key_where = jnp.transpose(jnp.concatenate(where_columns, axis=0).astype(jnp.float32), (1, 0, 2))
    key_where = jnp.pad(key_where.reshape(4, -1), ((0, 4), (0, 0)))
    query_where = jnp.pad(jnp.transpose(where_rows).astype(jnp.float32), ((0, 0), (0, 4)))
    segment_rows = where_rows[3]
    residue_rows = jnp.concatenate(residue_parts, axis=0).astype(jnp.float32)

    bias_full = in_order(bias_parts).reshape(KERNELS, HEADS)
    order, factor = kernel_order()
    table_weight = (
        jnp.transpose(bias_full).astype(jnp.float32)[:, order] * (factor * LOG2E)
    ).astype(jnp.bfloat16)
    tiles = 2 * held // FINE
    lead = tiles // 8
    bias = pair_bias(query_where, key_where, table_weight, 0, lead, None)

    vectors = in_order(
        spread_dp(jnp.concatenate([jnp.stack([norm1_gain, norm1_bias, norm2_gain, norm2_bias]), force_weight], axis=0))
    )
    vectors = jnp.transpose(vectors, (1, 0, 2)).reshape(7, D)
    gain_one, shift_one, gain_two, shift_two = [vectors[i:i + 1].astype(jnp.float32) for i in range(4)]
    force_full = vectors[4:]
    proteins = my_steps.shape[0]
    features = time_features(jnp.concatenate(step_list).astype(jnp.float32), D).astype(jnp.bfloat16)
    features = part_of(features, place, dp_count, 1)
    stamp_part = jnp.dot(features, time_weight, preferred_element_type=jnp.float32)
    stamp_rows = stamp_part[:proteins]
    for step in range(1, dp_count):
        stamp_rows = stamp_rows + shifted(
            stamp_part[step * proteins:(step + 1) * proteins], "dp", -step
        )
    query_own, pair_own = qkv_weight[:, :D], qkv_weight[:, D:]
    pair_half = fetch_shards(pair_own)
    query_half = fetch_shards(query_own)
    bias, stamp_rows, vectors_ready = tie(bias, stamp_rows, (gain_one, shift_one))
    gain_one, shift_one = vectors_ready

    def by_protein(table):
        picked = jnp.zeros((2 * held, table.shape[1]), jnp.float32)
        for index in range(proteins):
            picked = picked + jnp.where((segment_rows == index)[:, None], table[index][None, :], 0.0)
        return picked

    first = residue_rows + by_protein(stamp_rows)
    normed, norm_one_back = jax.vjp(layer_norm, first, gain_one, shift_one)
    normed_low = normed.astype(jnp.bfloat16)

    columns = [[None] * z_count for _ in range(x_count)]
    current = normed_low
    done = lead
    out_half = up_half = down_half = None
    for z_step in range(z_count):
        steps = (tiles - done) // (z_count - z_step)
        across = [current]
        for x_step in range(1, x_count):
            across.append(shifted(across[-1], "x", 1))
        following = shifted(current, "z", 1) if z_step < z_count - 1 else current
        bias = pair_bias(query_where, key_where, table_weight, done, steps, bias)
        done += steps
        bias, current, across = tie(bias, following, across)
        for x_step in range(x_count):
            columns[x_step][z_step] = across[x_step]
        if z_step == 1:
            bias, pair_half, query_half, later = tie(bias, pair_half, query_half, (out_weight, up_weight, down_weight))
            out_weight, up_weight, down_weight = later
            out_half, up_half, down_half = fetch_shards(out_weight), fetch_shards(up_weight), fetch_shards(down_weight)
            pair_passed = pass_on(pair_half)
            query_passed = pass_on(query_half)
    normed_all = jnp.concatenate([piece for column in columns for piece in column], axis=0)

    query_weight = gather_weight(query_own, query_half, query_passed)
    pair_weight = gather_weight(pair_own, pair_half, pair_passed)
    query = by_group(jnp.dot(normed_low, query_weight, preferred_element_type=jnp.float32).astype(jnp.bfloat16))
    turned, key_flat, value_flat = project(normed_all, pair_weight)
    probs, attended, inverse = attend(query, turned, value_flat, bias)
    attended_low = flat_groups(attended).astype(jnp.bfloat16)
    attended_low, out_half, up_half, down_half, cotangents = tie(
        attended_low, out_half, up_half, down_half, (out_cotangent, force_cotangent)
    )
    out_cotangent, force_cotangent = cotangents
    out_full = gather_weight(out_weight, out_half, pass_on(out_half))
    up_full = gather_weight(up_weight, up_half, pass_on(up_half))
    down_full = gather_weight(down_weight, down_half, pass_on(down_half))
    cot_rows = jnp.concatenate(take_row(out_cotangent), axis=0).astype(jnp.float32)
    force_cot = jnp.concatenate(take_row(force_cotangent), axis=1)

    second = first + jnp.dot(attended_low, out_full, preferred_element_type=jnp.float32)
    normed_two, norm_two_back = jax.vjp(layer_norm, second, gain_two, shift_two)
    normed_two_low = normed_two.astype(jnp.bfloat16)
    hidden = jnp.dot(normed_two_low, up_full, preferred_element_type=jnp.float32)
    activated, gelu_back = jax.vjp(exact_gelu, hidden)
    activated_low = activated.astype(jnp.bfloat16)
    third = second + jnp.dot(activated_low, down_full, preferred_element_type=jnp.float32)
    block_low = third.astype(jnp.bfloat16)
    forces = jnp.einsum("cd,qd->cq", force_full, block_low, preferred_element_type=jnp.float32)
    third_grad = cot_rows + jnp.einsum(
        "cq,cd->qd", force_cot, force_full.astype(jnp.float32), precision=highest
    )
    force_grad = jnp.einsum(
        "cq,qd->cd", force_cot, block_low.astype(jnp.float32), precision=highest
    )
    third_low = third_grad.astype(jnp.bfloat16)
    activated_grad = dot32(third_low, down_full, (1, 1))
    hidden_grad = gelu_back(activated_grad)[0].astype(jnp.bfloat16)
    normed_two_grad = dot32(hidden_grad, up_full, (1, 1))
    second_part, gain_two_grad, shift_two_grad = norm_two_back(normed_two_grad)
    second_grad = third_grad + second_part
    second_low = second_grad.astype(jnp.bfloat16)
    attended_grad = by_group(dot32(second_low, out_full, (1, 1)).astype(jnp.bfloat16))
    scaled_grad = (attended_grad.astype(jnp.float32) * inverse).astype(jnp.bfloat16)

    down = Flight(weight_chain([(activated_low, third_low)], ("dp", "x", "z")))
    up = Flight(weight_chain([(normed_two_low, hidden_grad), (attended_low, second_low)], ("x", "dp", "z")))

    scaled_grad = advance(scaled_grad, down, up)
    back = attend_back(query, scaled_grad, attended, key_flat, turned, probs, 0, 4)
    backs = [back[1:]]
    pairs, scaled_grad = advance((back[0], scaled_grad))
    back = attend_back(query, scaled_grad, attended, key_flat, turned, pairs, 1, 4)
    backs.append(back[1:])
    pairs, scaled_grad = advance((back[0], scaled_grad), down, up)
    back = attend_back(query, scaled_grad, attended, key_flat, turned, pairs, 2, 4)
    backs.append(back[1:])
    pairs, scaled_grad = advance((back[0], scaled_grad), down, up)
    back = attend_back(query, scaled_grad, attended, key_flat, turned, pairs, 3, 4)
    backs.append(back[1:])
    logit_grad, backs = advance((back[0], backs), down)
    query_grad = flat_groups(jnp.concatenate([back[0] for back in backs], axis=0)).astype(jnp.bfloat16)
    pair_grad_turn = jnp.concatenate([back[1] for back in backs] + [back[2] for back in backs], axis=0)

    query_part = dot32(normed_low, query_grad, (0, 0)).astype(jnp.bfloat16)
    pair_part = dot32(normed_all, pair_grad_turn, (0, 1)).astype(jnp.bfloat16)
    table = Flight(table_chain(jnp.concatenate([query_part, pair_part], axis=1), ("dp", "x", "z")))
    pair_share = dot32(pair_grad_turn, pair_weight, (0, 1)).astype(jnp.bfloat16)
    own = pair_share.reshape(x_count, z_count, 2 * held, D)
    first_half, second_half = own[..., :D // 2], own[..., D // 2:]
    share_one = Flight(share_chain(first_half))
    steps = tiles // 4
    logit_grad, second_half = advance((logit_grad, second_half), up, table)
    sums = table_grad(query_where, key_where, logit_grad, 0, steps)
    sums, logit_grad, second_half = advance((sums, logit_grad, second_half), share_one, down)
    share_two = Flight(share_chain(second_half))
    piece = table_grad(query_where, key_where, logit_grad, steps, steps)
    sums, piece, logit_grad = advance((sums, piece, logit_grad), share_one, share_two, table)
    sums = sums + piece
    piece = table_grad(query_where, key_where, logit_grad, 2 * steps, steps)
    sums, piece, logit_grad = advance((sums, piece, logit_grad), share_two, table, up)
    sums = sums + piece
    piece = table_grad(query_where, key_where, logit_grad, 3 * steps, steps)
    sums, piece = advance((sums, piece), table, down)
    bias_grad = table_sums(sums + piece)
    pair_normed_grad = jnp.concatenate([finish(share_one), finish(share_two)], axis=1)
    (down_grad,), (up_grad, out_grad), (qkv_grad,) = [finish(flight) for flight in (down, up, table)]

    normed_grad = dot32(query_grad, query_weight, (1, 1)) + pair_normed_grad
    first_part, gain_one_grad, shift_one_grad = norm_one_back(normed_grad)
    first_grad = second_grad + first_part
    first_low = first_grad.astype(jnp.bfloat16).astype(jnp.float32)
    protein_sum = jnp.stack(
        [
            jnp.sum(jnp.where((segment_rows == index)[:, None], first_low, 0.0), axis=0)
            for index in range(proteins)
        ]
    )
    slots = 2 * dp_count
    slot = jnp.arange(slots) == 2 * place + core
    protein_slots = jnp.where(slot[:, None, None], protein_sum[None], 0.0)
    padding = jnp.zeros((6 * D - KERNELS * HEADS,), jnp.float32)
    last = sum_all(jnp.concatenate(
        [
            gain_one_grad,
            shift_one_grad,
            gain_two_grad,
            shift_two_grad,
            force_grad,
            jnp.concatenate([bias_grad.reshape(-1), padding]).reshape(6, D),
            protein_slots.reshape(slots * proteins, D),
        ],
        axis=0,
    ))
    vectors = part_of(last[:4], place, dp_count, 1)
    force_sum = part_of(last[4:7], place, dp_count, 1)
    bias_sum = part_of(last[7:13].reshape(-1)[:KERNELS * HEADS].reshape(KERNELS, HEADS), place, dp_count, 0)
    protein_all = last[13:]
    other_steps = lax.dynamic_index_in_dim(time_steps, 1 - core, 0, keepdims=False)
    both_steps = jnp.where(core == 0, jnp.stack([my_steps, other_steps]), jnp.stack([other_steps, my_steps]))
    all_features = time_features(both_steps.reshape(-1).astype(jnp.float32), D).astype(jnp.bfloat16)
    all_features = in_order(spread_dp(all_features)).reshape(slots * proteins, D)
    time_grad = jnp.einsum(
        "sd,se->de",
        part_of(all_features, place, dp_count, 1).astype(jnp.float32),
        protein_all,
        precision=highest,
    )

    return (
        give_row(block_low, 0),
        give_row(forces, 1),
        give_row(first_grad, 0),
        time_grad,
        vectors[0],
        vectors[1],
        qkv_grad,
        bias_sum,
        out_grad,
        vectors[2],
        vectors[3],
        up_grad,
        down_grad,
        force_sum,
    )


def solution(mesh):
    chips = mesh.shape["blk"] // 2
    rows = CHIP_ROW if chips % CHIP_ROW == 0 else 1
    fine = jax.sharding.Mesh(
        mesh.devices.reshape(mesh.shape["dp"], rows, chips // rows, 2), ("dp", "z", "x", "core")
    )
    blk = ("z", "x", "core")
    return jax.shard_map(
        body,
        mesh=fine,
        in_specs=(
            P("dp", blk, None),
            P("dp", None, blk),
            P("dp", blk),
            P("dp", None),
            P("dp", None),
            P("dp"),
            P("dp"),
            P("dp", None),
            P("dp", None),
            P("dp", None),
            P("dp"),
            P("dp"),
            P("dp", None),
            P("dp", None),
            P(None, "dp"),
            P("dp", blk, None),
            P("dp", None, blk),
        ),
        out_specs=(
            P("dp", blk, None),
            P("dp", None, blk),
            P("dp", blk, None),
            P("dp", None),
            P("dp"),
            P("dp"),
            P("dp", None),
            P("dp", None),
            P("dp", None),
            P("dp"),
            P("dp"),
            P("dp", None),
            P("dp", None),
            P(None, "dp"),
        ),
        check_vma=False,
    )
```

```python
import functools
import jax
import jax.numpy as jnp
import numpy as np
from jax import lax
from jax.sharding import PartitionSpec as P
from jax.experimental import pallas as pl
from jax.experimental.pallas import tpu as pltpu

D = 768
HEADS = 32
HEAD_DIM = 24
KERNELS = 128
GROUPS = 4
GROUP_HEADS = 8
GROUP_DIM = 192
GROUP_PAD = 256
LOG2E = 1.4426950408889634
SCALE = HEAD_DIM ** -0.5
SPAN = 8
NA = KERNELS // SPAN
masked_value = -1e30
VMEM_LIMIT = 60 * 2**20
FORWARD_TILE = 32
BACKWARD_TILE = 64
FINE = 8
KERNEL_COST = 2.5e8


def cost(micros, bytes_moved):
    return pl.CostEstimate(flops=int(micros * KERNEL_COST), bytes_accessed=int(bytes_moved), transcendentals=0)


def distance_tile(q_ref, k_ref):
    total = None
    for axis in range(3):
        offset = q_ref[:, axis:axis + 1] - k_ref[axis:axis + 1, :]
        total = offset * offset if total is None else total + offset * offset
    return jnp.sqrt(total) * (KERNELS / 48.0)


def kernel_rows(x):
    centre = lax.broadcasted_iota(jnp.int32, (NA, 1), 0).astype(jnp.float32) * (SPAN / 2.0) + SPAN / 4.0
    y = jnp.clip(x - centre, -24.0, 24.0)
    up_step = jnp.exp2(y * (0.5 * LOG2E))
    down_step = jnp.exp2(y * (-0.5 * LOG2E))
    middle = jnp.exp2((y * y) * (-0.5 * LOG2E))
    above = [middle]
    for _ in range(SPAN // 2 - 1):
        above.append(above[-1] * up_step)
    below = []
    current = middle
    for _ in range(SPAN // 2):
        current = current * down_step
        below.append(current)
    rows = below[::-1] + above
    return jnp.concatenate([r.astype(jnp.bfloat16) for r in rows], axis=0)


def kernel_order():
    step = np.arange(SPAN) - SPAN // 2
    order = np.array([[a * SPAN + SPAN // 2 + b for a in range(NA)] for b in step]).reshape(-1)
    factor = np.repeat(np.exp(-(step ** 2) / 8.0), NA).astype(np.float32)
    return order, factor


def bias_kernel(chunk, q_ref, k_ref, w_ref, *refs):
    out_ref, x_ref, m_ref = refs[-3:]
    rows = q_ref.shape[0]
    keys = k_ref.shape[1]
    x_ref[...] = distance_tile(q_ref, k_ref)
    m_ref[...] = jnp.where(q_ref[:, 3:4] == k_ref[3:4, :], 0.0, masked_value)
    w = w_ref[...]

    def step(t, carry):
        for start in range(0, keys, chunk):
            cols = slice(start, start + chunk)
            values = []
            for q in (2 * t, 2 * t + 1):
                value = jnp.dot(w, kernel_rows(x_ref[pl.ds(q, 1), cols]), preferred_element_type=jnp.float32)
                values.append(value + m_ref[pl.ds(q, 1), cols])
            for g in range(GROUPS):
                both = jnp.concatenate([value[g * GROUP_HEADS:(g + 1) * GROUP_HEADS] for value in values], axis=0)
                out_ref[g, pl.ds(t * 2 * GROUP_HEADS, 2 * GROUP_HEADS), cols] = both.astype(out_ref.dtype)
        return carry

    lax.fori_loop(0, rows // 2, step, 0, unroll=True)


def pair_bias(q_where, k_where, w, first, steps, previous):
    rows, keys = q_where.shape[0], k_where.shape[1]
    in_specs = [
        pl.BlockSpec((FINE, 8), lambda i: (i + first, 0)),
        pl.BlockSpec((8, keys), lambda i: (0, 0)),
        pl.BlockSpec((HEADS, KERNELS), lambda i: (0, 0)),
    ]
    operands = [q_where, k_where, w]
    aliases = {}
    if previous is not None:
        in_specs.append(pl.BlockSpec(memory_space=pl.ANY))
        operands.append(previous)
        aliases = {3: 0}
    return pl.pallas_call(
        functools.partial(bias_kernel, 256),
        grid=(steps,),
        in_specs=in_specs,
        out_specs=pl.BlockSpec((GROUPS, FINE * GROUP_HEADS, keys), lambda i: (0, i + first, 0)),
        out_shape=jax.ShapeDtypeStruct((GROUPS, rows * GROUP_HEADS, keys), jnp.bfloat16),
        scratch_shapes=[pltpu.VMEM((FINE, keys), jnp.float32), pltpu.VMEM((FINE, keys), jnp.float32)],
        input_output_aliases=aliases,
        cost_estimate=cost(1.5 * steps, FINE * steps * HEADS * keys * 2),
        compiler_params=pltpu.CompilerParams(vmem_limit_bytes=VMEM_LIMIT),
        name="pair_bias",
    )(*operands)


def project_kernel(x_ref, w_ref, turn_ref, key_ref, value_ref, w_turn_ref):
    @pl.when(pl.program_id(0) == 0)
    def turn_weight():
        w_turn_ref[...] = w_ref[...].T

    x = x_ref[...]
    rows = x.shape[0]
    turn_ref[...] = lax.dot_general(
        w_turn_ref[...], x, (((1,), (1,)), ((), ())), preferred_element_type=jnp.float32
    ).astype(turn_ref.dtype)
    flat = jnp.dot(x, w_ref[...], preferred_element_type=jnp.float32)
    for out_ref, first, filler in ((key_ref, 0, 0.0), (value_ref, D, 1.0)):
        for g in range(GROUPS):
            part = flat[:, first + g * GROUP_DIM:first + (g + 1) * GROUP_DIM]
            wide = jnp.concatenate([part, jnp.full((rows, GROUP_PAD - GROUP_DIM), filler, jnp.float32)], axis=1)
            out_ref[:, g * GROUP_PAD:(g + 1) * GROUP_PAD] = wide.astype(out_ref.dtype)


def project(values, weight):
    keys, depth = values.shape
    width = weight.shape[1]
    wide = GROUPS * GROUP_PAD
    block = 256
    return pl.pallas_call(
        project_kernel,
        grid=(keys // block,),
        in_specs=[
            pl.BlockSpec((block, depth), lambda i: (i, 0)),
            pl.BlockSpec((depth, width), lambda i: (0, 0)),
        ],
        out_specs=[
            pl.BlockSpec((width, block), lambda i: (0, i)),
            pl.BlockSpec((block, wide), lambda i: (i, 0)),
            pl.BlockSpec((block, wide), lambda i: (i, 0)),
        ],
        out_shape=[
            jax.ShapeDtypeStruct((width, keys), jnp.bfloat16),
            jax.ShapeDtypeStruct((keys, wide), jnp.bfloat16),
            jax.ShapeDtypeStruct((keys, wide), jnp.bfloat16),
        ],
        scratch_shapes=[pltpu.VMEM((width, depth), jnp.bfloat16)],
        cost_estimate=cost(12, keys * (depth + 3 * width) * 2),
        compiler_params=pltpu.CompilerParams(vmem_limit_bytes=VMEM_LIMIT),
        name="project",
    )(values, weight)


def head_mask(width):
    head = lax.broadcasted_iota(jnp.int32, (GROUP_HEADS, width), 0)
    lane = lax.broadcasted_iota(jnp.int32, (GROUP_HEADS, width), 1)
    return ((lane >= head * HEAD_DIM) & (lane < (head + 1) * HEAD_DIM)).astype(jnp.float32)


def spread_heads(values, mask):
    rows, width = values.shape
    return (values[:, None, :] * mask[None]).reshape(rows * GROUP_HEADS, width)


def gather_heads(values, mask):
    rows, width = values.shape
    return jnp.sum(values.reshape(rows // GROUP_HEADS, GROUP_HEADS, width) * mask[None], axis=1)


def forward_kernel(chunk, q_ref, kt_ref, v_ref, bias_ref, p_ref, o_ref, inv_ref, s_ref):
    keys = kt_ref.shape[1]
    mask = head_mask(GROUP_PAD)

    for g in range(GROUPS):
        rows = slice(g * GROUP_DIM, (g + 1) * GROUP_DIM)
        spread = spread_heads(q_ref[g].astype(jnp.float32), mask).astype(jnp.bfloat16)[:, :GROUP_DIM]
        peak = None
        for start in range(0, keys, chunk):
            s = jnp.dot(spread, kt_ref[rows, start:start + chunk], preferred_element_type=jnp.float32)
            s = s * (SCALE * LOG2E) + bias_ref[g, :, start:start + chunk].astype(jnp.float32)
            s_ref[:, start:start + chunk] = s
            for lane in range(0, chunk, 128):
                part = s[:, lane:lane + 128]
                peak = part if peak is None else jnp.maximum(peak, part)
        top = jnp.max(peak, axis=1, keepdims=True)
        for start in range(0, keys, chunk):
            p_ref[g, :, start:start + chunk] = jnp.exp2(s_ref[:, start:start + chunk] - top).astype(jnp.bfloat16)
        mixed = jnp.dot(p_ref[g], v_ref[:, g * GROUP_PAD:(g + 1) * GROUP_PAD], preferred_element_type=jnp.float32)
        inverse = 1.0 / mixed[:, GROUP_DIM:GROUP_DIM + 1]
        o_ref[g] = gather_heads(mixed * inverse, mask)
        inv_ref[g] = gather_heads(jnp.broadcast_to(inverse, mixed.shape), mask)


def attend(q, turned, value_flat, bias):
    rows, keys = q.shape[1], turned.shape[1]
    tile = min(FORWARD_TILE, FORWARD_TILE * 2048 // keys)
    whole = pl.Buffered(1)
    return pl.pallas_call(
        functools.partial(forward_kernel, 512),
        grid=(rows // tile,),
        in_specs=[
            pl.BlockSpec((GROUPS, tile, GROUP_PAD), lambda i: (0, i, 0)),
            pl.BlockSpec((D, keys), lambda i: (0, 0), pipeline_mode=whole),
            pl.BlockSpec((keys, GROUPS * GROUP_PAD), lambda i: (0, 0), pipeline_mode=whole),
            pl.BlockSpec((GROUPS, tile * GROUP_HEADS, keys), lambda i: (0, i, 0)),
        ],
        out_specs=[
            pl.BlockSpec((GROUPS, tile * GROUP_HEADS, keys), lambda i: (0, i, 0)),
            pl.BlockSpec((GROUPS, tile, GROUP_PAD), lambda i: (0, i, 0)),
            pl.BlockSpec((GROUPS, tile, GROUP_PAD), lambda i: (0, i, 0)),
        ],
        out_shape=[
            jax.ShapeDtypeStruct((GROUPS, rows * GROUP_HEADS, keys), jnp.bfloat16),
            jax.ShapeDtypeStruct((GROUPS, rows, GROUP_PAD), jnp.float32),
            jax.ShapeDtypeStruct((GROUPS, rows, GROUP_PAD), jnp.float32),
        ],
        scratch_shapes=[
            pltpu.VMEM((tile * GROUP_HEADS, keys), jnp.float32),
        ],
        input_output_aliases={3: 0},
        cost_estimate=cost(45, rows * HEADS * keys * 4),
        compiler_params=pltpu.CompilerParams(vmem_limit_bytes=VMEM_LIMIT),
        name="attend",
    )(q, turned, value_flat, bias)


def backward_kernel(chunk, q_ref, do_ref, o_ref, k_ref, vt_ref, p_ref, ds_ref, dq_ref, dkt_ref, dvt_ref, dk_acc, dv_acc):
    keys = vt_ref.shape[1]
    mask = head_mask(GROUP_PAD)
    tile = pl.program_id(0)
    groups = q_ref.shape[0]

    @pl.when(tile == 0)
    def start_group():
        dk_acc[...] = jnp.zeros_like(dk_acc)
        dv_acc[...] = jnp.zeros_like(dv_acc)

    for g in range(groups):
        rows = slice(g * GROUP_DIM, (g + 1) * GROUP_DIM)
        q_wide = spread_heads(q_ref[g].astype(jnp.float32), mask)
        do_wide = spread_heads(do_ref[g].astype(jnp.float32), mask)
        o_wide = spread_heads(o_ref[g], mask)
        delta = jnp.sum(do_wide * o_wide, axis=1, keepdims=True)
        do_low = do_wide.astype(jnp.bfloat16)[:, :GROUP_DIM]
        do_turn = do_wide[:, :GROUP_DIM].T.astype(jnp.bfloat16)
        q_turn = q_wide[:, :GROUP_DIM].T.astype(jnp.bfloat16)
        for start in range(0, keys, chunk):
            cols = slice(start, start + chunk)
            dp = jnp.dot(do_low, vt_ref[rows, cols], preferred_element_type=jnp.float32)
            p = p_ref[g, :, cols]
            ds = (p.astype(jnp.float32) * (dp - delta)).astype(jnp.bfloat16)
            ds_ref[g, :, cols] = ds
            dv_acc[rows, cols] += jnp.dot(do_turn, p, preferred_element_type=jnp.float32)
            dk_acc[rows, cols] += jnp.dot(q_turn, ds, preferred_element_type=jnp.float32)
        dq = jnp.dot(ds_ref[g], k_ref[:, g * GROUP_PAD:(g + 1) * GROUP_PAD], preferred_element_type=jnp.float32)
        dq_ref[g] = gather_heads(dq, mask) * SCALE

    @pl.when(tile == pl.num_programs(0) - 1)
    def finish():
        dkt_ref[...] = (dk_acc[...] * SCALE).astype(dkt_ref.dtype)
        dvt_ref[...] = dv_acc[...].astype(dvt_ref.dtype)


def attend_back(q, do, o, key_flat, turned, p, part, parts):
    rows, keys = q.shape[1], turned.shape[1]
    tile = min(BACKWARD_TILE, BACKWARD_TILE * 2048 // keys)
    groups = GROUPS // parts
    width = groups * GROUP_DIM
    whole = pl.Buffered(1)
    narrow = pl.BlockSpec((groups, tile, GROUP_PAD), lambda i: (part, i, 0))
    return pl.pallas_call(
        functools.partial(backward_kernel, 512),
        grid=(rows // tile,),
        in_specs=[
            narrow,
            narrow,
            narrow,
            pl.BlockSpec((keys, groups * GROUP_PAD), lambda i: (0, part), pipeline_mode=whole),
            pl.BlockSpec((width, keys), lambda i: (part + parts, 0), pipeline_mode=whole),
            pl.BlockSpec((groups, tile * GROUP_HEADS, keys), lambda i: (part, i, 0)),
        ],
        out_specs=[
            pl.BlockSpec((groups, tile * GROUP_HEADS, keys), lambda i: (part, i, 0)),
            pl.BlockSpec((groups, tile, GROUP_PAD), lambda i: (0, i, 0)),
            pl.BlockSpec((width, keys), lambda i: (0, 0), pipeline_mode=whole),
            pl.BlockSpec((width, keys), lambda i: (0, 0), pipeline_mode=whole),
        ],
        out_shape=[
            jax.ShapeDtypeStruct(p.shape, p.dtype),
            jax.ShapeDtypeStruct((groups, rows, GROUP_PAD), jnp.float32),
            jax.ShapeDtypeStruct((width, keys), jnp.bfloat16),
            jax.ShapeDtypeStruct((width, keys), jnp.bfloat16),
        ],
        scratch_shapes=[
            pltpu.VMEM((width, keys), jnp.float32),
            pltpu.VMEM((width, keys), jnp.float32),
        ],
        input_output_aliases={5: 0},
        cost_estimate=cost(56 / parts, rows * HEADS * keys * 4 // parts),
        compiler_params=pltpu.CompilerParams(vmem_limit_bytes=VMEM_LIMIT),
        name="attend_back",
    )(q, do, o, key_flat, turned, p)


def table_grad_kernel(chunk, q_ref, k_ref, ds_ref, out_ref, x_ref):
    rows = q_ref.shape[0]
    keys = k_ref.shape[1]
    pair = 2 * GROUP_HEADS

    @pl.when(pl.program_id(0) == 0)
    def start_zero():
        out_ref[...] = jnp.zeros_like(out_ref)

    x_ref[...] = distance_tile(q_ref, k_ref)

    def step(t, total):
        for start in range(0, keys, chunk):
            x = x_ref[pl.ds(2 * t, 2), start:start + chunk]
            table = jnp.concatenate([kernel_rows(x[0:1]), kernel_rows(x[1:2])], axis=0)
            grads = jnp.concatenate(
                [ds_ref[g, pl.ds(t * pair, pair), start:start + chunk] for g in range(GROUPS)], axis=0
            )
            total = total + lax.dot_general(table, grads, (((1,), (1,)), ((), ())), preferred_element_type=jnp.float32)
        return total

    out_ref[...] += lax.fori_loop(0, rows // 2, step, jnp.zeros(out_ref.shape, jnp.float32), unroll=True)


def table_grad(q_where, k_where, ds, first, steps):
    rows, keys = q_where.shape[0], k_where.shape[1]
    wide = 2 * HEADS
    return pl.pallas_call(
        functools.partial(table_grad_kernel, 256),
        grid=(steps,),
        in_specs=[
            pl.BlockSpec((FINE, 8), lambda i: (i + first, 0)),
            pl.BlockSpec((8, keys), lambda i: (0, 0)),
            pl.BlockSpec((GROUPS, FINE * GROUP_HEADS, keys), lambda i: (0, i + first, 0)),
        ],
        out_specs=pl.BlockSpec((2 * KERNELS, wide), lambda i: (0, 0)),
        out_shape=jax.ShapeDtypeStruct((2 * KERNELS, wide), jnp.float32),
        scratch_shapes=[pltpu.VMEM((FINE, keys), jnp.float32)],
        cost_estimate=cost(1.6 * steps, FINE * steps * HEADS * keys * 2),
        compiler_params=pltpu.CompilerParams(vmem_limit_bytes=VMEM_LIMIT),
        name="table_grad",
    )(q_where, k_where, ds)


def table_sums(sums):
    sums = sums.reshape(2, KERNELS, GROUPS, 2, GROUP_HEADS)
    both = (sums[0, :, :, 0] + sums[1, :, :, 1]).reshape(KERNELS, HEADS)
    order, factor = kernel_order()
    return (both * factor[:, None])[np.argsort(order)]


def place_kernel(steps, s_ref, *refs):
    own_ref = refs[0]
    mine, other = refs[1:1 + steps], refs[1 + steps:1 + 2 * steps]
    out_ref = refs[-1]
    j = pl.program_id(0)
    place, core = s_ref[0], s_ref[1]
    away = lax.rem(place - j // 2 + steps + 1, steps + 1)

    @pl.when(away == 0)
    def own_part():
        out_ref[...] = own_ref[...]

    for step in range(1, steps + 1):
        @pl.when((away == step) & (core == j % 2))
        def fetched_part():
            out_ref[...] = mine[step - 1][...]

        @pl.when((away == step) & (core != j % 2))
        def passed_part():
            out_ref[...] = other[step - 1][...]


def place_shards(where, own, mine, other):
    steps = len(mine)
    rows, columns = own.shape
    half = rows // 2
    fixed = pl.BlockSpec((half, columns), lambda j, s: (0, 0))
    return pl.pallas_call(
        functools.partial(place_kernel, steps),
        grid_spec=pltpu.PrefetchScalarGridSpec(
            num_scalar_prefetch=1,
            grid=(2 * (steps + 1),),
            in_specs=[pl.BlockSpec((half, columns), lambda j, s: (j % 2, 0))] + [fixed] * (2 * steps),
            out_specs=pl.BlockSpec((half, columns), lambda j, s: (j, 0)),
        ),
        out_shape=jax.ShapeDtypeStruct(((steps + 1) * rows, columns), own.dtype),
        cost_estimate=cost(3, 2 * (steps + 1) * own.size * 2),
        compiler_params=pltpu.CompilerParams(vmem_limit_bytes=VMEM_LIMIT),
        name="place_shards",
    )(where, own, *mine, *other)


def assemble_kernel(xs, widths, s_ref, *refs):
    own_refs, other_refs, out_refs = refs[:xs], refs[xs:2 * xs], refs[2 * xs:]
    zs = own_refs[0].shape[0]
    x, core = s_ref[0], s_ref[1]
    jx = pl.program_id(0)
    from_x = lax.rem(x - jx + xs, xs)
    first = core == 0
    for step in range(xs):
        @pl.when(from_x == step)
        def copy_piece():
            for jz in range(zs):
                begin = 0
                for half, out_ref in zip(widths, out_refs):
                    own = own_refs[step][jz, :, begin:begin + half].astype(jnp.float32)
                    other = other_refs[step][jz, :, begin:begin + half].astype(jnp.float32)
                    out_ref[0, jz, :, :half] = jnp.where(first, own, other)
                    out_ref[0, jz, :, half:] = jnp.where(first, other, own)
                    begin += half


def assemble(where, own, other, widths):
    xs = len(own)
    zs, rows, columns = own[0].shape
    spec = pl.BlockSpec((zs, rows, columns), lambda i, s: (0, 0, 0))
    wholes = pl.pallas_call(
        functools.partial(assemble_kernel, xs, widths),
        grid_spec=pltpu.PrefetchScalarGridSpec(
            num_scalar_prefetch=1,
            grid=(xs,),
            in_specs=[spec] * (2 * xs),
            out_specs=[pl.BlockSpec((1, zs, rows, 2 * half), lambda i, s: (i, 0, 0, 0)) for half in widths],
        ),
        out_shape=[jax.ShapeDtypeStruct((xs, zs, rows, 2 * half), jnp.float32) for half in widths],
        cost_estimate=cost(4, xs * zs * rows * columns * 12),
        compiler_params=pltpu.CompilerParams(vmem_limit_bytes=VMEM_LIMIT),
        name="assemble",
    )(where, *own, *other)
    return [whole.reshape(xs * zs * rows, -1) for whole in wholes]


eps = 1e-05
highest = lax.Precision.HIGHEST
CHIP_ROW = 4
Z_EXCHANGE = True


def layer_norm(values, norm_gain, norm_shift):
    centred = values - jnp.mean(values, axis=-1, keepdims=True)
    spread = jnp.mean(centred * centred, axis=-1, keepdims=True)
    return centred * lax.rsqrt(spread + eps) * norm_gain + norm_shift


def exact_gelu(values):
    return jax.nn.gelu(values, approximate=False)


def time_features(stamps, feature_width):
    half_width = feature_width // 2
    frequency = jnp.exp(-jnp.log(10000.0) * jnp.arange(half_width, dtype=jnp.float32) / half_width)
    angles = stamps[:, None] * frequency[None, :]
    return jnp.concatenate([jnp.sin(angles), jnp.cos(angles)], axis=1)


def shifted(values, axis, step):
    size = lax.axis_size(axis)
    return lax.ppermute(values, axis, [(i, (i + step) % size) for i in range(size)])


def part_of(values, index, count, axis):
    length = values.shape[axis] // count
    return lax.dynamic_slice_in_dim(values, index * length, length, axis)


def dot32(left, right, contract):
    return lax.dot_general(left, right, ((contract[:1], contract[1:]), ((), ())), preferred_element_type=jnp.float32)


def in_order(pieces):
    count = len(pieces)
    place = lax.axis_index("dp")
    chosen = []
    for index in range(count):
        step = lax.rem(place - index + count, count)
        picked = pieces[0]
        for other in range(1, count):
            picked = jnp.where(step == other, pieces[other], picked)
        chosen.append(picked)
    return jnp.stack(chosen)


def spread_dp(values):
    return [values] + [shifted(values, "dp", step) for step in range(1, lax.axis_size("dp"))]


def fetch_shards(weight):
    half = part_of(weight, lax.axis_index("core"), 2, 0)
    return [shifted(half, "dp", step) for step in range(1, lax.axis_size("dp"))]


def pass_on(mine):
    return [shifted(piece, "core", 1) for piece in mine]


def gather_weight(weight, mine, other):
    where = jnp.stack([lax.axis_index("dp"), lax.axis_index("core")]).astype(jnp.int32)
    return place_shards(where, weight, mine, other)


def tie(*groups):
    return lax.optimization_barrier(groups)


def add_parts(own, incoming):
    total = own.astype(jnp.float32)
    for share in incoming:
        total = total + share.astype(jnp.float32)
    return total


def turn_back(values, axis):
    count, place = lax.axis_size(axis), lax.axis_index(axis)
    ring = jnp.concatenate([values, values], axis=0)[::-1]
    return lax.dynamic_slice_in_dim(ring, count - 1 - place, count, 0)


def reduce_chain(local, hops, widths):
    left = ["dp", "x", "z"]
    for axis in hops:
        dim = left.index(axis)
        left.pop(dim)
        count, place = lax.axis_size(axis), lax.axis_index(axis)
        if axis == "z" and Z_EXCHANGE:
            local = yield lax.all_to_all(local.astype(jnp.bfloat16), "z", dim, 0)
            local = jnp.sum(local.astype(jnp.float32), axis=0)
            continue
        own = lax.dynamic_index_in_dim(local, place, dim, keepdims=False)
        incoming = [
            shifted(
                lax.dynamic_index_in_dim(local, lax.rem(place + step, count), dim, keepdims=False).astype(jnp.bfloat16),
                axis,
                step,
            )
            for step in range(1, count)
        ]
        own, incoming = yield own, incoming
        local = add_parts(own, incoming)
    owned = local.astype(jnp.bfloat16)
    if Z_EXCHANGE:
        copies = jnp.broadcast_to(owned[None], (lax.axis_size("z"),) + owned.shape)
        pieces = yield lax.all_to_all(copies, "z", 0, 0)
    else:
        owned, incoming = yield owned, [shifted(owned, "z", step) for step in range(1, lax.axis_size("z"))]
        pieces = turn_back(jnp.stack([owned] + incoming), "z")
    own = yield [pieces] + [shifted(pieces, "x", step) for step in range(1, lax.axis_size("x"))]
    own, other = yield own, [shifted(piece, "core", 1) for piece in own]
    where = jnp.stack([lax.axis_index(axis) for axis in ("x", "core")]).astype(jnp.int32)
    return assemble(where, own, other, widths)


def by_owner(values):
    counts = [lax.axis_size(axis) for axis in ("dp", "x", "z")]
    return values.reshape(counts + [-1, values.shape[1]])


def weight_chain(factors, hops):
    core = lax.axis_index("core")
    moving = []
    for inputs, grads in factors:
        moving.append((
            inputs, shifted(inputs, "core", 1),
            part_of(grads, core, 2, 1), shifted(part_of(grads, 1 - core, 2, 1), "core", 1),
        ))
    moving = yield moving
    local = [
        dot32(jnp.concatenate([left, other_left], axis=0), jnp.concatenate([right, other_right], axis=0), (0, 0))
        .astype(jnp.bfloat16)
        for left, other_left, right, other_right in moving
    ]
    return (yield from reduce_chain(by_owner(jnp.concatenate(local, axis=1)), hops, [part.shape[1] for part in local]))


def table_chain(local, hops):
    core = lax.axis_index("core")
    own = part_of(local, core, 2, 1)
    own, other = yield own, shifted(part_of(local, 1 - core, 2, 1), "core", 1)
    chip = (own.astype(jnp.float32) + other.astype(jnp.float32)).astype(jnp.bfloat16)
    return (yield from reduce_chain(by_owner(chip), hops, [chip.shape[1]]))


def share_chain(shares):
    x_count, z_count = shares.shape[:2]
    own, incoming = yield shares[0], [shifted(shares[step], "x", -step) for step in range(1, x_count)]
    total = add_parts(own, incoming)
    low = total.astype(jnp.bfloat16)
    own, incoming = yield total[0], [shifted(low[step], "z", -step) for step in range(1, z_count)]
    return add_parts(own, incoming)


class Flight:
    def __init__(self, chain):
        self.chain = chain
        self.values = next(chain)
        self.result = None

    def land(self, values):
        try:
            self.values = self.chain.send(values)
        except StopIteration as stop:
            self.values, self.result = None, stop.value


def advance(inputs, *flights):
    flights = [flight for flight in flights if flight.values is not None]
    inputs, landed = lax.optimization_barrier((inputs, [flight.values for flight in flights]))
    for flight, values in zip(flights, landed):
        flight.land(values)
    return inputs


def finish(flight):
    while flight.values is not None:
        flight.land(flight.values)
    return flight.result


def sum_all(values):
    for axis in ("core", "dp", "x", "z"):
        values = functools.reduce(
            jnp.add, [shifted(values, axis, step) for step in range(1, lax.axis_size(axis))], values
        )
    return values


def by_group(values):
    wide = values.reshape(values.shape[0], GROUPS, GROUP_DIM)
    wide = jnp.pad(wide, ((0, 0), (0, 0), (0, GROUP_PAD - GROUP_DIM)))
    return jnp.transpose(wide, (1, 0, 2))


def flat_groups(values):
    return jnp.transpose(values[:, :, :GROUP_DIM], (1, 0, 2)).reshape(values.shape[1], D)


def body(
    residues,
    coordinates,
    segment_ids,
    time_steps,
    time_weight,
    norm1_gain,
    norm1_bias,
    qkv_weight,
    bias_weight,
    out_weight,
    norm2_gain,
    norm2_bias,
    up_weight,
    down_weight,
    force_weight,
    out_cotangent,
    force_cotangent,
):
    core = lax.axis_index("core")
    place = lax.axis_index("dp")
    dp_count = lax.axis_size("dp")
    x_count, z_count = lax.axis_size("x"), lax.axis_size("z")
    held = residues.shape[1]

    def take_row(values):
        mine = lax.dynamic_index_in_dim(values, core, 0, keepdims=False)
        other = lax.dynamic_index_in_dim(values, 1 - core, 0, keepdims=False)
        return mine, shifted(other, "core", 1)

    def give_row(values, axis):
        mine = lax.slice_in_dim(values, 0, held, axis=axis)
        other = shifted(lax.slice_in_dim(values, held, 2 * held, axis=axis), "core", 1)
        first_row = jnp.where(core == 0, mine, other)
        second_row = jnp.where(core == 0, other, mine)
        return jnp.stack([first_row, second_row])

    where_own = jnp.concatenate(
        [coordinates, segment_ids[:, None, :].astype(jnp.bfloat16)], axis=1
    )
    where_rows = jnp.concatenate(take_row(where_own), axis=1)
    bias_parts = [bias_weight] + [shifted(bias_weight, "dp", step) for step in range(1, dp_count)]
    residue_parts = take_row(residues)
    step_list = spread_dp(time_steps)

    where_keys = where_rows[None]
    reach = 1
    while reach < z_count:
        where_keys = jnp.concatenate([where_keys, shifted(where_keys, "z", reach)], axis=0)
        reach *= 2
    where_columns = [where_keys[:z_count]]
    for x_step in range(1, x_count):
        where_columns.append(shifted(where_columns[0], "x", x_step))
    (
        where_columns,
        where_rows,
        bias_parts,
        residue_parts,
        step_list,
        (norm1_gain, norm1_bias, norm2_gain, norm2_bias, force_weight),
        (time_weight, qkv_weight, out_weight, up_weight, down_weight),
        (out_cotangent, force_cotangent),
    ) = tie(
        where_columns,
        where_rows,
        bias_parts,
        residue_parts,
        step_list,
        (norm1_gain, norm1_bias, norm2_gain, norm2_bias, force_weight),
        (time_weight, qkv_weight, out_weight, up_weight, down_weight),
        (out_cotangent, force_cotangent),
    )
    key_where = jnp.transpose(jnp.concatenate(where_columns, axis=0).astype(jnp.float32), (1, 0, 2))
    key_where = jnp.pad(key_where.reshape(4, -1), ((0, 4), (0, 0)))
    query_where = jnp.pad(jnp.transpose(where_rows).astype(jnp.float32), ((0, 0), (0, 4)))
    segment_rows = where_rows[3]
    residue_rows = jnp.concatenate(residue_parts, axis=0).astype(jnp.float32)

    bias_full = in_order(bias_parts).reshape(KERNELS, HEADS)
    order, factor = kernel_order()
    table_weight = (
        jnp.transpose(bias_full).astype(jnp.float32)[:, order] * (factor * LOG2E)
    ).astype(jnp.bfloat16)
    tiles = 2 * held // FINE
    lead = tiles // 8
    bias = pair_bias(query_where, key_where, table_weight, 0, lead, None)

    vectors = in_order(
        spread_dp(jnp.concatenate([jnp.stack([norm1_gain, norm1_bias, norm2_gain, norm2_bias]), force_weight], axis=0))
    )
    vectors = jnp.transpose(vectors, (1, 0, 2)).reshape(7, D)
    gain_one, shift_one, gain_two, shift_two = [vectors[i:i + 1].astype(jnp.float32) for i in range(4)]
    force_full = vectors[4:]
    proteins = time_steps.shape[1]
    row_steps = [lax.dynamic_index_in_dim(steps, core, 0, keepdims=False) for steps in step_list]
    features = time_features(jnp.concatenate(row_steps).astype(jnp.float32), D).astype(jnp.bfloat16)
    features = part_of(features, place, dp_count, 1)
    stamp_part = jnp.dot(features, time_weight, preferred_element_type=jnp.float32)
    stamp_rows = stamp_part[:proteins]
    for step in range(1, dp_count):
        stamp_rows = stamp_rows + shifted(
            stamp_part[step * proteins:(step + 1) * proteins], "dp", -step
        )
    query_own, pair_own = qkv_weight[:, :D], qkv_weight[:, D:]
    pair_half = fetch_shards(pair_own)
    query_half = fetch_shards(query_own)
    bias, stamp_rows, vectors_ready = tie(bias, stamp_rows, (gain_one, shift_one))
    gain_one, shift_one = vectors_ready

    def by_protein(table):
        picked = jnp.zeros((2 * held, table.shape[1]), jnp.float32)
        for index in range(proteins):
            picked = picked + jnp.where((segment_rows == index)[:, None], table[index][None, :], 0.0)
        return picked

    first = residue_rows + by_protein(stamp_rows)
    normed, norm_one_back = jax.vjp(layer_norm, first, gain_one, shift_one)
    normed_low = normed.astype(jnp.bfloat16)

    columns = [[None] * z_count for _ in range(x_count)]
    current = normed_low
    done = lead
    out_half = up_half = down_half = None
    for z_step in range(z_count):
        steps = (tiles - done) // (z_count - z_step)
        across = [current]
        for x_step in range(1, x_count):
            across.append(shifted(across[-1], "x", 1))
        following = shifted(current, "z", 1) if z_step < z_count - 1 else current
        bias = pair_bias(query_where, key_where, table_weight, done, steps, bias)
        done += steps
        bias, current, across = tie(bias, following, across)
        for x_step in range(x_count):
            columns[x_step][z_step] = across[x_step]
        if z_step == 1:
            bias, pair_half, query_half, later = tie(bias, pair_half, query_half, (out_weight, up_weight, down_weight))
            out_weight, up_weight, down_weight = later
            out_half, up_half, down_half = fetch_shards(out_weight), fetch_shards(up_weight), fetch_shards(down_weight)
            pair_passed = pass_on(pair_half)
            query_passed = pass_on(query_half)
    normed_all = jnp.concatenate([piece for column in columns for piece in column], axis=0)

    query_weight = gather_weight(query_own, query_half, query_passed)
    pair_weight = gather_weight(pair_own, pair_half, pair_passed)
    query = by_group(jnp.dot(normed_low, query_weight, preferred_element_type=jnp.float32).astype(jnp.bfloat16))
    turned, key_flat, value_flat = project(normed_all, pair_weight)
    probs, attended, inverse = attend(query, turned, value_flat, bias)
    attended_low = flat_groups(attended).astype(jnp.bfloat16)
    attended_low, out_half, up_half, down_half, cotangents = tie(
        attended_low, out_half, up_half, down_half, (out_cotangent, force_cotangent)
    )
    out_cotangent, force_cotangent = cotangents
    out_full = gather_weight(out_weight, out_half, pass_on(out_half))
    up_full = gather_weight(up_weight, up_half, pass_on(up_half))
    down_full = gather_weight(down_weight, down_half, pass_on(down_half))
    cot_rows = jnp.concatenate(take_row(out_cotangent), axis=0).astype(jnp.float32)
    force_cot = jnp.concatenate(take_row(force_cotangent), axis=1)

    second = first + jnp.dot(attended_low, out_full, preferred_element_type=jnp.float32)
    normed_two, norm_two_back = jax.vjp(layer_norm, second, gain_two, shift_two)
    normed_two_low = normed_two.astype(jnp.bfloat16)
    hidden = jnp.dot(normed_two_low, up_full, preferred_element_type=jnp.float32)
    activated, gelu_back = jax.vjp(exact_gelu, hidden)
    activated_low = activated.astype(jnp.bfloat16)
    third = second + jnp.dot(activated_low, down_full, preferred_element_type=jnp.float32)
    block_low = third.astype(jnp.bfloat16)
    forces = jnp.einsum("cd,qd->cq", force_full, block_low, preferred_element_type=jnp.float32)
    third_grad = cot_rows + jnp.einsum(
        "cq,cd->qd", force_cot, force_full.astype(jnp.float32), precision=highest
    )
    force_grad = jnp.einsum(
        "cq,qd->cd", force_cot, block_low.astype(jnp.float32), precision=highest
    )
    third_low = third_grad.astype(jnp.bfloat16)
    activated_grad = dot32(third_low, down_full, (1, 1))
    hidden_grad = gelu_back(activated_grad)[0].astype(jnp.bfloat16)
    normed_two_grad = dot32(hidden_grad, up_full, (1, 1))
    second_part, gain_two_grad, shift_two_grad = norm_two_back(normed_two_grad)
    second_grad = third_grad + second_part
    second_low = second_grad.astype(jnp.bfloat16)
    attended_grad = by_group(dot32(second_low, out_full, (1, 1)).astype(jnp.bfloat16))
    scaled_grad = (attended_grad.astype(jnp.float32) * inverse).astype(jnp.bfloat16)

    down = Flight(weight_chain([(activated_low, third_low)], ("dp", "x", "z")))
    up = Flight(weight_chain([(normed_two_low, hidden_grad), (attended_low, second_low)], ("x", "dp", "z")))

    scaled_grad = advance(scaled_grad, down, up)
    back = attend_back(query, scaled_grad, attended, key_flat, turned, probs, 0, 4)
    backs = [back[1:]]
    pairs, scaled_grad = advance((back[0], scaled_grad))
    back = attend_back(query, scaled_grad, attended, key_flat, turned, pairs, 1, 4)
    backs.append(back[1:])
    pairs, scaled_grad = advance((back[0], scaled_grad), down, up)
    back = attend_back(query, scaled_grad, attended, key_flat, turned, pairs, 2, 4)
    backs.append(back[1:])
    pairs, scaled_grad = advance((back[0], scaled_grad), down, up)
    back = attend_back(query, scaled_grad, attended, key_flat, turned, pairs, 3, 4)
    backs.append(back[1:])
    logit_grad, backs = advance((back[0], backs), down)
    query_grad = flat_groups(jnp.concatenate([back[0] for back in backs], axis=0)).astype(jnp.bfloat16)
    pair_grad_turn = jnp.concatenate([back[1] for back in backs] + [back[2] for back in backs], axis=0)

    query_part = dot32(normed_low, query_grad, (0, 0)).astype(jnp.bfloat16)
    pair_part = dot32(normed_all, pair_grad_turn, (0, 1)).astype(jnp.bfloat16)
    table = Flight(table_chain(jnp.concatenate([query_part, pair_part], axis=1), ("dp", "x", "z")))
    pair_share = dot32(pair_grad_turn, pair_weight, (0, 1)).astype(jnp.bfloat16)
    own = pair_share.reshape(x_count, z_count, 2 * held, D)
    first_half, second_half = own[..., :D // 2], own[..., D // 2:]
    share_one = Flight(share_chain(first_half))
    steps = tiles // 4
    logit_grad, second_half = advance((logit_grad, second_half), up, table)
    sums = table_grad(query_where, key_where, logit_grad, 0, steps)
    sums, logit_grad, second_half = advance((sums, logit_grad, second_half), share_one, down)
    share_two = Flight(share_chain(second_half))
    piece = table_grad(query_where, key_where, logit_grad, steps, steps)
    sums, piece, logit_grad = advance((sums, piece, logit_grad), share_one, share_two, table)
    sums = sums + piece
    piece = table_grad(query_where, key_where, logit_grad, 2 * steps, steps)
    sums, piece, logit_grad = advance((sums, piece, logit_grad), share_two, table, up)
    sums = sums + piece
    piece = table_grad(query_where, key_where, logit_grad, 3 * steps, steps)
    sums, piece = advance((sums, piece), table, down)
    bias_grad = table_sums(sums + piece)
    pair_normed_grad = jnp.concatenate([finish(share_one), finish(share_two)], axis=1)
    (down_grad,), (up_grad, out_grad), (qkv_grad,) = [finish(flight) for flight in (down, up, table)]

    normed_grad = dot32(query_grad, query_weight, (1, 1)) + pair_normed_grad
    first_part, gain_one_grad, shift_one_grad = norm_one_back(normed_grad)
    first_grad = second_grad + first_part
    first_low = first_grad.astype(jnp.bfloat16).astype(jnp.float32)
    protein_sum = jnp.stack(
        [
            jnp.sum(jnp.where((segment_rows == index)[:, None], first_low, 0.0), axis=0)
            for index in range(proteins)
        ]
    )
    slots = 2 * dp_count
    slot = jnp.arange(slots) == 2 * place + core
    protein_slots = jnp.where(slot[:, None, None], protein_sum[None], 0.0)
    padding = jnp.zeros((6 * D - KERNELS * HEADS,), jnp.float32)
    last = sum_all(jnp.concatenate(
        [
            gain_one_grad,
            shift_one_grad,
            gain_two_grad,
            shift_two_grad,
            force_grad,
            jnp.concatenate([bias_grad.reshape(-1), padding]).reshape(6, D),
            protein_slots.reshape(slots * proteins, D),
        ],
        axis=0,
    ))
    vectors = part_of(last[:4], place, dp_count, 1)
    force_sum = part_of(last[4:7], place, dp_count, 1)
    bias_sum = part_of(last[7:13].reshape(-1)[:KERNELS * HEADS].reshape(KERNELS, HEADS), place, dp_count, 0)
    protein_all = last[13:]
    all_steps = in_order(step_list).reshape(slots * proteins).astype(jnp.float32)
    all_features = time_features(all_steps, D).astype(jnp.bfloat16)
    time_grad = jnp.einsum(
        "sd,se->de",
        part_of(all_features, place, dp_count, 1).astype(jnp.float32),
        protein_all,
        precision=highest,
    )

    return (
        give_row(block_low, 0),
        give_row(forces, 1),
        give_row(first_grad, 0),
        time_grad,
        vectors[0],
        vectors[1],
        qkv_grad,
        bias_sum,
        out_grad,
        vectors[2],
        vectors[3],
        up_grad,
        down_grad,
        force_sum,
    )


def solution(mesh):
    chips = mesh.shape["blk"] // 2
    rows = CHIP_ROW if chips % CHIP_ROW == 0 else 1
    fine = jax.sharding.Mesh(
        mesh.devices.reshape(mesh.shape["dp"], rows, chips // rows, 2), ("dp", "z", "x", "core")
    )
    blk = ("z", "x", "core")
    return jax.shard_map(
        body,
        mesh=fine,
        in_specs=(
            P("dp", blk, None),
            P("dp", None, blk),
            P("dp", blk),
            P("dp", None),
            P("dp", None),
            P("dp"),
            P("dp"),
            P("dp", None),
            P("dp", None),
            P("dp", None),
            P("dp"),
            P("dp"),
            P("dp", None),
            P("dp", None),
            P(None, "dp"),
            P("dp", blk, None),
            P("dp", None, blk),
        ),
        out_specs=(
            P("dp", blk, None),
            P("dp", None, blk),
            P("dp", blk, None),
            P("dp", None),
            P("dp"),
            P("dp"),
            P("dp", None),
            P("dp", None),
            P("dp", None),
            P("dp"),
            P("dp"),
            P("dp", None),
            P("dp", None),
            P(None, "dp"),
        ),
        check_vma=False,
    )
```

```python
import functools
import jax
import jax.numpy as jnp
import numpy as np
from jax import lax
from jax.sharding import PartitionSpec as P
from jax.experimental import pallas as pl
from jax.experimental.pallas import tpu as pltpu

D = 768
HEADS = 32
HEAD_DIM = 24
KERNELS = 128
GROUPS = 4
GROUP_HEADS = 8
GROUP_DIM = 192
GROUP_PAD = 256
LOG2E = 1.4426950408889634
SCALE = HEAD_DIM ** -0.5
SPAN = 8
NA = KERNELS // SPAN
masked_value = -1e30
VMEM_LIMIT = 60 * 2**20
FORWARD_TILE = 32
BACKWARD_TILE = 64
FINE = 8
KERNEL_COST = 2.5e8


def cost(micros, bytes_moved):
    return pl.CostEstimate(flops=int(micros * KERNEL_COST), bytes_accessed=int(bytes_moved), transcendentals=0)


def distance_tile(q_ref, k_ref):
    total = None
    for axis in range(3):
        offset = q_ref[:, axis:axis + 1] - k_ref[axis:axis + 1, :]
        total = offset * offset if total is None else total + offset * offset
    return jnp.sqrt(total) * (KERNELS / 48.0)


def kernel_rows(x):
    centre = lax.broadcasted_iota(jnp.int32, (NA, 1), 0).astype(jnp.float32) * (SPAN / 2.0) + SPAN / 4.0
    y = jnp.clip(x - centre, -24.0, 24.0)
    up_step = jnp.exp2(y * (0.5 * LOG2E))
    down_step = jnp.exp2(y * (-0.5 * LOG2E))
    middle = jnp.exp2((y * y) * (-0.5 * LOG2E))
    above = [middle]
    for _ in range(SPAN // 2 - 1):
        above.append(above[-1] * up_step)
    below = []
    current = middle
    for _ in range(SPAN // 2):
        current = current * down_step
        below.append(current)
    rows = below[::-1] + above
    return jnp.concatenate([r.astype(jnp.bfloat16) for r in rows], axis=0)


def kernel_order():
    step = np.arange(SPAN) - SPAN // 2
    order = np.array([[a * SPAN + SPAN // 2 + b for a in range(NA)] for b in step]).reshape(-1)
    factor = np.repeat(np.exp(-(step ** 2) / 8.0), NA).astype(np.float32)
    return order, factor


def bias_kernel(chunk, q_ref, k_ref, w_ref, *refs):
    out_ref, x_ref, m_ref = refs[-3:]
    rows = q_ref.shape[0]
    keys = k_ref.shape[1]
    x_ref[...] = distance_tile(q_ref, k_ref)
    m_ref[...] = jnp.where(q_ref[:, 3:4] == k_ref[3:4, :], 0.0, masked_value)
    w = w_ref[...]

    def step(t, carry):
        for start in range(0, keys, chunk):
            cols = slice(start, start + chunk)
            values = []
            for q in (2 * t, 2 * t + 1):
                value = jnp.dot(w, kernel_rows(x_ref[pl.ds(q, 1), cols]), preferred_element_type=jnp.float32)
                values.append(value + m_ref[pl.ds(q, 1), cols])
            for g in range(GROUPS):
                both = jnp.concatenate([value[g * GROUP_HEADS:(g + 1) * GROUP_HEADS] for value in values], axis=0)
                out_ref[g, pl.ds(t * 2 * GROUP_HEADS, 2 * GROUP_HEADS), cols] = both.astype(out_ref.dtype)
        return carry

    lax.fori_loop(0, rows // 2, step, 0, unroll=True)


def pair_bias(q_where, k_where, w, first, steps, previous):
    rows, keys = q_where.shape[0], k_where.shape[1]
    in_specs = [
        pl.BlockSpec((FINE, 8), lambda i: (i + first, 0)),
        pl.BlockSpec((8, keys), lambda i: (0, 0)),
        pl.BlockSpec((HEADS, KERNELS), lambda i: (0, 0)),
    ]
    operands = [q_where, k_where, w]
    aliases = {}
    if previous is not None:
        in_specs.append(pl.BlockSpec(memory_space=pl.ANY))
        operands.append(previous)
        aliases = {3: 0}
    return pl.pallas_call(
        functools.partial(bias_kernel, 256),
        grid=(steps,),
        in_specs=in_specs,
        out_specs=pl.BlockSpec((GROUPS, FINE * GROUP_HEADS, keys), lambda i: (0, i + first, 0)),
        out_shape=jax.ShapeDtypeStruct((GROUPS, rows * GROUP_HEADS, keys), jnp.bfloat16),
        scratch_shapes=[pltpu.VMEM((FINE, keys), jnp.float32), pltpu.VMEM((FINE, keys), jnp.float32)],
        input_output_aliases=aliases,
        cost_estimate=cost(1.5 * steps, FINE * steps * HEADS * keys * 2),
        compiler_params=pltpu.CompilerParams(vmem_limit_bytes=VMEM_LIMIT),
        name="pair_bias",
    )(*operands)


def project_kernel(x_ref, w_ref, turn_ref, key_ref, value_ref, w_turn_ref):
    @pl.when(pl.program_id(0) == 0)
    def turn_weight():
        w_turn_ref[...] = w_ref[...].T

    x = x_ref[...]
    rows = x.shape[0]
    turn_ref[...] = lax.dot_general(
        w_turn_ref[...], x, (((1,), (1,)), ((), ())), preferred_element_type=jnp.float32
    ).astype(turn_ref.dtype)
    flat = jnp.dot(x, w_ref[...], preferred_element_type=jnp.float32)
    for out_ref, first, filler in ((key_ref, 0, 0.0), (value_ref, D, 1.0)):
        for g in range(GROUPS):
            part = flat[:, first + g * GROUP_DIM:first + (g + 1) * GROUP_DIM]
            wide = jnp.concatenate([part, jnp.full((rows, GROUP_PAD - GROUP_DIM), filler, jnp.float32)], axis=1)
            out_ref[:, g * GROUP_PAD:(g + 1) * GROUP_PAD] = wide.astype(out_ref.dtype)


def project(values, weight):
    keys, depth = values.shape
    width = weight.shape[1]
    wide = GROUPS * GROUP_PAD
    block = 256
    return pl.pallas_call(
        project_kernel,
        grid=(keys // block,),
        in_specs=[
            pl.BlockSpec((block, depth), lambda i: (i, 0)),
            pl.BlockSpec((depth, width), lambda i: (0, 0)),
        ],
        out_specs=[
            pl.BlockSpec((width, block), lambda i: (0, i)),
            pl.BlockSpec((block, wide), lambda i: (i, 0)),
            pl.BlockSpec((block, wide), lambda i: (i, 0)),
        ],
        out_shape=[
            jax.ShapeDtypeStruct((width, keys), jnp.bfloat16),
            jax.ShapeDtypeStruct((keys, wide), jnp.bfloat16),
            jax.ShapeDtypeStruct((keys, wide), jnp.bfloat16),
        ],
        scratch_shapes=[pltpu.VMEM((width, depth), jnp.bfloat16)],
        cost_estimate=cost(12, keys * (depth + 3 * width) * 2),
        compiler_params=pltpu.CompilerParams(vmem_limit_bytes=VMEM_LIMIT),
        name="project",
    )(values, weight)


def head_mask(width):
    head = lax.broadcasted_iota(jnp.int32, (GROUP_HEADS, width), 0)
    lane = lax.broadcasted_iota(jnp.int32, (GROUP_HEADS, width), 1)
    return ((lane >= head * HEAD_DIM) & (lane < (head + 1) * HEAD_DIM)).astype(jnp.float32)


def spread_heads(values, mask):
    rows, width = values.shape
    return (values[:, None, :] * mask[None]).reshape(rows * GROUP_HEADS, width)


def gather_heads(values, mask):
    rows, width = values.shape
    return jnp.sum(values.reshape(rows // GROUP_HEADS, GROUP_HEADS, width) * mask[None], axis=1)


def forward_kernel(chunk, q_ref, kt_ref, v_ref, bias_ref, p_ref, o_ref, inv_ref, s_ref):
    keys = kt_ref.shape[1]
    mask = head_mask(GROUP_PAD)

    for g in range(GROUPS):
        rows = slice(g * GROUP_DIM, (g + 1) * GROUP_DIM)
        spread = spread_heads(q_ref[g].astype(jnp.float32), mask).astype(jnp.bfloat16)[:, :GROUP_DIM]
        peak = None
        for start in range(0, keys, chunk):
            s = jnp.dot(spread, kt_ref[rows, start:start + chunk], preferred_element_type=jnp.float32)
            s = s * (SCALE * LOG2E) + bias_ref[g, :, start:start + chunk].astype(jnp.float32)
            s_ref[:, start:start + chunk] = s
            for lane in range(0, chunk, 128):
                part = s[:, lane:lane + 128]
                peak = part if peak is None else jnp.maximum(peak, part)
        top = jnp.max(peak, axis=1, keepdims=True)
        for start in range(0, keys, chunk):
            p_ref[g, :, start:start + chunk] = jnp.exp2(s_ref[:, start:start + chunk] - top).astype(jnp.bfloat16)
        mixed = jnp.dot(p_ref[g], v_ref[:, g * GROUP_PAD:(g + 1) * GROUP_PAD], preferred_element_type=jnp.float32)
        inverse = 1.0 / mixed[:, GROUP_DIM:GROUP_DIM + 1]
        o_ref[g] = gather_heads(mixed * inverse, mask)
        inv_ref[g] = gather_heads(jnp.broadcast_to(inverse, mixed.shape), mask)


def attend(q, turned, value_flat, bias):
    rows, keys = q.shape[1], turned.shape[1]
    tile = min(FORWARD_TILE, FORWARD_TILE * 2048 // keys)
    whole = pl.Buffered(1)
    return pl.pallas_call(
        functools.partial(forward_kernel, 512),
        grid=(rows // tile,),
        in_specs=[
            pl.BlockSpec((GROUPS, tile, GROUP_PAD), lambda i: (0, i, 0)),
            pl.BlockSpec((D, keys), lambda i: (0, 0), pipeline_mode=whole),
            pl.BlockSpec((keys, GROUPS * GROUP_PAD), lambda i: (0, 0), pipeline_mode=whole),
            pl.BlockSpec((GROUPS, tile * GROUP_HEADS, keys), lambda i: (0, i, 0)),
        ],
        out_specs=[
            pl.BlockSpec((GROUPS, tile * GROUP_HEADS, keys), lambda i: (0, i, 0)),
            pl.BlockSpec((GROUPS, tile, GROUP_PAD), lambda i: (0, i, 0)),
            pl.BlockSpec((GROUPS, tile, GROUP_PAD), lambda i: (0, i, 0)),
        ],
        out_shape=[
            jax.ShapeDtypeStruct((GROUPS, rows * GROUP_HEADS, keys), jnp.bfloat16),
            jax.ShapeDtypeStruct((GROUPS, rows, GROUP_PAD), jnp.float32),
            jax.ShapeDtypeStruct((GROUPS, rows, GROUP_PAD), jnp.float32),
        ],
        scratch_shapes=[
            pltpu.VMEM((tile * GROUP_HEADS, keys), jnp.float32),
        ],
        input_output_aliases={3: 0},
        cost_estimate=cost(45, rows * HEADS * keys * 4),
        compiler_params=pltpu.CompilerParams(vmem_limit_bytes=VMEM_LIMIT),
        name="attend",
    )(q, turned, value_flat, bias)


def backward_kernel(chunk, q_ref, do_ref, o_ref, k_ref, vt_ref, p_ref, ds_ref, dq_ref, dkt_ref, dvt_ref, dk_acc, dv_acc):
    keys = vt_ref.shape[1]
    mask = head_mask(GROUP_PAD)
    tile = pl.program_id(0)
    groups = q_ref.shape[0]

    @pl.when(tile == 0)
    def start_group():
        dk_acc[...] = jnp.zeros_like(dk_acc)
        dv_acc[...] = jnp.zeros_like(dv_acc)

    for g in range(groups):
        rows = slice(g * GROUP_DIM, (g + 1) * GROUP_DIM)
        q_wide = spread_heads(q_ref[g].astype(jnp.float32), mask)
        do_wide = spread_heads(do_ref[g].astype(jnp.float32), mask)
        o_wide = spread_heads(o_ref[g], mask)
        delta = jnp.sum(do_wide * o_wide, axis=1, keepdims=True)
        do_low = do_wide.astype(jnp.bfloat16)[:, :GROUP_DIM]
        do_turn = do_wide[:, :GROUP_DIM].T.astype(jnp.bfloat16)
        q_turn = q_wide[:, :GROUP_DIM].T.astype(jnp.bfloat16)
        for start in range(0, keys, chunk):
            cols = slice(start, start + chunk)
            dp = jnp.dot(do_low, vt_ref[rows, cols], preferred_element_type=jnp.float32)
            p = p_ref[g, :, cols]
            ds = (p.astype(jnp.float32) * (dp - delta)).astype(jnp.bfloat16)
            ds_ref[g, :, cols] = ds
            dv_acc[rows, cols] += jnp.dot(do_turn, p, preferred_element_type=jnp.float32)
            dk_acc[rows, cols] += jnp.dot(q_turn, ds, preferred_element_type=jnp.float32)
        dq = jnp.dot(ds_ref[g], k_ref[:, g * GROUP_PAD:(g + 1) * GROUP_PAD], preferred_element_type=jnp.float32)
        dq_ref[g] = gather_heads(dq, mask) * SCALE

    @pl.when(tile == pl.num_programs(0) - 1)
    def finish():
        dkt_ref[...] = (dk_acc[...] * SCALE).astype(dkt_ref.dtype)
        dvt_ref[...] = dv_acc[...].astype(dvt_ref.dtype)


def attend_back(q, do, o, key_flat, turned, p, part, parts):
    rows, keys = q.shape[1], turned.shape[1]
    tile = min(BACKWARD_TILE, BACKWARD_TILE * 2048 // keys)
    groups = GROUPS // parts
    width = groups * GROUP_DIM
    whole = pl.Buffered(1)
    narrow = pl.BlockSpec((groups, tile, GROUP_PAD), lambda i: (part, i, 0))
    return pl.pallas_call(
        functools.partial(backward_kernel, 512),
        grid=(rows // tile,),
        in_specs=[
            narrow,
            narrow,
            narrow,
            pl.BlockSpec((keys, groups * GROUP_PAD), lambda i: (0, part), pipeline_mode=whole),
            pl.BlockSpec((width, keys), lambda i: (part + parts, 0), pipeline_mode=whole),
            pl.BlockSpec((groups, tile * GROUP_HEADS, keys), lambda i: (part, i, 0)),
        ],
        out_specs=[
            pl.BlockSpec((groups, tile * GROUP_HEADS, keys), lambda i: (part, i, 0)),
            pl.BlockSpec((groups, tile, GROUP_PAD), lambda i: (0, i, 0)),
            pl.BlockSpec((width, keys), lambda i: (0, 0), pipeline_mode=whole),
            pl.BlockSpec((width, keys), lambda i: (0, 0), pipeline_mode=whole),
        ],
        out_shape=[
            jax.ShapeDtypeStruct(p.shape, p.dtype),
            jax.ShapeDtypeStruct((groups, rows, GROUP_PAD), jnp.float32),
            jax.ShapeDtypeStruct((width, keys), jnp.bfloat16),
            jax.ShapeDtypeStruct((width, keys), jnp.bfloat16),
        ],
        scratch_shapes=[
            pltpu.VMEM((width, keys), jnp.float32),
            pltpu.VMEM((width, keys), jnp.float32),
        ],
        input_output_aliases={5: 0},
        cost_estimate=cost(56 / parts, rows * HEADS * keys * 4 // parts),
        compiler_params=pltpu.CompilerParams(vmem_limit_bytes=VMEM_LIMIT),
        name="attend_back",
    )(q, do, o, key_flat, turned, p)


def table_grad_kernel(chunk, q_ref, k_ref, ds_ref, out_ref, x_ref):
    rows = q_ref.shape[0]
    keys = k_ref.shape[1]
    pair = 2 * GROUP_HEADS

    @pl.when(pl.program_id(0) == 0)
    def start_zero():
        out_ref[...] = jnp.zeros_like(out_ref)

    x_ref[...] = distance_tile(q_ref, k_ref)

    def step(t, total):
        for start in range(0, keys, chunk):
            x = x_ref[pl.ds(2 * t, 2), start:start + chunk]
            table = jnp.concatenate([kernel_rows(x[0:1]), kernel_rows(x[1:2])], axis=0)
            grads = jnp.concatenate(
                [ds_ref[g, pl.ds(t * pair, pair), start:start + chunk] for g in range(GROUPS)], axis=0
            )
            total = total + lax.dot_general(table, grads, (((1,), (1,)), ((), ())), preferred_element_type=jnp.float32)
        return total

    out_ref[...] += lax.fori_loop(0, rows // 2, step, jnp.zeros(out_ref.shape, jnp.float32), unroll=True)


def table_grad(q_where, k_where, ds, first, steps):
    rows, keys = q_where.shape[0], k_where.shape[1]
    wide = 2 * HEADS
    return pl.pallas_call(
        functools.partial(table_grad_kernel, 256),
        grid=(steps,),
        in_specs=[
            pl.BlockSpec((FINE, 8), lambda i: (i + first, 0)),
            pl.BlockSpec((8, keys), lambda i: (0, 0)),
            pl.BlockSpec((GROUPS, FINE * GROUP_HEADS, keys), lambda i: (0, i + first, 0)),
        ],
        out_specs=pl.BlockSpec((2 * KERNELS, wide), lambda i: (0, 0)),
        out_shape=jax.ShapeDtypeStruct((2 * KERNELS, wide), jnp.float32),
        scratch_shapes=[pltpu.VMEM((FINE, keys), jnp.float32)],
        cost_estimate=cost(1.6 * steps, FINE * steps * HEADS * keys * 2),
        compiler_params=pltpu.CompilerParams(vmem_limit_bytes=VMEM_LIMIT),
        name="table_grad",
    )(q_where, k_where, ds)


def table_sums(sums):
    sums = sums.reshape(2, KERNELS, GROUPS, 2, GROUP_HEADS)
    both = (sums[0, :, :, 0] + sums[1, :, :, 1]).reshape(KERNELS, HEADS)
    order, factor = kernel_order()
    return (both * factor[:, None])[np.argsort(order)]


def place_kernel(steps, s_ref, *refs):
    own_ref = refs[0]
    mine, other = refs[1:1 + steps], refs[1 + steps:1 + 2 * steps]
    out_ref = refs[-1]
    j = pl.program_id(0)
    place, core = s_ref[0], s_ref[1]
    away = lax.rem(place - j // 2 + steps + 1, steps + 1)

    @pl.when(away == 0)
    def own_part():
        out_ref[...] = own_ref[...]

    for step in range(1, steps + 1):
        @pl.when((away == step) & (core == j % 2))
        def fetched_part():
            out_ref[...] = mine[step - 1][...]

        @pl.when((away == step) & (core != j % 2))
        def passed_part():
            out_ref[...] = other[step - 1][...]


def place_shards(where, own, mine, other):
    steps = len(mine)
    rows, columns = own.shape
    half = rows // 2
    fixed = pl.BlockSpec((half, columns), lambda j, s: (0, 0))
    return pl.pallas_call(
        functools.partial(place_kernel, steps),
        grid_spec=pltpu.PrefetchScalarGridSpec(
            num_scalar_prefetch=1,
            grid=(2 * (steps + 1),),
            in_specs=[pl.BlockSpec((half, columns), lambda j, s: (j % 2, 0))] + [fixed] * (2 * steps),
            out_specs=pl.BlockSpec((half, columns), lambda j, s: (j, 0)),
        ),
        out_shape=jax.ShapeDtypeStruct(((steps + 1) * rows, columns), own.dtype),
        cost_estimate=cost(3, 2 * (steps + 1) * own.size * 2),
        compiler_params=pltpu.CompilerParams(vmem_limit_bytes=VMEM_LIMIT),
        name="place_shards",
    )(where, own, *mine, *other)


def assemble_kernel(xs, widths, s_ref, *refs):
    own_refs, other_refs, out_refs = refs[:xs], refs[xs:2 * xs], refs[2 * xs:]
    zs = own_refs[0].shape[0]
    x, core = s_ref[0], s_ref[1]
    jx = pl.program_id(0)
    from_x = lax.rem(x - jx + xs, xs)
    first = core == 0
    for step in range(xs):
        @pl.when(from_x == step)
        def copy_piece():
            for jz in range(zs):
                begin = 0
                for half, out_ref in zip(widths, out_refs):
                    own = own_refs[step][jz, :, begin:begin + half].astype(jnp.float32)
                    other = other_refs[step][jz, :, begin:begin + half].astype(jnp.float32)
                    out_ref[0, jz, :, :half] = jnp.where(first, own, other)
                    out_ref[0, jz, :, half:] = jnp.where(first, other, own)
                    begin += half


def assemble(where, own, other, widths):
    xs = len(own)
    zs, rows, columns = own[0].shape
    spec = pl.BlockSpec((zs, rows, columns), lambda i, s: (0, 0, 0))
    wholes = pl.pallas_call(
        functools.partial(assemble_kernel, xs, widths),
        grid_spec=pltpu.PrefetchScalarGridSpec(
            num_scalar_prefetch=1,
            grid=(xs,),
            in_specs=[spec] * (2 * xs),
            out_specs=[pl.BlockSpec((1, zs, rows, 2 * half), lambda i, s: (i, 0, 0, 0)) for half in widths],
        ),
        out_shape=[jax.ShapeDtypeStruct((xs, zs, rows, 2 * half), jnp.float32) for half in widths],
        cost_estimate=cost(4, xs * zs * rows * columns * 12),
        compiler_params=pltpu.CompilerParams(vmem_limit_bytes=VMEM_LIMIT),
        name="assemble",
    )(where, *own, *other)
    return [whole.reshape(xs * zs * rows, -1) for whole in wholes]


eps = 1e-05
highest = lax.Precision.HIGHEST
CHIP_ROW = 4
Z_EXCHANGE = True


def layer_norm(values, norm_gain, norm_shift):
    centred = values - jnp.mean(values, axis=-1, keepdims=True)
    spread = jnp.mean(centred * centred, axis=-1, keepdims=True)
    return centred * lax.rsqrt(spread + eps) * norm_gain + norm_shift


def exact_gelu(values):
    return jax.nn.gelu(values, approximate=False)


def time_features(stamps, feature_width):
    half_width = feature_width // 2
    frequency = jnp.exp(-jnp.log(10000.0) * jnp.arange(half_width, dtype=jnp.float32) / half_width)
    angles = stamps[:, None] * frequency[None, :]
    return jnp.concatenate([jnp.sin(angles), jnp.cos(angles)], axis=1)


def shifted(values, axis, step):
    size = lax.axis_size(axis)
    return lax.ppermute(values, axis, [(i, (i + step) % size) for i in range(size)])


def part_of(values, index, count, axis):
    length = values.shape[axis] // count
    return lax.dynamic_slice_in_dim(values, index * length, length, axis)


def dot32(left, right, contract):
    return lax.dot_general(left, right, ((contract[:1], contract[1:]), ((), ())), preferred_element_type=jnp.float32)


def in_order(pieces):
    count = len(pieces)
    place = lax.axis_index("dp")
    chosen = []
    for index in range(count):
        step = lax.rem(place - index + count, count)
        picked = pieces[0]
        for other in range(1, count):
            picked = jnp.where(step == other, pieces[other], picked)
        chosen.append(picked)
    return jnp.stack(chosen)


def spread_dp(values):
    return [values] + [shifted(values, "dp", step) for step in range(1, lax.axis_size("dp"))]


def fetch_shards(weight):
    half = part_of(weight, lax.axis_index("core"), 2, 0)
    return [shifted(half, "dp", step) for step in range(1, lax.axis_size("dp"))]


def pass_on(mine):
    return [shifted(piece, "core", 1) for piece in mine]


def gather_weight(weight, mine, other):
    where = jnp.stack([lax.axis_index("dp"), lax.axis_index("core")]).astype(jnp.int32)
    return place_shards(where, weight, mine, other)


def tie(*groups):
    return lax.optimization_barrier(groups)


def add_parts(own, incoming):
    total = own.astype(jnp.float32)
    for share in incoming:
        total = total + share.astype(jnp.float32)
    return total


def turn_back(values, axis):
    count, place = lax.axis_size(axis), lax.axis_index(axis)
    ring = jnp.concatenate([values, values], axis=0)[::-1]
    return lax.dynamic_slice_in_dim(ring, count - 1 - place, count, 0)


def reduce_chain(local, hops, widths):
    left = ["dp", "x", "z"]
    for axis in hops:
        dim = left.index(axis)
        left.pop(dim)
        count, place = lax.axis_size(axis), lax.axis_index(axis)
        if axis == "z" and Z_EXCHANGE:
            local = yield lax.all_to_all(local.astype(jnp.bfloat16), "z", dim, 0)
            local = jnp.sum(local.astype(jnp.float32), axis=0)
            continue
        own = lax.dynamic_index_in_dim(local, place, dim, keepdims=False)
        incoming = [
            shifted(
                lax.dynamic_index_in_dim(local, lax.rem(place + step, count), dim, keepdims=False).astype(jnp.bfloat16),
                axis,
                step,
            )
            for step in range(1, count)
        ]
        own, incoming = yield own, incoming
        local = add_parts(own, incoming)
    owned = local.astype(jnp.bfloat16)
    if Z_EXCHANGE:
        copies = jnp.broadcast_to(owned[None], (lax.axis_size("z"),) + owned.shape)
        pieces = yield lax.all_to_all(copies, "z", 0, 0)
    else:
        owned, incoming = yield owned, [shifted(owned, "z", step) for step in range(1, lax.axis_size("z"))]
        pieces = turn_back(jnp.stack([owned] + incoming), "z")
    own = yield [pieces] + [shifted(pieces, "x", step) for step in range(1, lax.axis_size("x"))]
    own, other = yield own, [shifted(piece, "core", 1) for piece in own]
    where = jnp.stack([lax.axis_index(axis) for axis in ("x", "core")]).astype(jnp.int32)
    return assemble(where, own, other, widths)


def by_owner(values):
    counts = [lax.axis_size(axis) for axis in ("dp", "x", "z")]
    return values.reshape(counts + [-1, values.shape[1]])


def weight_chain(factors, hops):
    core = lax.axis_index("core")
    moving = []
    for inputs, grads in factors:
        moving.append((
            inputs, shifted(inputs, "core", 1),
            part_of(grads, core, 2, 1), shifted(part_of(grads, 1 - core, 2, 1), "core", 1),
        ))
    moving = yield moving
    local = [
        dot32(jnp.concatenate([left, other_left], axis=0), jnp.concatenate([right, other_right], axis=0), (0, 0))
        .astype(jnp.bfloat16)
        for left, other_left, right, other_right in moving
    ]
    return (yield from reduce_chain(by_owner(jnp.concatenate(local, axis=1)), hops, [part.shape[1] for part in local]))


def table_chain(local, hops):
    core = lax.axis_index("core")
    own = part_of(local, core, 2, 1)
    own, other = yield own, shifted(part_of(local, 1 - core, 2, 1), "core", 1)
    chip = (own.astype(jnp.float32) + other.astype(jnp.float32)).astype(jnp.bfloat16)
    return (yield from reduce_chain(by_owner(chip), hops, [chip.shape[1]]))


def share_chain(shares):
    x_count, z_count = shares.shape[:2]
    own, incoming = yield shares[0], [shifted(shares[step], "x", -step) for step in range(1, x_count)]
    total = add_parts(own, incoming)
    low = total.astype(jnp.bfloat16)
    own, incoming = yield total[0], [shifted(low[step], "z", -step) for step in range(1, z_count)]
    return add_parts(own, incoming)


class Flight:
    def __init__(self, chain):
        self.chain = chain
        self.values = next(chain)
        self.result = None

    def land(self, values):
        try:
            self.values = self.chain.send(values)
        except StopIteration as stop:
            self.values, self.result = None, stop.value


def advance(inputs, *flights):
    flights = [flight for flight in flights if flight.values is not None]
    inputs, landed = lax.optimization_barrier((inputs, [flight.values for flight in flights]))
    for flight, values in zip(flights, landed):
        flight.land(values)
    return inputs


def finish(flight):
    while flight.values is not None:
        flight.land(flight.values)
    return flight.result


def sum_all(values):
    for axis in ("core", "dp", "x", "z"):
        values = functools.reduce(
            jnp.add, [shifted(values, axis, step) for step in range(1, lax.axis_size(axis))], values
        )
    return values


def by_group(values):
    wide = values.reshape(values.shape[0], GROUPS, GROUP_DIM)
    wide = jnp.pad(wide, ((0, 0), (0, 0), (0, GROUP_PAD - GROUP_DIM)))
    return jnp.transpose(wide, (1, 0, 2))


def flat_groups(values):
    return jnp.transpose(values[:, :, :GROUP_DIM], (1, 0, 2)).reshape(values.shape[1], D)


def body(
    residues,
    coordinates,
    segment_ids,
    time_steps,
    time_weight,
    norm1_gain,
    norm1_bias,
    qkv_weight,
    bias_weight,
    out_weight,
    norm2_gain,
    norm2_bias,
    up_weight,
    down_weight,
    force_weight,
    out_cotangent,
    force_cotangent,
):
    core = lax.axis_index("core")
    place = lax.axis_index("dp")
    dp_count = lax.axis_size("dp")
    x_count, z_count = lax.axis_size("x"), lax.axis_size("z")
    held = residues.shape[1]

    def take_row(values):
        mine = lax.dynamic_index_in_dim(values, core, 0, keepdims=False)
        other = lax.dynamic_index_in_dim(values, 1 - core, 0, keepdims=False)
        return mine, shifted(other, "core", 1)

    def give_row(values, axis):
        mine = lax.slice_in_dim(values, 0, held, axis=axis)
        other = shifted(lax.slice_in_dim(values, held, 2 * held, axis=axis), "core", 1)
        first_row = jnp.where(core == 0, mine, other)
        second_row = jnp.where(core == 0, other, mine)
        return jnp.stack([first_row, second_row])

    where_own = jnp.concatenate(
        [coordinates, segment_ids[:, None, :].astype(jnp.bfloat16)], axis=1
    )
    where_rows = jnp.concatenate(take_row(where_own), axis=1)
    bias_parts = [bias_weight] + [shifted(bias_weight, "dp", step) for step in range(1, dp_count)]
    residue_parts = take_row(residues)
    step_list = spread_dp(time_steps)

    where_keys = where_rows[None]
    reach = 1
    while reach < z_count:
        where_keys = jnp.concatenate([where_keys, shifted(where_keys, "z", reach)], axis=0)
        reach *= 2
    where_columns = [where_keys[:z_count]]
    for x_step in range(1, x_count):
        where_columns.append(shifted(where_columns[0], "x", x_step))
    (
        where_columns,
        where_rows,
        bias_parts,
        residue_parts,
        step_list,
        (norm1_gain, norm1_bias, norm2_gain, norm2_bias, force_weight),
        (time_weight, qkv_weight, out_weight, up_weight, down_weight),
        (out_cotangent, force_cotangent),
    ) = tie(
        where_columns,
        where_rows,
        bias_parts,
        residue_parts,
        step_list,
        (norm1_gain, norm1_bias, norm2_gain, norm2_bias, force_weight),
        (time_weight, qkv_weight, out_weight, up_weight, down_weight),
        (out_cotangent, force_cotangent),
    )
    key_where = jnp.transpose(jnp.concatenate(where_columns, axis=0).astype(jnp.float32), (1, 0, 2))
    key_where = jnp.pad(key_where.reshape(4, -1), ((0, 4), (0, 0)))
    query_where = jnp.pad(jnp.transpose(where_rows).astype(jnp.float32), ((0, 0), (0, 4)))
    segment_rows = where_rows[3]
    residue_rows = jnp.concatenate(residue_parts, axis=0).astype(jnp.float32)

    bias_full = in_order(bias_parts).reshape(KERNELS, HEADS)
    order, factor = kernel_order()
    table_weight = (
        jnp.transpose(bias_full).astype(jnp.float32)[:, order] * (factor * LOG2E)
    ).astype(jnp.bfloat16)
    tiles = 2 * held // FINE
    lead = tiles // 8
    bias = pair_bias(query_where, key_where, table_weight, 0, lead, None)

    vectors = in_order(
        spread_dp(jnp.concatenate([jnp.stack([norm1_gain, norm1_bias, norm2_gain, norm2_bias]), force_weight], axis=0))
    )
    vectors = jnp.transpose(vectors, (1, 0, 2)).reshape(7, D)
    gain_one, shift_one, gain_two, shift_two = [vectors[i:i + 1].astype(jnp.float32) for i in range(4)]
    force_full = vectors[4:]
    proteins = time_steps.shape[1]
    row_steps = [lax.dynamic_index_in_dim(steps, core, 0, keepdims=False) for steps in step_list]
    features = time_features(jnp.concatenate(row_steps).astype(jnp.float32), D).astype(jnp.bfloat16)
    features = part_of(features, place, dp_count, 1)
    stamp_part = jnp.dot(features, time_weight, preferred_element_type=jnp.float32)
    stamp_rows = stamp_part[:proteins]
    for step in range(1, dp_count):
        stamp_rows = stamp_rows + shifted(
            stamp_part[step * proteins:(step + 1) * proteins], "dp", -step
        )
    query_own, pair_own = qkv_weight[:, :D], qkv_weight[:, D:]
    pair_half = fetch_shards(pair_own)
    query_half = fetch_shards(query_own)
    bias, stamp_rows, vectors_ready = tie(bias, stamp_rows, (gain_one, shift_one))
    gain_one, shift_one = vectors_ready

    def by_protein(table):
        picked = jnp.zeros((2 * held, table.shape[1]), jnp.float32)
        for index in range(proteins):
            picked = picked + jnp.where((segment_rows == index)[:, None], table[index][None, :], 0.0)
        return picked

    first = residue_rows + by_protein(stamp_rows)
    normed, norm_one_back = jax.vjp(layer_norm, first, gain_one, shift_one)
    normed_low = normed.astype(jnp.bfloat16)

    columns = [[None] * z_count for _ in range(x_count)]
    current = normed_low
    done = lead
    out_half = up_half = down_half = None
    for z_step in range(z_count):
        steps = (tiles - done) // (z_count - z_step)
        across = [current]
        for x_step in range(1, x_count):
            across.append(shifted(across[-1], "x", 1))
        following = shifted(current, "z", 1) if z_step < z_count - 1 else current
        bias = pair_bias(query_where, key_where, table_weight, done, steps, bias)
        done += steps
        bias, current, across = tie(bias, following, across)
        for x_step in range(x_count):
            columns[x_step][z_step] = across[x_step]
        if z_step == 1:
            bias, pair_half, query_half, later = tie(bias, pair_half, query_half, (out_weight, up_weight, down_weight))
            out_weight, up_weight, down_weight = later
            out_half, up_half, down_half = fetch_shards(out_weight), fetch_shards(up_weight), fetch_shards(down_weight)
            pair_passed = pass_on(pair_half)
            query_passed = pass_on(query_half)
    normed_all = jnp.concatenate([piece for column in columns for piece in column], axis=0)

    query_weight = gather_weight(query_own, query_half, query_passed)
    pair_weight = gather_weight(pair_own, pair_half, pair_passed)
    query = by_group(jnp.dot(normed_low, query_weight, preferred_element_type=jnp.float32).astype(jnp.bfloat16))
    turned, key_flat, value_flat = project(normed_all, pair_weight)
    probs, attended, inverse = attend(query, turned, value_flat, bias)
    attended_low = flat_groups(attended).astype(jnp.bfloat16)
    attended_low, out_half, up_half, down_half, cotangents = tie(
        attended_low, out_half, up_half, down_half, (out_cotangent, force_cotangent)
    )
    out_cotangent, force_cotangent = cotangents
    out_full = gather_weight(out_weight, out_half, pass_on(out_half))
    up_full = gather_weight(up_weight, up_half, pass_on(up_half))
    down_full = gather_weight(down_weight, down_half, pass_on(down_half))
    cot_rows = jnp.concatenate(take_row(out_cotangent), axis=0).astype(jnp.float32)
    force_cot = jnp.concatenate(take_row(force_cotangent), axis=1)

    second = first + jnp.dot(attended_low, out_full, preferred_element_type=jnp.float32)
    normed_two, norm_two_back = jax.vjp(layer_norm, second, gain_two, shift_two)
    normed_two_low = normed_two.astype(jnp.bfloat16)
    hidden = jnp.dot(normed_two_low, up_full, preferred_element_type=jnp.float32)
    activated, gelu_back = jax.vjp(exact_gelu, hidden)
    activated_low = activated.astype(jnp.bfloat16)
    third = second + jnp.dot(activated_low, down_full, preferred_element_type=jnp.float32)
    block_low = third.astype(jnp.bfloat16)
    forces = jnp.einsum("cd,qd->cq", force_full, block_low, preferred_element_type=jnp.float32)
    third_grad = cot_rows + jnp.einsum(
        "cq,cd->qd", force_cot, force_full.astype(jnp.float32), precision=highest
    )
    force_grad = jnp.einsum(
        "cq,qd->cd", force_cot, block_low.astype(jnp.float32), precision=highest
    )
    third_low = third_grad.astype(jnp.bfloat16)
    activated_grad = dot32(third_low, down_full, (1, 1))
    hidden_grad = gelu_back(activated_grad)[0].astype(jnp.bfloat16)
    normed_two_grad = dot32(hidden_grad, up_full, (1, 1))
    second_part, gain_two_grad, shift_two_grad = norm_two_back(normed_two_grad)
    second_grad = third_grad + second_part
    second_low = second_grad.astype(jnp.bfloat16)
    attended_grad = by_group(dot32(second_low, out_full, (1, 1)).astype(jnp.bfloat16))
    scaled_grad = (attended_grad.astype(jnp.float32) * inverse).astype(jnp.bfloat16)

    down = Flight(weight_chain([(activated_low, third_low)], ("dp", "x", "z")))
    up = Flight(weight_chain([(normed_two_low, hidden_grad), (attended_low, second_low)], ("x", "dp", "z")))

    scaled_grad = advance(scaled_grad, down, up)
    back = attend_back(query, scaled_grad, attended, key_flat, turned, probs, 0, 4)
    backs = [back[1:]]
    pairs, scaled_grad = advance((back[0], scaled_grad))
    back = attend_back(query, scaled_grad, attended, key_flat, turned, pairs, 1, 4)
    backs.append(back[1:])
    pairs, scaled_grad = advance((back[0], scaled_grad), down, up)
    back = attend_back(query, scaled_grad, attended, key_flat, turned, pairs, 2, 4)
    backs.append(back[1:])
    pairs, scaled_grad = advance((back[0], scaled_grad), down, up)
    back = attend_back(query, scaled_grad, attended, key_flat, turned, pairs, 3, 4)
    backs.append(back[1:])
    logit_grad, backs = advance((back[0], backs), down)
    query_grad = flat_groups(jnp.concatenate([back[0] for back in backs], axis=0)).astype(jnp.bfloat16)
    pair_grad_turn = jnp.concatenate([back[1] for back in backs] + [back[2] for back in backs], axis=0)

    query_part = dot32(normed_low, query_grad, (0, 0)).astype(jnp.bfloat16)
    pair_part = dot32(normed_all, pair_grad_turn, (0, 1)).astype(jnp.bfloat16)
    table = Flight(table_chain(jnp.concatenate([query_part, pair_part], axis=1), ("dp", "x", "z")))
    pair_share = dot32(pair_grad_turn, pair_weight, (0, 1)).astype(jnp.bfloat16)
    own = pair_share.reshape(x_count, z_count, 2 * held, D)
    first_half, second_half = own[..., :D // 2], own[..., D // 2:]
    share_one = Flight(share_chain(first_half))
    steps = tiles // 4
    logit_grad, second_half = advance((logit_grad, second_half), up, table)
    sums = table_grad(query_where, key_where, logit_grad, 0, steps)
    sums, logit_grad, second_half = advance((sums, logit_grad, second_half), share_one, down)
    share_two = Flight(share_chain(second_half))
    piece = table_grad(query_where, key_where, logit_grad, steps, steps)
    sums, piece, logit_grad = advance((sums, piece, logit_grad), share_one, share_two, table)
    sums = sums + piece
    piece = table_grad(query_where, key_where, logit_grad, 2 * steps, steps)
    sums, piece, logit_grad = advance((sums, piece, logit_grad), share_two, table, up)
    sums = sums + piece
    piece = table_grad(query_where, key_where, logit_grad, 3 * steps, steps)
    sums, piece = advance((sums, piece), table, down)
    bias_grad = table_sums(sums + piece)
    pair_normed_grad = jnp.concatenate([finish(share_one), finish(share_two)], axis=1)
    (down_grad,), (up_grad, out_grad) = finish(down), finish(up)
    table.land(table.values)
    table.land(table.values)
    (down_grad, up_grad, out_grad), last_pieces = tie((down_grad, up_grad, out_grad), table.values)
    table.land(last_pieces)
    (qkv_grad,) = finish(table)

    normed_grad = dot32(query_grad, query_weight, (1, 1)) + pair_normed_grad
    first_part, gain_one_grad, shift_one_grad = norm_one_back(normed_grad)
    first_grad = second_grad + first_part
    first_low = first_grad.astype(jnp.bfloat16).astype(jnp.float32)
    protein_sum = jnp.stack(
        [
            jnp.sum(jnp.where((segment_rows == index)[:, None], first_low, 0.0), axis=0)
            for index in range(proteins)
        ]
    )
    slots = 2 * dp_count
    slot = jnp.arange(slots) == 2 * place + core
    protein_slots = jnp.where(slot[:, None, None], protein_sum[None], 0.0)
    padding = jnp.zeros((6 * D - KERNELS * HEADS,), jnp.float32)
    last = sum_all(jnp.concatenate(
        [
            gain_one_grad,
            shift_one_grad,
            gain_two_grad,
            shift_two_grad,
            force_grad,
            jnp.concatenate([bias_grad.reshape(-1), padding]).reshape(6, D),
            protein_slots.reshape(slots * proteins, D),
        ],
        axis=0,
    ))
    vectors = part_of(last[:4], place, dp_count, 1)
    force_sum = part_of(last[4:7], place, dp_count, 1)
    bias_sum = part_of(last[7:13].reshape(-1)[:KERNELS * HEADS].reshape(KERNELS, HEADS), place, dp_count, 0)
    protein_all = last[13:]
    all_steps = in_order(step_list).reshape(slots * proteins).astype(jnp.float32)
    all_features = time_features(all_steps, D).astype(jnp.bfloat16)
    time_grad = jnp.einsum(
        "sd,se->de",
        part_of(all_features, place, dp_count, 1).astype(jnp.float32),
        protein_all,
        precision=highest,
    )

    return (
        give_row(block_low, 0),
        give_row(forces, 1),
        give_row(first_grad, 0),
        time_grad,
        vectors[0],
        vectors[1],
        qkv_grad,
        bias_sum,
        out_grad,
        vectors[2],
        vectors[3],
        up_grad,
        down_grad,
        force_sum,
    )


def solution(mesh):
    chips = mesh.shape["blk"] // 2
    rows = CHIP_ROW if chips % CHIP_ROW == 0 else 1
    fine = jax.sharding.Mesh(
        mesh.devices.reshape(mesh.shape["dp"], rows, chips // rows, 2), ("dp", "z", "x", "core")
    )
    blk = ("z", "x", "core")
    return jax.shard_map(
        body,
        mesh=fine,
        in_specs=(
            P("dp", blk, None),
            P("dp", None, blk),
            P("dp", blk),
            P("dp", None),
            P("dp", None),
            P("dp"),
            P("dp"),
            P("dp", None),
            P("dp", None),
            P("dp", None),
            P("dp"),
            P("dp"),
            P("dp", None),
            P("dp", None),
            P(None, "dp"),
            P("dp", blk, None),
            P("dp", None, blk),
        ),
        out_specs=(
            P("dp", blk, None),
            P("dp", None, blk),
            P("dp", blk, None),
            P("dp", None),
            P("dp"),
            P("dp"),
            P("dp", None),
            P("dp", None),
            P("dp", None),
            P("dp"),
            P("dp"),
            P("dp", None),
            P("dp", None),
            P(None, "dp"),
        ),
        check_vma=False,
    )
```

```python
import functools
import jax
import jax.numpy as jnp
import numpy as np
from jax import lax
from jax.sharding import PartitionSpec as P
from jax.experimental import pallas as pl
from jax.experimental.pallas import tpu as pltpu

D = 768
HEADS = 32
HEAD_DIM = 24
KERNELS = 128
GROUPS = 4
GROUP_HEADS = 8
GROUP_DIM = 192
GROUP_PAD = 256
LOG2E = 1.4426950408889634
SCALE = HEAD_DIM ** -0.5
SPAN = 8
NA = KERNELS // SPAN
masked_value = -1e30
VMEM_LIMIT = 60 * 2**20
FORWARD_TILE = 32
BACKWARD_TILE = 64
FINE = 8
KERNEL_COST = 2.5e8


def cost(micros, bytes_moved):
    return pl.CostEstimate(flops=int(micros * KERNEL_COST), bytes_accessed=int(bytes_moved), transcendentals=0)


def distance_tile(q_ref, k_ref):
    total = None
    for axis in range(3):
        offset = q_ref[:, axis:axis + 1] - k_ref[axis:axis + 1, :]
        total = offset * offset if total is None else total + offset * offset
    return jnp.sqrt(total) * (KERNELS / 48.0)


def kernel_rows(x):
    centre = lax.broadcasted_iota(jnp.int32, (NA, 1), 0).astype(jnp.float32) * (SPAN / 2.0) + SPAN / 4.0
    y = jnp.clip(x - centre, -24.0, 24.0)
    up_step = jnp.exp2(y * (0.5 * LOG2E))
    down_step = jnp.exp2(y * (-0.5 * LOG2E))
    middle = jnp.exp2((y * y) * (-0.5 * LOG2E))
    above = [middle]
    for _ in range(SPAN // 2 - 1):
        above.append(above[-1] * up_step)
    below = []
    current = middle
    for _ in range(SPAN // 2):
        current = current * down_step
        below.append(current)
    rows = below[::-1] + above
    return jnp.concatenate([r.astype(jnp.bfloat16) for r in rows], axis=0)


def kernel_order():
    step = np.arange(SPAN) - SPAN // 2
    order = np.array([[a * SPAN + SPAN // 2 + b for a in range(NA)] for b in step]).reshape(-1)
    factor = np.repeat(np.exp(-(step ** 2) / 8.0), NA).astype(np.float32)
    return order, factor


def bias_kernel(chunk, q_ref, k_ref, w_ref, *refs):
    out_ref, x_ref, m_ref = refs[-3:]
    rows = q_ref.shape[0]
    keys = k_ref.shape[1]
    x_ref[...] = distance_tile(q_ref, k_ref)
    m_ref[...] = jnp.where(q_ref[:, 3:4] == k_ref[3:4, :], 0.0, masked_value)
    w = w_ref[...]

    def step(t, carry):
        for start in range(0, keys, chunk):
            cols = slice(start, start + chunk)
            values = []
            for q in (2 * t, 2 * t + 1):
                value = jnp.dot(w, kernel_rows(x_ref[pl.ds(q, 1), cols]), preferred_element_type=jnp.float32)
                values.append(value + m_ref[pl.ds(q, 1), cols])
            for g in range(GROUPS):
                both = jnp.concatenate([value[g * GROUP_HEADS:(g + 1) * GROUP_HEADS] for value in values], axis=0)
                out_ref[g, pl.ds(t * 2 * GROUP_HEADS, 2 * GROUP_HEADS), cols] = both.astype(out_ref.dtype)
        return carry

    lax.fori_loop(0, rows // 2, step, 0, unroll=True)


def pair_bias(q_where, k_where, w, first, steps, previous):
    rows, keys = q_where.shape[0], k_where.shape[1]
    in_specs = [
        pl.BlockSpec((FINE, 8), lambda i: (i + first, 0)),
        pl.BlockSpec((8, keys), lambda i: (0, 0)),
        pl.BlockSpec((HEADS, KERNELS), lambda i: (0, 0)),
    ]
    operands = [q_where, k_where, w]
    aliases = {}
    if previous is not None:
        in_specs.append(pl.BlockSpec(memory_space=pl.ANY))
        operands.append(previous)
        aliases = {3: 0}
    return pl.pallas_call(
        functools.partial(bias_kernel, 256),
        grid=(steps,),
        in_specs=in_specs,
        out_specs=pl.BlockSpec((GROUPS, FINE * GROUP_HEADS, keys), lambda i: (0, i + first, 0)),
        out_shape=jax.ShapeDtypeStruct((GROUPS, rows * GROUP_HEADS, keys), jnp.bfloat16),
        scratch_shapes=[pltpu.VMEM((FINE, keys), jnp.float32), pltpu.VMEM((FINE, keys), jnp.float32)],
        input_output_aliases=aliases,
        cost_estimate=cost(1.5 * steps, FINE * steps * HEADS * keys * 2),
        compiler_params=pltpu.CompilerParams(vmem_limit_bytes=VMEM_LIMIT),
        name="pair_bias",
    )(*operands)


def project_kernel(x_ref, w_ref, turn_ref, key_ref, value_ref, w_turn_ref):
    @pl.when(pl.program_id(0) == 0)
    def turn_weight():
        w_turn_ref[...] = w_ref[...].T

    x = x_ref[...]
    rows = x.shape[0]
    turn_ref[...] = lax.dot_general(
        w_turn_ref[...], x, (((1,), (1,)), ((), ())), preferred_element_type=jnp.float32
    ).astype(turn_ref.dtype)
    flat = jnp.dot(x, w_ref[...], preferred_element_type=jnp.float32)
    for out_ref, first, filler in ((key_ref, 0, 0.0), (value_ref, D, 1.0)):
        for g in range(GROUPS):
            part = flat[:, first + g * GROUP_DIM:first + (g + 1) * GROUP_DIM]
            wide = jnp.concatenate([part, jnp.full((rows, GROUP_PAD - GROUP_DIM), filler, jnp.float32)], axis=1)
            out_ref[:, g * GROUP_PAD:(g + 1) * GROUP_PAD] = wide.astype(out_ref.dtype)


def project(values, weight):
    keys, depth = values.shape
    width = weight.shape[1]
    wide = GROUPS * GROUP_PAD
    block = 256
    return pl.pallas_call(
        project_kernel,
        grid=(keys // block,),
        in_specs=[
            pl.BlockSpec((block, depth), lambda i: (i, 0)),
            pl.BlockSpec((depth, width), lambda i: (0, 0)),
        ],
        out_specs=[
            pl.BlockSpec((width, block), lambda i: (0, i)),
            pl.BlockSpec((block, wide), lambda i: (i, 0)),
            pl.BlockSpec((block, wide), lambda i: (i, 0)),
        ],
        out_shape=[
            jax.ShapeDtypeStruct((width, keys), jnp.bfloat16),
            jax.ShapeDtypeStruct((keys, wide), jnp.bfloat16),
            jax.ShapeDtypeStruct((keys, wide), jnp.bfloat16),
        ],
        scratch_shapes=[pltpu.VMEM((width, depth), jnp.bfloat16)],
        cost_estimate=cost(12, keys * (depth + 3 * width) * 2),
        compiler_params=pltpu.CompilerParams(vmem_limit_bytes=VMEM_LIMIT),
        name="project",
    )(values, weight)


def head_mask(width):
    head = lax.broadcasted_iota(jnp.int32, (GROUP_HEADS, width), 0)
    lane = lax.broadcasted_iota(jnp.int32, (GROUP_HEADS, width), 1)
    return ((lane >= head * HEAD_DIM) & (lane < (head + 1) * HEAD_DIM)).astype(jnp.float32)


def spread_heads(values, mask):
    rows, width = values.shape
    return (values[:, None, :] * mask[None]).reshape(rows * GROUP_HEADS, width)


def gather_heads(values, mask):
    rows, width = values.shape
    return jnp.sum(values.reshape(rows // GROUP_HEADS, GROUP_HEADS, width) * mask[None], axis=1)


def forward_kernel(chunk, q_ref, kt_ref, v_ref, bias_ref, p_ref, o_ref, inv_ref, s_ref):
    keys = kt_ref.shape[1]
    mask = head_mask(GROUP_PAD)

    for g in range(GROUPS):
        rows = slice(g * GROUP_DIM, (g + 1) * GROUP_DIM)
        spread = spread_heads(q_ref[g].astype(jnp.float32), mask).astype(jnp.bfloat16)[:, :GROUP_DIM]
        peak = None
        for start in range(0, keys, chunk):
            s = jnp.dot(spread, kt_ref[rows, start:start + chunk], preferred_element_type=jnp.float32)
            s = s * (SCALE * LOG2E) + bias_ref[g, :, start:start + chunk].astype(jnp.float32)
            s_ref[:, start:start + chunk] = s
            for lane in range(0, chunk, 128):
                part = s[:, lane:lane + 128]
                peak = part if peak is None else jnp.maximum(peak, part)
        top = jnp.max(peak, axis=1, keepdims=True)
        for start in range(0, keys, chunk):
            p_ref[g, :, start:start + chunk] = jnp.exp2(s_ref[:, start:start + chunk] - top).astype(jnp.bfloat16)
        mixed = jnp.dot(p_ref[g], v_ref[:, g * GROUP_PAD:(g + 1) * GROUP_PAD], preferred_element_type=jnp.float32)
        inverse = 1.0 / mixed[:, GROUP_DIM:GROUP_DIM + 1]
        o_ref[g] = gather_heads(mixed * inverse, mask)
        inv_ref[g] = gather_heads(jnp.broadcast_to(inverse, mixed.shape), mask)


def attend(q, turned, value_flat, bias):
    rows, keys = q.shape[1], turned.shape[1]
    tile = min(FORWARD_TILE, FORWARD_TILE * 2048 // keys)
    whole = pl.Buffered(1)
    return pl.pallas_call(
        functools.partial(forward_kernel, 512),
        grid=(rows // tile,),
        in_specs=[
            pl.BlockSpec((GROUPS, tile, GROUP_PAD), lambda i: (0, i, 0)),
            pl.BlockSpec((D, keys), lambda i: (0, 0), pipeline_mode=whole),
            pl.BlockSpec((keys, GROUPS * GROUP_PAD), lambda i: (0, 0), pipeline_mode=whole),
            pl.BlockSpec((GROUPS, tile * GROUP_HEADS, keys), lambda i: (0, i, 0)),
        ],
        out_specs=[
            pl.BlockSpec((GROUPS, tile * GROUP_HEADS, keys), lambda i: (0, i, 0)),
            pl.BlockSpec((GROUPS, tile, GROUP_PAD), lambda i: (0, i, 0)),
            pl.BlockSpec((GROUPS, tile, GROUP_PAD), lambda i: (0, i, 0)),
        ],
        out_shape=[
            jax.ShapeDtypeStruct((GROUPS, rows * GROUP_HEADS, keys), jnp.bfloat16),
            jax.ShapeDtypeStruct((GROUPS, rows, GROUP_PAD), jnp.float32),
            jax.ShapeDtypeStruct((GROUPS, rows, GROUP_PAD), jnp.float32),
        ],
        scratch_shapes=[
            pltpu.VMEM((tile * GROUP_HEADS, keys), jnp.float32),
        ],
        input_output_aliases={3: 0},
        cost_estimate=cost(45, rows * HEADS * keys * 4),
        compiler_params=pltpu.CompilerParams(vmem_limit_bytes=VMEM_LIMIT),
        name="attend",
    )(q, turned, value_flat, bias)


def backward_kernel(chunk, q_ref, do_ref, o_ref, k_ref, vt_ref, p_ref, ds_ref, dq_ref, dkt_ref, dvt_ref, dk_acc, dv_acc):
    keys = vt_ref.shape[1]
    mask = head_mask(GROUP_PAD)
    tile = pl.program_id(0)
    groups = q_ref.shape[0]

    @pl.when(tile == 0)
    def start_group():
        dk_acc[...] = jnp.zeros_like(dk_acc)
        dv_acc[...] = jnp.zeros_like(dv_acc)

    for g in range(groups):
        rows = slice(g * GROUP_DIM, (g + 1) * GROUP_DIM)
        q_wide = spread_heads(q_ref[g].astype(jnp.float32), mask)
        do_wide = spread_heads(do_ref[g].astype(jnp.float32), mask)
        o_wide = spread_heads(o_ref[g], mask)
        delta = jnp.sum(do_wide * o_wide, axis=1, keepdims=True)
        do_low = do_wide.astype(jnp.bfloat16)[:, :GROUP_DIM]
        do_turn = do_wide[:, :GROUP_DIM].T.astype(jnp.bfloat16)
        q_turn = q_wide[:, :GROUP_DIM].T.astype(jnp.bfloat16)
        for start in range(0, keys, chunk):
            cols = slice(start, start + chunk)
            dp = jnp.dot(do_low, vt_ref[rows, cols], preferred_element_type=jnp.float32)
            p = p_ref[g, :, cols]
            ds = (p.astype(jnp.float32) * (dp - delta)).astype(jnp.bfloat16)
            ds_ref[g, :, cols] = ds
            dv_acc[rows, cols] += jnp.dot(do_turn, p, preferred_element_type=jnp.float32)
            dk_acc[rows, cols] += jnp.dot(q_turn, ds, preferred_element_type=jnp.float32)
        dq = jnp.dot(ds_ref[g], k_ref[:, g * GROUP_PAD:(g + 1) * GROUP_PAD], preferred_element_type=jnp.float32)
        dq_ref[g] = gather_heads(dq, mask) * SCALE

    @pl.when(tile == pl.num_programs(0) - 1)
    def finish():
        dkt_ref[...] = (dk_acc[...] * SCALE).astype(dkt_ref.dtype)
        dvt_ref[...] = dv_acc[...].astype(dvt_ref.dtype)


def attend_back(q, do, o, key_flat, turned, p, part, parts):
    rows, keys = q.shape[1], turned.shape[1]
    tile = min(BACKWARD_TILE, BACKWARD_TILE * 2048 // keys)
    groups = GROUPS // parts
    width = groups * GROUP_DIM
    whole = pl.Buffered(1)
    narrow = pl.BlockSpec((groups, tile, GROUP_PAD), lambda i: (part, i, 0))
    return pl.pallas_call(
        functools.partial(backward_kernel, 512),
        grid=(rows // tile,),
        in_specs=[
            narrow,
            narrow,
            narrow,
            pl.BlockSpec((keys, groups * GROUP_PAD), lambda i: (0, part), pipeline_mode=whole),
            pl.BlockSpec((width, keys), lambda i: (part + parts, 0), pipeline_mode=whole),
            pl.BlockSpec((groups, tile * GROUP_HEADS, keys), lambda i: (part, i, 0)),
        ],
        out_specs=[
            pl.BlockSpec((groups, tile * GROUP_HEADS, keys), lambda i: (part, i, 0)),
            pl.BlockSpec((groups, tile, GROUP_PAD), lambda i: (0, i, 0)),
            pl.BlockSpec((width, keys), lambda i: (0, 0), pipeline_mode=whole),
            pl.BlockSpec((width, keys), lambda i: (0, 0), pipeline_mode=whole),
        ],
        out_shape=[
            jax.ShapeDtypeStruct(p.shape, p.dtype),
            jax.ShapeDtypeStruct((groups, rows, GROUP_PAD), jnp.float32),
            jax.ShapeDtypeStruct((width, keys), jnp.bfloat16),
            jax.ShapeDtypeStruct((width, keys), jnp.bfloat16),
        ],
        scratch_shapes=[
            pltpu.VMEM((width, keys), jnp.float32),
            pltpu.VMEM((width, keys), jnp.float32),
        ],
        input_output_aliases={5: 0},
        cost_estimate=cost(56 / parts, rows * HEADS * keys * 4 // parts),
        compiler_params=pltpu.CompilerParams(vmem_limit_bytes=VMEM_LIMIT),
        name="attend_back",
    )(q, do, o, key_flat, turned, p)


def table_grad_kernel(chunk, q_ref, k_ref, ds_ref, out_ref, x_ref):
    rows = q_ref.shape[0]
    keys = k_ref.shape[1]
    pair = 2 * GROUP_HEADS

    @pl.when(pl.program_id(0) == 0)
    def start_zero():
        out_ref[...] = jnp.zeros_like(out_ref)

    x_ref[...] = distance_tile(q_ref, k_ref)

    def step(t, total):
        for start in range(0, keys, chunk):
            x = x_ref[pl.ds(2 * t, 2), start:start + chunk]
            table = jnp.concatenate([kernel_rows(x[0:1]), kernel_rows(x[1:2])], axis=0)
            grads = jnp.concatenate(
                [ds_ref[g, pl.ds(t * pair, pair), start:start + chunk] for g in range(GROUPS)], axis=0
            )
            total = total + lax.dot_general(table, grads, (((1,), (1,)), ((), ())), preferred_element_type=jnp.float32)
        return total

    out_ref[...] += lax.fori_loop(0, rows // 2, step, jnp.zeros(out_ref.shape, jnp.float32), unroll=True)


def table_grad(q_where, k_where, ds, first, steps):
    rows, keys = q_where.shape[0], k_where.shape[1]
    wide = 2 * HEADS
    return pl.pallas_call(
        functools.partial(table_grad_kernel, 256),
        grid=(steps,),
        in_specs=[
            pl.BlockSpec((FINE, 8), lambda i: (i + first, 0)),
            pl.BlockSpec((8, keys), lambda i: (0, 0)),
            pl.BlockSpec((GROUPS, FINE * GROUP_HEADS, keys), lambda i: (0, i + first, 0)),
        ],
        out_specs=pl.BlockSpec((2 * KERNELS, wide), lambda i: (0, 0)),
        out_shape=jax.ShapeDtypeStruct((2 * KERNELS, wide), jnp.float32),
        scratch_shapes=[pltpu.VMEM((FINE, keys), jnp.float32)],
        cost_estimate=cost(1.6 * steps, FINE * steps * HEADS * keys * 2),
        compiler_params=pltpu.CompilerParams(vmem_limit_bytes=VMEM_LIMIT),
        name="table_grad",
    )(q_where, k_where, ds)


def table_sums(sums):
    sums = sums.reshape(2, KERNELS, GROUPS, 2, GROUP_HEADS)
    both = (sums[0, :, :, 0] + sums[1, :, :, 1]).reshape(KERNELS, HEADS)
    order, factor = kernel_order()
    return (both * factor[:, None])[np.argsort(order)]


def place_kernel(steps, s_ref, *refs):
    own_ref = refs[0]
    mine, other = refs[1:1 + steps], refs[1 + steps:1 + 2 * steps]
    out_ref = refs[-1]
    j = pl.program_id(0)
    place, core = s_ref[0], s_ref[1]
    away = lax.rem(place - j // 2 + steps + 1, steps + 1)

    @pl.when(away == 0)
    def own_part():
        out_ref[...] = own_ref[...]

    for step in range(1, steps + 1):
        @pl.when((away == step) & (core == j % 2))
        def fetched_part():
            out_ref[...] = mine[step - 1][...]

        @pl.when((away == step) & (core != j % 2))
        def passed_part():
            out_ref[...] = other[step - 1][...]


def place_shards(where, own, mine, other):
    steps = len(mine)
    rows, columns = own.shape
    half = rows // 2
    fixed = pl.BlockSpec((half, columns), lambda j, s: (0, 0))
    return pl.pallas_call(
        functools.partial(place_kernel, steps),
        grid_spec=pltpu.PrefetchScalarGridSpec(
            num_scalar_prefetch=1,
            grid=(2 * (steps + 1),),
            in_specs=[pl.BlockSpec((half, columns), lambda j, s: (j % 2, 0))] + [fixed] * (2 * steps),
            out_specs=pl.BlockSpec((half, columns), lambda j, s: (j, 0)),
        ),
        out_shape=jax.ShapeDtypeStruct(((steps + 1) * rows, columns), own.dtype),
        cost_estimate=cost(3, 2 * (steps + 1) * own.size * 2),
        compiler_params=pltpu.CompilerParams(vmem_limit_bytes=VMEM_LIMIT),
        name="place_shards",
    )(where, own, *mine, *other)


def assemble_kernel(xs, widths, s_ref, *refs):
    own_refs, other_refs, out_refs = refs[:xs], refs[xs:2 * xs], refs[2 * xs:]
    zs = own_refs[0].shape[0]
    x, core, z = s_ref[0], s_ref[1], s_ref[2]
    jx = pl.program_id(0)
    from_x = lax.rem(x - jx + xs, xs)
    first = core == 0
    for step in range(xs):
        @pl.when(from_x == step)
        def copy_piece():
            for jz in range(zs):
                from_z = lax.rem(z - jz + zs, zs)
                begin = 0
                for half, out_ref in zip(widths, out_refs):
                    own = own_refs[step][from_z, :, begin:begin + half].astype(jnp.float32)
                    other = other_refs[step][from_z, :, begin:begin + half].astype(jnp.float32)
                    out_ref[0, jz, :, :half] = jnp.where(first, own, other)
                    out_ref[0, jz, :, half:] = jnp.where(first, other, own)
                    begin += half


def assemble(where, own, other, widths):
    xs = len(own)
    zs, rows, columns = own[0].shape
    spec = pl.BlockSpec((zs, rows, columns), lambda i, s: (0, 0, 0))
    wholes = pl.pallas_call(
        functools.partial(assemble_kernel, xs, widths),
        grid_spec=pltpu.PrefetchScalarGridSpec(
            num_scalar_prefetch=1,
            grid=(xs,),
            in_specs=[spec] * (2 * xs),
            out_specs=[pl.BlockSpec((1, zs, rows, 2 * half), lambda i, s: (i, 0, 0, 0)) for half in widths],
        ),
        out_shape=[jax.ShapeDtypeStruct((xs, zs, rows, 2 * half), jnp.float32) for half in widths],
        cost_estimate=cost(4, xs * zs * rows * columns * 12),
        compiler_params=pltpu.CompilerParams(vmem_limit_bytes=VMEM_LIMIT),
        name="assemble",
    )(where, *own, *other)
    return [whole.reshape(xs * zs * rows, -1) for whole in wholes]


eps = 1e-05
highest = lax.Precision.HIGHEST
CHIP_ROW = 4
Z_EXCHANGE = True


def layer_norm(values, norm_gain, norm_shift):
    centred = values - jnp.mean(values, axis=-1, keepdims=True)
    spread = jnp.mean(centred * centred, axis=-1, keepdims=True)
    return centred * lax.rsqrt(spread + eps) * norm_gain + norm_shift


def exact_gelu(values):
    return jax.nn.gelu(values, approximate=False)


def time_features(stamps, feature_width):
    half_width = feature_width // 2
    frequency = jnp.exp(-jnp.log(10000.0) * jnp.arange(half_width, dtype=jnp.float32) / half_width)
    angles = stamps[:, None] * frequency[None, :]
    return jnp.concatenate([jnp.sin(angles), jnp.cos(angles)], axis=1)


def shifted(values, axis, step):
    size = lax.axis_size(axis)
    return lax.ppermute(values, axis, [(i, (i + step) % size) for i in range(size)])


def part_of(values, index, count, axis):
    length = values.shape[axis] // count
    return lax.dynamic_slice_in_dim(values, index * length, length, axis)


def dot32(left, right, contract):
    return lax.dot_general(left, right, ((contract[:1], contract[1:]), ((), ())), preferred_element_type=jnp.float32)


def in_order(pieces):
    count = len(pieces)
    place = lax.axis_index("dp")
    chosen = []
    for index in range(count):
        step = lax.rem(place - index + count, count)
        picked = pieces[0]
        for other in range(1, count):
            picked = jnp.where(step == other, pieces[other], picked)
        chosen.append(picked)
    return jnp.stack(chosen)


def spread_dp(values):
    return [values] + [shifted(values, "dp", step) for step in range(1, lax.axis_size("dp"))]


def fetch_shards(weight):
    half = part_of(weight, lax.axis_index("core"), 2, 0)
    return [shifted(half, "dp", step) for step in range(1, lax.axis_size("dp"))]


def pass_on(mine):
    return [shifted(piece, "core", 1) for piece in mine]


def gather_weight(weight, mine, other):
    where = jnp.stack([lax.axis_index("dp"), lax.axis_index("core")]).astype(jnp.int32)
    return place_shards(where, weight, mine, other)


def tie(*groups):
    return lax.optimization_barrier(groups)


def add_parts(own, incoming):
    total = own.astype(jnp.float32)
    for share in incoming:
        total = total + share.astype(jnp.float32)
    return total


def reduce_chain(local, hops, widths):
    left = ["dp", "x", "z"]
    for axis in hops:
        dim = left.index(axis)
        left.pop(dim)
        count, place = lax.axis_size(axis), lax.axis_index(axis)
        if axis == "z" and Z_EXCHANGE:
            local = yield lax.all_to_all(local.astype(jnp.bfloat16), "z", dim, 0)
            local = jnp.sum(local.astype(jnp.float32), axis=0)
            continue
        own = lax.dynamic_index_in_dim(local, place, dim, keepdims=False)
        incoming = [
            shifted(
                lax.dynamic_index_in_dim(local, lax.rem(place + step, count), dim, keepdims=False).astype(jnp.bfloat16),
                axis,
                step,
            )
            for step in range(1, count)
        ]
        own, incoming = yield own, incoming
        local = add_parts(own, incoming)
    owned = local.astype(jnp.bfloat16)
    owned, incoming = yield owned, [shifted(owned, "z", step) for step in range(1, lax.axis_size("z"))]
    pieces = jnp.stack([owned] + incoming)
    own = yield [pieces] + [shifted(pieces, "x", step) for step in range(1, lax.axis_size("x"))]
    own, other = yield own, [shifted(piece, "core", 1) for piece in own]
    where = jnp.stack([lax.axis_index(axis) for axis in ("x", "core", "z")]).astype(jnp.int32)
    return assemble(where, own, other, widths)


def by_owner(values):
    counts = [lax.axis_size(axis) for axis in ("dp", "x", "z")]
    return values.reshape(counts + [-1, values.shape[1]])


def weight_chain(factors, hops):
    core = lax.axis_index("core")
    moving = []
    for inputs, grads in factors:
        moving.append((
            inputs, shifted(inputs, "core", 1),
            part_of(grads, core, 2, 1), shifted(part_of(grads, 1 - core, 2, 1), "core", 1),
        ))
    moving = yield moving
    local = [
        dot32(jnp.concatenate([left, other_left], axis=0), jnp.concatenate([right, other_right], axis=0), (0, 0))
        .astype(jnp.bfloat16)
        for left, other_left, right, other_right in moving
    ]
    return (yield from reduce_chain(by_owner(jnp.concatenate(local, axis=1)), hops, [part.shape[1] for part in local]))


def table_chain(local, hops):
    core = lax.axis_index("core")
    own = part_of(local, core, 2, 1)
    own, other = yield own, shifted(part_of(local, 1 - core, 2, 1), "core", 1)
    chip = (own.astype(jnp.float32) + other.astype(jnp.float32)).astype(jnp.bfloat16)
    return (yield from reduce_chain(by_owner(chip), hops, [chip.shape[1]]))


def share_chain(shares):
    x_count, z_count = shares.shape[:2]
    own, incoming = yield shares[0], [shifted(shares[step], "x", -step) for step in range(1, x_count)]
    total = add_parts(own, incoming)
    low = total.astype(jnp.bfloat16)
    own, incoming = yield total[0], [shifted(low[step], "z", -step) for step in range(1, z_count)]
    return add_parts(own, incoming)


class Flight:
    def __init__(self, chain):
        self.chain = chain
        self.values = next(chain)
        self.result = None

    def land(self, values):
        try:
            self.values = self.chain.send(values)
        except StopIteration as stop:
            self.values, self.result = None, stop.value


def advance(inputs, *flights):
    flights = [flight for flight in flights if flight.values is not None]
    inputs, landed = lax.optimization_barrier((inputs, [flight.values for flight in flights]))
    for flight, values in zip(flights, landed):
        flight.land(values)
    return inputs


def finish(flight):
    while flight.values is not None:
        flight.land(flight.values)
    return flight.result


def sum_all(values):
    for axis in ("core", "dp", "x", "z"):
        values = functools.reduce(
            jnp.add, [shifted(values, axis, step) for step in range(1, lax.axis_size(axis))], values
        )
    return values


def by_group(values):
    wide = values.reshape(values.shape[0], GROUPS, GROUP_DIM)
    wide = jnp.pad(wide, ((0, 0), (0, 0), (0, GROUP_PAD - GROUP_DIM)))
    return jnp.transpose(wide, (1, 0, 2))


def flat_groups(values):
    return jnp.transpose(values[:, :, :GROUP_DIM], (1, 0, 2)).reshape(values.shape[1], D)


def body(
    residues,
    coordinates,
    segment_ids,
    time_steps,
    time_weight,
    norm1_gain,
    norm1_bias,
    qkv_weight,
    bias_weight,
    out_weight,
    norm2_gain,
    norm2_bias,
    up_weight,
    down_weight,
    force_weight,
    out_cotangent,
    force_cotangent,
):
    core = lax.axis_index("core")
    place = lax.axis_index("dp")
    dp_count = lax.axis_size("dp")
    x_count, z_count = lax.axis_size("x"), lax.axis_size("z")
    held = residues.shape[1]

    def take_row(values):
        mine = lax.dynamic_index_in_dim(values, core, 0, keepdims=False)
        other = lax.dynamic_index_in_dim(values, 1 - core, 0, keepdims=False)
        return mine, shifted(other, "core", 1)

    def give_row(values, axis):
        mine = lax.slice_in_dim(values, 0, held, axis=axis)
        other = shifted(lax.slice_in_dim(values, held, 2 * held, axis=axis), "core", 1)
        first_row = jnp.where(core == 0, mine, other)
        second_row = jnp.where(core == 0, other, mine)
        return jnp.stack([first_row, second_row])

    where_own = jnp.concatenate(
        [coordinates, segment_ids[:, None, :].astype(jnp.bfloat16)], axis=1
    )
    where_rows = jnp.concatenate(take_row(where_own), axis=1)
    bias_parts = [bias_weight] + [shifted(bias_weight, "dp", step) for step in range(1, dp_count)]
    residue_parts = take_row(residues)
    step_list = spread_dp(time_steps)

    where_keys = where_rows[None]
    reach = 1
    while reach < z_count:
        where_keys = jnp.concatenate([where_keys, shifted(where_keys, "z", reach)], axis=0)
        reach *= 2
    where_columns = [where_keys[:z_count]]
    for x_step in range(1, x_count):
        where_columns.append(shifted(where_columns[0], "x", x_step))
    (
        where_columns,
        where_rows,
        bias_parts,
        residue_parts,
        step_list,
        (norm1_gain, norm1_bias, norm2_gain, norm2_bias, force_weight),
        (time_weight, qkv_weight, out_weight, up_weight, down_weight),
        (out_cotangent, force_cotangent),
    ) = tie(
        where_columns,
        where_rows,
        bias_parts,
        residue_parts,
        step_list,
        (norm1_gain, norm1_bias, norm2_gain, norm2_bias, force_weight),
        (time_weight, qkv_weight, out_weight, up_weight, down_weight),
        (out_cotangent, force_cotangent),
    )
    key_where = jnp.transpose(jnp.concatenate(where_columns, axis=0).astype(jnp.float32), (1, 0, 2))
    key_where = jnp.pad(key_where.reshape(4, -1), ((0, 4), (0, 0)))
    query_where = jnp.pad(jnp.transpose(where_rows).astype(jnp.float32), ((0, 0), (0, 4)))
    segment_rows = where_rows[3]
    residue_rows = jnp.concatenate(residue_parts, axis=0).astype(jnp.float32)

    bias_full = in_order(bias_parts).reshape(KERNELS, HEADS)
    order, factor = kernel_order()
    table_weight = (
        jnp.transpose(bias_full).astype(jnp.float32)[:, order] * (factor * LOG2E)
    ).astype(jnp.bfloat16)
    tiles = 2 * held // FINE
    lead = tiles // 8
    bias = pair_bias(query_where, key_where, table_weight, 0, lead, None)

    vectors = in_order(
        spread_dp(jnp.concatenate([jnp.stack([norm1_gain, norm1_bias, norm2_gain, norm2_bias]), force_weight], axis=0))
    )
    vectors = jnp.transpose(vectors, (1, 0, 2)).reshape(7, D)
    gain_one, shift_one, gain_two, shift_two = [vectors[i:i + 1].astype(jnp.float32) for i in range(4)]
    force_full = vectors[4:]
    proteins = time_steps.shape[1]
    row_steps = [lax.dynamic_index_in_dim(steps, core, 0, keepdims=False) for steps in step_list]
    features = time_features(jnp.concatenate(row_steps).astype(jnp.float32), D).astype(jnp.bfloat16)
    features = part_of(features, place, dp_count, 1)
    stamp_part = jnp.dot(features, time_weight, preferred_element_type=jnp.float32)
    stamp_rows = stamp_part[:proteins]
    for step in range(1, dp_count):
        stamp_rows = stamp_rows + shifted(
            stamp_part[step * proteins:(step + 1) * proteins], "dp", -step
        )
    query_own, pair_own = qkv_weight[:, :D], qkv_weight[:, D:]
    pair_half = fetch_shards(pair_own)
    query_half = fetch_shards(query_own)
    bias, stamp_rows, vectors_ready = tie(bias, stamp_rows, (gain_one, shift_one))
    gain_one, shift_one = vectors_ready

    def by_protein(table):
        picked = jnp.zeros((2 * held, table.shape[1]), jnp.float32)
        for index in range(proteins):
            picked = picked + jnp.where((segment_rows == index)[:, None], table[index][None, :], 0.0)
        return picked

    first = residue_rows + by_protein(stamp_rows)
    normed, norm_one_back = jax.vjp(layer_norm, first, gain_one, shift_one)
    normed_low = normed.astype(jnp.bfloat16)

    columns = [[None] * z_count for _ in range(x_count)]
    current = normed_low
    done = lead
    out_half = up_half = down_half = None
    for z_step in range(z_count):
        steps = (tiles - done) // (z_count - z_step)
        across = [current]
        for x_step in range(1, x_count):
            across.append(shifted(across[-1], "x", 1))
        following = shifted(current, "z", 1) if z_step < z_count - 1 else current
        bias = pair_bias(query_where, key_where, table_weight, done, steps, bias)
        done += steps
        bias, current, across = tie(bias, following, across)
        for x_step in range(x_count):
            columns[x_step][z_step] = across[x_step]
        if z_step == 1:
            bias, pair_half, query_half, later = tie(bias, pair_half, query_half, (out_weight, up_weight, down_weight))
            out_weight, up_weight, down_weight = later
            out_half, up_half, down_half = fetch_shards(out_weight), fetch_shards(up_weight), fetch_shards(down_weight)
            pair_passed = pass_on(pair_half)
            query_passed = pass_on(query_half)
    normed_all = jnp.concatenate([piece for column in columns for piece in column], axis=0)

    query_weight = gather_weight(query_own, query_half, query_passed)
    pair_weight = gather_weight(pair_own, pair_half, pair_passed)
    query = by_group(jnp.dot(normed_low, query_weight, preferred_element_type=jnp.float32).astype(jnp.bfloat16))
    turned, key_flat, value_flat = project(normed_all, pair_weight)
    probs, attended, inverse = attend(query, turned, value_flat, bias)
    attended_low = flat_groups(attended).astype(jnp.bfloat16)
    attended_low, out_half, up_half, down_half, cotangents = tie(
        attended_low, out_half, up_half, down_half, (out_cotangent, force_cotangent)
    )
    out_cotangent, force_cotangent = cotangents
    out_full = gather_weight(out_weight, out_half, pass_on(out_half))
    up_full = gather_weight(up_weight, up_half, pass_on(up_half))
    down_full = gather_weight(down_weight, down_half, pass_on(down_half))
    cot_rows = jnp.concatenate(take_row(out_cotangent), axis=0).astype(jnp.float32)
    force_cot = jnp.concatenate(take_row(force_cotangent), axis=1)

    second = first + jnp.dot(attended_low, out_full, preferred_element_type=jnp.float32)
    normed_two, norm_two_back = jax.vjp(layer_norm, second, gain_two, shift_two)
    normed_two_low = normed_two.astype(jnp.bfloat16)
    hidden = jnp.dot(normed_two_low, up_full, preferred_element_type=jnp.float32)
    activated, gelu_back = jax.vjp(exact_gelu, hidden)
    activated_low = activated.astype(jnp.bfloat16)
    third = second + jnp.dot(activated_low, down_full, preferred_element_type=jnp.float32)
    block_low = third.astype(jnp.bfloat16)
    forces = jnp.einsum("cd,qd->cq", force_full, block_low, preferred_element_type=jnp.float32)
    third_grad = cot_rows + jnp.einsum(
        "cq,cd->qd", force_cot, force_full.astype(jnp.float32), precision=highest
    )
    force_grad = jnp.einsum(
        "cq,qd->cd", force_cot, block_low.astype(jnp.float32), precision=highest
    )
    third_low = third_grad.astype(jnp.bfloat16)
    activated_grad = dot32(third_low, down_full, (1, 1))
    hidden_grad = gelu_back(activated_grad)[0].astype(jnp.bfloat16)
    normed_two_grad = dot32(hidden_grad, up_full, (1, 1))
    second_part, gain_two_grad, shift_two_grad = norm_two_back(normed_two_grad)
    second_grad = third_grad + second_part
    second_low = second_grad.astype(jnp.bfloat16)
    attended_grad = by_group(dot32(second_low, out_full, (1, 1)).astype(jnp.bfloat16))
    scaled_grad = (attended_grad.astype(jnp.float32) * inverse).astype(jnp.bfloat16)

    down = Flight(weight_chain([(activated_low, third_low)], ("dp", "x", "z")))
    up = Flight(weight_chain([(normed_two_low, hidden_grad), (attended_low, second_low)], ("x", "dp", "z")))

    scaled_grad = advance(scaled_grad, down, up)
    back = attend_back(query, scaled_grad, attended, key_flat, turned, probs, 0, 4)
    backs = [back[1:]]
    pairs, scaled_grad = advance((back[0], scaled_grad))
    back = attend_back(query, scaled_grad, attended, key_flat, turned, pairs, 1, 4)
    backs.append(back[1:])
    pairs, scaled_grad = advance((back[0], scaled_grad), down, up)
    back = attend_back(query, scaled_grad, attended, key_flat, turned, pairs, 2, 4)
    backs.append(back[1:])
    pairs, scaled_grad = advance((back[0], scaled_grad), down, up)
    back = attend_back(query, scaled_grad, attended, key_flat, turned, pairs, 3, 4)
    backs.append(back[1:])
    logit_grad, backs = advance((back[0], backs), down)
    query_grad = flat_groups(jnp.concatenate([back[0] for back in backs], axis=0)).astype(jnp.bfloat16)
    pair_grad_turn = jnp.concatenate([back[1] for back in backs] + [back[2] for back in backs], axis=0)

    query_part = dot32(normed_low, query_grad, (0, 0)).astype(jnp.bfloat16)
    pair_part = dot32(normed_all, pair_grad_turn, (0, 1)).astype(jnp.bfloat16)
    table = Flight(table_chain(jnp.concatenate([query_part, pair_part], axis=1), ("dp", "x", "z")))
    pair_share = dot32(pair_grad_turn, pair_weight, (0, 1)).astype(jnp.bfloat16)
    own = pair_share.reshape(x_count, z_count, 2 * held, D)
    first_half, second_half = own[..., :D // 2], own[..., D // 2:]
    share_one = Flight(share_chain(first_half))
    steps = tiles // 4
    logit_grad, second_half = advance((logit_grad, second_half), up, table)
    sums = table_grad(query_where, key_where, logit_grad, 0, steps)
    sums, logit_grad, second_half = advance((sums, logit_grad, second_half), share_one, down)
    share_two = Flight(share_chain(second_half))
    piece = table_grad(query_where, key_where, logit_grad, steps, steps)
    sums, piece, logit_grad = advance((sums, piece, logit_grad), share_one, share_two, table)
    sums = sums + piece
    piece = table_grad(query_where, key_where, logit_grad, 2 * steps, steps)
    sums, piece, logit_grad = advance((sums, piece, logit_grad), share_two, table, up)
    sums = sums + piece
    piece = table_grad(query_where, key_where, logit_grad, 3 * steps, steps)
    sums, piece = advance((sums, piece), table, down)
    bias_grad = table_sums(sums + piece)
    pair_normed_grad = jnp.concatenate([finish(share_one), finish(share_two)], axis=1)
    (down_grad,), (up_grad, out_grad) = finish(down), finish(up)
    table.land(table.values)
    table.land(table.values)
    (down_grad, up_grad, out_grad), last_pieces = tie((down_grad, up_grad, out_grad), table.values)
    table.land(last_pieces)
    (qkv_grad,) = finish(table)

    normed_grad = dot32(query_grad, query_weight, (1, 1)) + pair_normed_grad
    first_part, gain_one_grad, shift_one_grad = norm_one_back(normed_grad)
    first_grad = second_grad + first_part
    first_low = first_grad.astype(jnp.bfloat16).astype(jnp.float32)
    protein_sum = jnp.stack(
        [
            jnp.sum(jnp.where((segment_rows == index)[:, None], first_low, 0.0), axis=0)
            for index in range(proteins)
        ]
    )
    slots = 2 * dp_count
    slot = jnp.arange(slots) == 2 * place + core
    protein_slots = jnp.where(slot[:, None, None], protein_sum[None], 0.0)
    padding = jnp.zeros((6 * D - KERNELS * HEADS,), jnp.float32)
    last = sum_all(jnp.concatenate(
        [
            gain_one_grad,
            shift_one_grad,
            gain_two_grad,
            shift_two_grad,
            force_grad,
            jnp.concatenate([bias_grad.reshape(-1), padding]).reshape(6, D),
            protein_slots.reshape(slots * proteins, D),
        ],
        axis=0,
    ))
    vectors = part_of(last[:4], place, dp_count, 1)
    force_sum = part_of(last[4:7], place, dp_count, 1)
    bias_sum = part_of(last[7:13].reshape(-1)[:KERNELS * HEADS].reshape(KERNELS, HEADS), place, dp_count, 0)
    protein_all = last[13:]
    all_steps = in_order(step_list).reshape(slots * proteins).astype(jnp.float32)
    all_features = time_features(all_steps, D).astype(jnp.bfloat16)
    time_grad = jnp.einsum(
        "sd,se->de",
        part_of(all_features, place, dp_count, 1).astype(jnp.float32),
        protein_all,
        precision=highest,
    )

    return (
        give_row(block_low, 0),
        give_row(forces, 1),
        give_row(first_grad, 0),
        time_grad,
        vectors[0],
        vectors[1],
        qkv_grad,
        bias_sum,
        out_grad,
        vectors[2],
        vectors[3],
        up_grad,
        down_grad,
        force_sum,
    )


def solution(mesh):
    chips = mesh.shape["blk"] // 2
    rows = CHIP_ROW if chips % CHIP_ROW == 0 else 1
    fine = jax.sharding.Mesh(
        mesh.devices.reshape(mesh.shape["dp"], rows, chips // rows, 2), ("dp", "z", "x", "core")
    )
    blk = ("z", "x", "core")
    return jax.shard_map(
        body,
        mesh=fine,
        in_specs=(
            P("dp", blk, None),
            P("dp", None, blk),
            P("dp", blk),
            P("dp", None),
            P("dp", None),
            P("dp"),
            P("dp"),
            P("dp", None),
            P("dp", None),
            P("dp", None),
            P("dp"),
            P("dp"),
            P("dp", None),
            P("dp", None),
            P(None, "dp"),
            P("dp", blk, None),
            P("dp", None, blk),
        ),
        out_specs=(
            P("dp", blk, None),
            P("dp", None, blk),
            P("dp", blk, None),
            P("dp", None),
            P("dp"),
            P("dp"),
            P("dp", None),
            P("dp", None),
            P("dp", None),
            P("dp"),
            P("dp"),
            P("dp", None),
            P("dp", None),
            P(None, "dp"),
        ),
        check_vma=False,
    )
```
